256 devices in a mesh: dp: 16 (over z, core), row: 4 (over y), col: 4 (over x).
Axes of the slice: x: 4, y: 4, z: 8, core: 2. Of those that a mesh axis runs over, the one named last changes fastest.
Arguments:
- flat_iterate: bfloat16 [256, 270336], P(('dp', 'row', 'col')), as said below
- lengths: int32 [16, 16], replicated, may hold values from 1 to 270336, 2883584 in all within a row
Outputs:
- new_flat: bfloat16 [256, 270336], P(('dp', 'row', 'col'))
The draws below stay inside these ranges and needn't reach their ends.
Inputs may be any that keep to these rules, and one draw needn't show every extreme that they name: Every row of lengths sums to 2883584, and its largest entry is 270336. `flat_iterate`: slots at or past a shard's length belong to no group.
All inputs are finite; a program needn't handle non-finite values.
Results may differ from the reference program's by a relative error of at most 0.02.
Values may be sent and summed in bfloat16 or wider, within the bound.
A program may use at most 64 MiB of HBM per device.

```python
import math
import jax
import jax.numpy as jnp
import numpy as np
from jax import lax

COLS = 8192
ROWS = 5632
GROUP_ELEMS = 2883584
FLAT_CAP = 270336
N_DP = 16
N_ROW = 4
N_COL = 4
DEVICES = 256


def draw_flat_iterate(key, part):
    key = jax.random.fold_in(key, 7)
    spread = 1.0 / (math.sqrt(ROWS) + math.sqrt(COLS))
    extent = (DEVICES, FLAT_CAP)
    values = jax.random.truncated_normal(key, -4.0, 4.0, extent, jnp.float32)
    return (values * spread).astype(jnp.bfloat16)


def length_profile(count, total, reach, slope):
    portions = [(1 << 20) // math.isqrt(grade ** slope) + 1 for grade in range(2, count + 1)]
    rest, holding = total - reach - (count - 1), [1] * (count - 1)
    while rest > 0:
        movable = [i for i in range(count - 1) if holding[i] < reach]
        pool, remaining = sum([portions[i] for i in movable]), rest
        for i in movable:
            more = min(reach - holding[i], max(1, remaining * portions[i] // pool), rest)
            holding[i] = holding[i] + more
            rest = rest - more
    return np.array([reach] + holding)


def uneven(stream_key, number_of, total, most, slope):
    if number_of == 2:
        one = jax.random.randint(stream_key, (), max(1, total - most), min(most, total - 1) + 1)
        return jnp.stack([one, total - one])
    sizes = jnp.asarray(length_profile(number_of, total, most, slope), jnp.int32)
    couples = (number_of - 1) // 2
    giver, taker = sizes[1:1 + 2 * couples:2], sizes[2:2 + 2 * couples:2]
    room = jnp.minimum(giver - 1, most - taker)
    passed = jax.random.randint(jax.random.fold_in(stream_key, 1), (couples,), 0, 1 << 20) % (room + 1)
    sizes = sizes.at[1:1 + 2 * couples:2].set(giver - passed).at[2:2 + 2 * couples:2].set(taker + passed)
    return sizes[jax.random.permutation(jax.random.fold_in(stream_key, 2), number_of)]


def setup_inputs(seed: int = 0) -> dict:
    seeds = jax.random.split(jax.random.key(seed), 3)
    return {
        "flat_iterate": draw_flat_iterate(jax.random.fold_in(seeds[2], 71), 0),
        "lengths": jax.vmap(lambda own: uneven(own, N_DP, GROUP_ELEMS, FLAT_CAP, 1))(jax.random.split(seeds[1], (N_ROW * N_COL))).reshape((N_ROW * N_COL, N_DP)).astype(jnp.int32),
    }


LINEAR_COEF = 3.4445
CUBIC_COEF = -4.775
QUINTIC_COEF = 2.0315

def assemble(flat_iterate, lengths):
    groups = N_ROW * N_COL
    shard_ends = jnp.cumsum(lengths, axis=1).astype(jnp.int32)
    starts = (shard_ends - lengths).astype(jnp.int32)
    places = jnp.arange(GROUP_ELEMS, dtype=jnp.int32)
    pieces = []
    for group_index in range(groups):
        owner_index = jnp.searchsorted(shard_ends[group_index], places, side='right').astype(jnp.int32)
        offset = (places - starts[group_index][owner_index]).astype(jnp.int32)
        pieces.append(flat_iterate[owner_index * groups + group_index, offset])
    return (jnp.concatenate(pieces).reshape(ROWS, COLS), starts)

def reference(flat_iterate, lengths):
    groups = N_ROW * N_COL
    matrix, starts = assemble(flat_iterate, lengths)
    slab_width = COLS // N_DP
    gram = jnp.zeros((ROWS, ROWS), jnp.float32)
    for dp_slot in range(N_DP):
        columns = matrix[:, dp_slot * slab_width:(dp_slot + 1) * slab_width]
        term_value = jnp.dot(columns, columns.T, preferred_element_type=jnp.float32).astype(jnp.bfloat16)
        gram = gram + lax.optimization_barrier(term_value).astype(jnp.float32)
    gram = gram.astype(jnp.bfloat16)
    share_width = ROWS // N_DP
    square = jnp.zeros((ROWS, ROWS), jnp.float32)
    for dp_slot in range(N_DP):
        left_part = gram[:, dp_slot * share_width:(dp_slot + 1) * share_width]
        right_part = gram[dp_slot * share_width:(dp_slot + 1) * share_width, :]
        term_value = jnp.dot(left_part, right_part, preferred_element_type=jnp.float32).astype(jnp.bfloat16)
        square = square + lax.optimization_barrier(term_value).astype(jnp.float32)
    poly_rows = (CUBIC_COEF * gram.astype(jnp.float32) + QUINTIC_COEF * square).astype(jnp.bfloat16)
    product = jnp.dot(poly_rows, matrix, preferred_element_type=jnp.float32)
    scale_factor = 0.2 * math.sqrt(max(ROWS, COLS))
    update = (scale_factor * (LINEAR_COEF * matrix.astype(jnp.float32) + product)).astype(jnp.bfloat16)
    grouped = update.reshape(groups, GROUP_ELEMS)
    slots = jnp.arange(FLAT_CAP, dtype=jnp.int32)
    source_place = jnp.clip(starts[:, :, None] + slots[None, None, :], 0, GROUP_ELEMS - 1).astype(jnp.int32)
    group_ids = jnp.arange(groups, dtype=jnp.int32)[:, None, None]
    values = grouped[group_ids, source_place]
    inside = slots[None, None, :] < lengths[:, :, None]
    values = jnp.where(inside, values, jnp.zeros((), values.dtype))
    return jnp.transpose(values, (1, 0, 2)).reshape(N_DP * groups, FLAT_CAP)
```

```python
import math

import jax
import jax.numpy as jnp
from jax import lax
from jax.experimental import pallas as pl
from jax.experimental.pallas import tpu as pltpu
from jax.sharding import PartitionSpec as P

COLS = 8192
ROWS = 5632


LINEAR_COEF = 3.4445
CUBIC_COEF = -4.775
QUINTIC_COEF = 2.0315

N_DP = 16
N_Z = 8
RING = 4
GROUP_ROWS = 352
HALF_ROWS = 176
SLAB = 512
BLOCK = 1408
CORE_ROWS = 704
SHARD = 96
HALF_SHARD = 48
FWD = 768
N_MESSAGES = 96
MESH = pl.DeviceIdType.MESH
SCALE = 0.2 * math.sqrt(max(ROWS, COLS))


def core_kernel(
    x_ref, out_ref, xr, xs, own_f32, to_sib, from_sib, gh, ring_f, ring_b, g_full,
    part, got_a, got_b, got_c, got_d, y_f32, ya, yb, part2, z_b, send_sem, recv_sem,
):
    dp = lax.axis_index("dp")
    y = lax.axis_index("row")
    x = lax.axis_index("col")
    z, c = dp // 2, dp % 2
    sib_dp = z * 2 + 1 - c
    up_dp = ((z + 1) % N_Z) * 2 + c
    down_dp = ((z + 7) % N_Z) * 2 + c
    dev_sib = (sib_dp, y, x)
    dev_up = (up_dp, y, x)
    dev_down = (down_dp, y, x)
    near = {
        "col": ((dp, y, (x + 1) % RING), (dp, y, (x + 3) % RING)),
        "row": ((dp, (y + 1) % RING, x), (dp, (y + 3) % RING, x)),
    }
    place = {"col": x, "row": y}

    barrier = pltpu.get_barrier_semaphore()
    for peer in (dev_sib, dev_up, dev_down) + near["col"] + near["row"]:
        pl.semaphore_signal(barrier, inc=1, device_id=peer, device_id_type=MESH)
    pl.semaphore_wait(barrier, 7)

    counter = [0]
    started = []

    def message(src, dst, device, slot=None):
        if slot is None:
            slot = counter[0]
            counter[0] += 1
        return pltpu.make_async_remote_copy(
            src_ref=src, dst_ref=dst, send_sem=send_sem.at[slot], recv_sem=recv_sem.at[slot],
            device_id=device, device_id_type=MESH,
        )

    def send(src, dst, device):
        copy = message(src, dst, device)
        copy.start()
        started.append(copy)
        return copy

    top, bottom = pl.ds(0, HALF_ROWS), pl.ds(HALF_ROWS, HALF_ROWS)

    def gather_start(axis, buf):
        p = place[axis]
        right, left = near[axis]
        a = [send(buf.at[p, h], buf.at[p, h], right) for h in (top, bottom)]
        b = [send(buf.at[p, h], buf.at[p, h], left) for h in (bottom, top)]
        return a, b

    def gather_pass(axis, buf, state):
        p = place[axis]
        right, left = near[axis]
        a, b = state
        before, after = (p + 3) % RING, (p + 1) % RING
        a[0].wait_recv()
        f = send(buf.at[before, top], buf.at[before, top], right)
        b[0].wait_recv()
        g = send(buf.at[after, bottom], buf.at[after, bottom], left)
        return a[1], b[1], f, g

    def gather_end(tail):
        for copy in tail:
            copy.wait_recv()

    xr[x] = x_ref[...]
    xs[y] = x_ref[...]
    s1 = gather_start("col", xr)
    s2 = gather_start("row", xs)
    t1 = gather_pass("col", xr, s1)
    t2 = gather_pass("row", xs, s2)
    gather_end(t1)
    gather_end(t2)

    base = counter[0]
    counter[0] += 4

    def sib_message(i):
        rows = pl.ds(pl.multiple_of(i * HALF_ROWS, 16), HALF_ROWS)
        return message(to_sib.at[rows], from_sib.at[rows], dev_sib, slot=base + i)

    def gram_tile(half, i):
        left = xr[2 * half + i // 2, pl.ds(pl.multiple_of((i % 2) * HALF_ROWS, 16), HALF_ROWS)]
        return lax.dot_general(
            left, xs[...].reshape(BLOCK, SLAB), (((1,), (1,)), ((), ())), preferred_element_type=jnp.float32
        )

    def sib_step(i, _):
        rows = pl.ds(pl.multiple_of(i * HALF_ROWS, 16), HALF_ROWS)
        to_sib[rows] = gram_tile(1 - c, i).astype(jnp.bfloat16)
        sib_message(i).start()
        return 0

    lax.fori_loop(0, 4, sib_step, 0)

    def own_step(i, _):
        rows = pl.ds(pl.multiple_of(i * HALF_ROWS, 16), HALF_ROWS)
        own_f32[rows] = gram_tile(c, i)
        return 0

    lax.fori_loop(0, 4, own_step, 0)
    gh[pl.ds(CORE_ROWS, N_Z * SHARD - CORE_ROWS)] = jnp.zeros((N_Z * SHARD - CORE_ROWS, BLOCK), jnp.bfloat16)

    def join_step(i, _):
        rows = pl.ds(pl.multiple_of(i * HALF_ROWS, 16), HALF_ROWS)
        sib_message(i).wait()
        gh[rows] = (own_f32[rows] + from_sib[rows].astype(jnp.float32)).astype(jnp.bfloat16)
        return 0

    lax.fori_loop(0, 4, join_step, 0)

    def shard_rows(s):
        return pl.ds(pl.multiple_of(s * SHARD, 16), SHARD)

    f_cols, b_cols = pl.ds(0, FWD), pl.ds(FWD, BLOCK - FWD)
    f_copy = b_copy = None
    for t in range(N_Z - 1):
        sf, sb = (z + 7 - t + N_Z) % N_Z, (z + 1 + t) % N_Z
        if t == 0:
            f_src, b_src = gh.at[shard_rows(sf), f_cols], gh.at[shard_rows(sb), b_cols]
        else:
            f_copy.wait_recv()
            ring_f[t - 1] = (ring_f[t - 1].astype(jnp.float32) + gh[shard_rows(sf), f_cols].astype(jnp.float32)).astype(jnp.bfloat16)
            f_src, b_src = ring_f.at[t - 1], ring_b.at[t - 1]
        f_next = send(f_src, ring_f.at[t], dev_up)
        if t > 0:
            b_copy.wait_recv()
            ring_b[t - 1] = (ring_b[t - 1].astype(jnp.float32) + gh[shard_rows(sb), b_cols].astype(jnp.float32)).astype(jnp.bfloat16)
        b_next = send(b_src, ring_b.at[t], dev_down)
        f_copy, b_copy = f_next, b_next
    mine = shard_rows(z)
    f_copy.wait_recv()
    g_full[c, mine, f_cols] = (ring_f[N_Z - 2].astype(jnp.float32) + gh[mine, f_cols].astype(jnp.float32)).astype(jnp.bfloat16)
    b_copy.wait_recv()
    g_full[c, mine, b_cols] = (ring_b[N_Z - 2].astype(jnp.float32) + gh[mine, b_cols].astype(jnp.float32)).astype(jnp.bfloat16)

    pending = []

    def relay(rows, device):
        ref = g_full.at[c, rows]
        return send(ref, ref, device)

    up = relay(mine, dev_up)
    down = relay(mine, dev_down)
    pending.append(relay(mine, dev_sib))
    for step in range(1, 4):
        before, after = shard_rows((z + N_Z - step) % N_Z), shard_rows((z + step) % N_Z)
        if step == 3:
            before_next = pl.ds(pl.multiple_of(((z + N_Z - step) % N_Z) * SHARD, 16), HALF_SHARD)
            after_next = pl.ds(pl.multiple_of(((z + step) % N_Z) * SHARD + HALF_SHARD, 16), HALF_SHARD)
        else:
            before_next, after_next = before, after
        up.wait_recv()
        up = relay(before_next, dev_up)
        pending.append(relay(before, dev_sib))
        down.wait_recv()
        down = relay(after_next, dev_down)
        pending.append(relay(after, dev_sib))
    far = ((z + 4) % N_Z) * SHARD
    up.wait_recv()
    pending.append(relay(pl.ds(pl.multiple_of(far, 16), HALF_SHARD), dev_sib))
    down.wait_recv()
    pending.append(relay(pl.ds(pl.multiple_of(far + HALF_SHARD, 16), HALF_SHARD), dev_sib))
    for copy in pending:
        copy.wait_recv()

    def reduce4(axis, buf, cols, a_ref, b_ref, c_ref, d_ref, make):
        p = place[axis]
        right, left = near[axis]
        after, before, far = (p + 1) % RING, (p + 3) % RING, (p + 2) % RING
        make(far)
        a = send(buf.at[far, top], a_ref, right)
        b = send(buf.at[far, bottom], b_ref, left)
        make(after)
        c1 = send(buf.at[after, bottom], c_ref.at[bottom], right)
        make(before)
        d1 = send(buf.at[before, top], d_ref.at[top], left)
        a.wait_recv()
        buf[after, top] = (buf[after, top].astype(jnp.float32) + a_ref[...].astype(jnp.float32)).astype(jnp.bfloat16)
        c2 = send(buf.at[after, top], c_ref.at[top], right)
        b.wait_recv()
        buf[before, bottom] = (buf[before, bottom].astype(jnp.float32) + b_ref[...].astype(jnp.float32)).astype(jnp.bfloat16)
        d2 = send(buf.at[before, bottom], d_ref.at[bottom], left)
        return (c1, d1, c2, d2)

    def g_rows(q):
        return g_full[q // 2, pl.ds(pl.multiple_of((q % 2) * GROUP_ROWS, 16), GROUP_ROWS)]

    def make_y(q):
        part[q] = jnp.dot(g_rows(q), xs[...].reshape(BLOCK, SLAB), preferred_element_type=jnp.float32).astype(jnp.bfloat16)

    tail = reduce4("col", part, SLAB, got_a, got_b, got_c, got_d, make_y)
    y_f32[...] = jnp.dot(g_rows(x), xs[...].reshape(BLOCK, SLAB), preferred_element_type=jnp.float32)
    gather_end(tail)
    y_f32[...] = y_f32[...] + got_c[...].astype(jnp.float32) + got_d[...].astype(jnp.float32)
    ya[y] = y_f32[:, : SLAB // 2].astype(jnp.bfloat16)
    yb[x] = y_f32[:, SLAB // 2 :].astype(jnp.bfloat16)
    s1 = gather_start("row", ya)
    s2 = gather_start("col", yb)
    t1 = gather_pass("row", ya, s1)
    t2 = gather_pass("col", yb, s2)
    gather_end(t1)
    gather_end(t2)

    first, second = pl.ds(0, SLAB // 2), pl.ds(SLAB // 2, SLAB // 2)

    def make_za(q):
        part2[0, q] = jnp.dot(g_rows(q), ya[...].reshape(BLOCK, SLAB // 2), preferred_element_type=jnp.float32).astype(jnp.bfloat16)

    z_b[...] = jnp.zeros_like(z_b)
    for q in range(4):
        z_b[...] += lax.dot_general(
            g_full[q // 2, pl.ds((q % 2) * GROUP_ROWS, GROUP_ROWS)], yb[q], (((0,), (0,)), ((), ())),
            preferred_element_type=jnp.float32,
        )
    part2[1] = z_b[...].astype(jnp.bfloat16).reshape(4, GROUP_ROWS, SLAB // 2)

    ta = reduce4("col", part2.at[0], None, got_a.at[:, first], got_b.at[:, first], got_c.at[:, first], got_d.at[:, first], make_za)
    tb = reduce4("row", part2.at[1], None, got_a.at[:, second], got_b.at[:, second], got_c.at[:, second], got_d.at[:, second], lambda q: None)
    za_own = jnp.dot(g_rows(x), ya[...].reshape(BLOCK, SLAB // 2), preferred_element_type=jnp.float32)
    gather_end(ta)
    gather_end(tb)
    for cols, own in ((first, za_own), (second, z_b[pl.ds(pl.multiple_of(y * GROUP_ROWS, 8), GROUP_ROWS)])):
        z_val = own + got_c[:, cols].astype(jnp.float32) + got_d[:, cols].astype(jnp.float32)
        out_ref[:, cols] = (
            SCALE * (LINEAR_COEF * x_ref[:, cols].astype(jnp.float32) + (CUBIC_COEF * y_f32[:, cols] + QUINTIC_COEF * z_val))
        ).astype(jnp.bfloat16)
    for copy in started:
        copy.wait_send()


def newton_schulz(own_block):
    bf, f32 = jnp.bfloat16, jnp.float32
    vmem = pltpu.VMEM
    return pl.pallas_call(
        core_kernel,
        out_shape=jax.ShapeDtypeStruct((GROUP_ROWS, SLAB), bf),
        in_specs=[pl.BlockSpec(memory_space=pltpu.VMEM)],
        out_specs=pl.BlockSpec(memory_space=pltpu.VMEM),
        scratch_shapes=[
            vmem((RING, GROUP_ROWS, SLAB), bf),
            vmem((RING, GROUP_ROWS, SLAB), bf),
            vmem((CORE_ROWS, BLOCK), f32),
            vmem((CORE_ROWS, BLOCK), bf),
            vmem((CORE_ROWS, BLOCK), bf),
            vmem((N_Z * SHARD, BLOCK), bf),
            vmem((N_Z - 1, SHARD, FWD), bf),
            vmem((N_Z - 1, SHARD, BLOCK - FWD), bf),
            vmem((2, N_Z * SHARD, BLOCK), bf),
            vmem((RING, GROUP_ROWS, SLAB), bf),
            vmem((HALF_ROWS, SLAB), bf),
            vmem((HALF_ROWS, SLAB), bf),
            vmem((GROUP_ROWS, SLAB), bf),
            vmem((GROUP_ROWS, SLAB), bf),
            vmem((GROUP_ROWS, SLAB), f32),
            vmem((RING, GROUP_ROWS, SLAB // 2), bf),
            vmem((RING, GROUP_ROWS, SLAB // 2), bf),
            vmem((2, RING, GROUP_ROWS, SLAB // 2), bf),
            vmem((BLOCK, SLAB // 2), f32),
            pltpu.SemaphoreType.DMA((N_MESSAGES,)),
            pltpu.SemaphoreType.DMA((N_MESSAGES,)),
        ],
        compiler_params=pltpu.CompilerParams(
            collective_id=0, has_side_effects=True, vmem_limit_bytes=56 * 1024 * 1024
        ),
    )(own_block)


def local(flat_iterate, lengths):
    dp_count = lax.axis_size("dp")
    row_count = lax.axis_size("row")
    col_count = lax.axis_size("col")
    groups = row_count * col_count
    dp_index = lax.axis_index("dp")
    group_index = lax.axis_index("row") * col_count + lax.axis_index("col")
    capacity = flat_iterate.shape[1]
    span_rows = (capacity + COLS - 1) // COLS + 1
    group_rows = ROWS // groups
    slab_width = COLS // dp_count
    shard_ends = jnp.cumsum(lengths, axis=1)
    starts = shard_ends - lengths
    own_starts = lax.dynamic_index_in_dim(starts, group_index, 0, keepdims=False)
    own_lengths = lax.dynamic_index_in_dim(lengths, group_index, 0, keepdims=False)
    first_rows = own_starts // COLS
    my_start = lax.dynamic_index_in_dim(own_starts, dp_index, 0, keepdims=False)
    my_length = lax.dynamic_index_in_dim(own_lengths, dp_index, 0, keepdims=False)
    lead_cols = my_start - my_start // COLS * COLS
    places = jnp.arange(capacity, dtype=jnp.int32)
    segment = jnp.where(places < my_length, flat_iterate[0], jnp.zeros((), jnp.bfloat16))
    canvas = lax.dynamic_update_slice(
        jnp.zeros((span_rows * COLS,), jnp.bfloat16), segment, (lead_cols,)
    )
    canvas = canvas.reshape(span_rows, COLS)
    arrived = lax.all_to_all(canvas, "dp", split_axis=1, concat_axis=0, tiled=True)
    targets = (first_rows[:, None] + jnp.arange(span_rows, dtype=jnp.int32)[None, :]).reshape(-1)
    landing = jnp.zeros((group_rows + span_rows, slab_width), jnp.float32)
    landing = landing.at[targets].add(arrived.astype(jnp.float32))
    own_block = landing[:group_rows].astype(jnp.bfloat16)
    update = newton_schulz(own_block)
    padded = jnp.concatenate([update, jnp.zeros((span_rows, slab_width), jnp.bfloat16)], axis=0)
    outgoing = jnp.take(padded, targets, axis=0)
    returned = lax.all_to_all(outgoing, "dp", split_axis=0, concat_axis=1, tiled=True)
    flat_back = lax.dynamic_slice_in_dim(returned.reshape(-1), lead_cols, capacity)
    flat_back = jnp.where(places < my_length, flat_back, jnp.zeros((), jnp.bfloat16))
    return flat_back[None, :]


def solution(mesh):
    return jax.shard_map(
        local,
        mesh=mesh,
        in_specs=(P(("dp", "row", "col"), None), P()),
        out_specs=P(("dp", "row", "col"), None),
        check_vma=False,
    )
```

```python
import math

import jax
import jax.numpy as jnp
from jax import lax
from jax.experimental import pallas as pl
from jax.experimental.pallas import tpu as pltpu
from jax.sharding import PartitionSpec as P

COLS = 8192
ROWS = 5632


LINEAR_COEF = 3.4445
CUBIC_COEF = -4.775
QUINTIC_COEF = 2.0315

N_DP = 16
N_Z = 8
RING = 4
GROUP_ROWS = 352
HALF_ROWS = 176
SLAB = 512
BLOCK = 1408
CORE_ROWS = 704
SHARD = 96
HALF_SHARD = 48
LANES = 128
CHUNKS = COLS // LANES
FLAT_ROWS = 2112
MAIN = 32
EXTRA = 16
LEAD = 72
FWD = 768
N_MESSAGES = 160
MESH = pl.DeviceIdType.MESH
SCALE = 0.2 * math.sqrt(max(ROWS, COLS))


def core_kernel(
    lengths_ref, flat_ref, out_ref, staged, canvas, extra_tmp, extra, arrived, arrived_extra, back, x_ref, xr, xs, own_f32, to_sib, from_sib, gh, ring_f, ring_b, g_full,
    part, got_a, got_b, got_c, got_d, y_f32, ya, yb, part2, z_b, update, returned, returned_extra, send_sem, recv_sem,
):
    dp = lax.axis_index("dp")
    y = lax.axis_index("row")
    x = lax.axis_index("col")
    z, c = dp // 2, dp % 2
    sib_dp = z * 2 + 1 - c
    up_dp = ((z + 1) % N_Z) * 2 + c
    down_dp = ((z + 7) % N_Z) * 2 + c
    dev_sib = (sib_dp, y, x)
    dev_up = (up_dp, y, x)
    dev_down = (down_dp, y, x)
    near = {
        "col": ((dp, y, (x + 1) % RING), (dp, y, (x + 3) % RING)),
        "row": ((dp, (y + 1) % RING, x), (dp, (y + 3) % RING, x)),
    }
    place = {"col": x, "row": y}

    barrier = pltpu.get_barrier_semaphore()
    for peer in near["col"] + near["row"]:
        pl.semaphore_signal(barrier, inc=1, device_id=peer, device_id_type=MESH)

    def greet(o, _):
        pl.semaphore_signal(barrier, inc=1, device_id=((dp + o) % N_DP, y, x), device_id_type=MESH)
        return 0

    lax.fori_loop(1, N_DP, greet, 0)
    pl.semaphore_wait(barrier, 4 + N_DP - 1)

    counter = [4 * N_DP]
    started = []

    def message(src, dst, device, slot=None):
        if slot is None:
            slot = counter[0]
            counter[0] += 1
        return pltpu.make_async_remote_copy(
            src_ref=src, dst_ref=dst, send_sem=send_sem.at[slot], recv_sem=recv_sem.at[slot],
            device_id=device, device_id_type=MESH,
        )

    def send(src, dst, device):
        copy = message(src, dst, device)
        copy.start()
        started.append(copy)
        return copy

    top, bottom = pl.ds(0, HALF_ROWS), pl.ds(HALF_ROWS, HALF_ROWS)

    def gather_start(axis, buf):
        p = place[axis]
        right, left = near[axis]
        a = [send(buf.at[p, h], buf.at[p, h], right) for h in (top, bottom)]
        b = [send(buf.at[p, h], buf.at[p, h], left) for h in (bottom, top)]
        return a, b

    def gather_pass(axis, buf, state):
        p = place[axis]
        right, left = near[axis]
        a, b = state
        before, after = (p + 3) % RING, (p + 1) % RING
        a[0].wait_recv()
        f = send(buf.at[before, top], buf.at[before, top], right)
        b[0].wait_recv()
        g = send(buf.at[after, bottom], buf.at[after, bottom], left)
        return a[1], b[1], f, g

    def gather_end(tail):
        for copy in tail:
            copy.wait_recv()

    group = y * RING + x
    my_start = jnp.int32(0)
    begin = jnp.int32(0)
    first_rows = []
    for d in range(N_DP):
        first_rows.append(begin // COLS)
        my_start = jnp.where(dp == d, begin, my_start)
        begin = begin + lengths_ref[group, d]
    my_length = lengths_ref[group, dp]
    lead = my_start % COLS
    lead_rows, lead_lanes = lead // LANES, lead % LANES
    staged[pl.ds(0, LEAD)] = jnp.zeros((LEAD, LANES), jnp.float32)
    tail_rows = staged.shape[0] - LEAD - FLAT_ROWS
    staged[pl.ds(LEAD + FLAT_ROWS, tail_rows)] = jnp.zeros((tail_rows, LANES), jnp.float32)
    STEP = 176

    def slots(i):
        return (
            i * (STEP * LANES)
            + lax.broadcasted_iota(jnp.int32, (STEP, LANES), 0) * LANES
            + lax.broadcasted_iota(jnp.int32, (STEP, LANES), 1)
        )

    def stage(i, _):
        rows = pl.ds(pl.multiple_of(i * STEP, 8), STEP)
        value = jnp.where(slots(i) < my_length, flat_ref[rows], 0.0)
        staged[pl.ds(pl.multiple_of(i * STEP + LEAD, 8), STEP)] = pltpu.roll(value, lead_lanes, 1)
        return 0

    lax.fori_loop(0, FLAT_ROWS // STEP, stage, 0)
    extra_tmp[...] = jnp.zeros_like(extra_tmp)

    def exchange(o, base, src, src_extra, dst, dst_extra, there):
        device = (there, y, x)
        return (
            message(src, dst, device, slot=base + o),
            message(src_extra, dst_extra, device, slot=base + N_DP + o),
        )

    def out_copies(o):
        there = (dp + o) % N_DP
        return exchange(o, 0, canvas.at[there], extra.at[there], arrived.at[dp], arrived_extra.at[dp], there)

    def place_part(o, _):
        there = (dp + o) % N_DP
        lane = lax.broadcasted_iota(jnp.int32, (MAIN, LANES), 1)
        lane2 = lax.broadcasted_iota(jnp.int32, (2, LANES), 1)
        start = LEAD - lead_rows + there * 4
        before = staged[pl.ds(start - 1, MAIN, stride=CHUNKS)]
        before2 = staged[pl.ds(start - 1 + MAIN * CHUNKS, 2, stride=CHUNKS)]
        for j in range(4):
            here = staged[pl.ds(start + j, MAIN, stride=CHUNKS)]
            here2 = staged[pl.ds(start + j + MAIN * CHUNKS, 2, stride=CHUNKS)]
            canvas[there, :, pl.ds(j * LANES, LANES)] = jnp.where(lane >= lead_lanes, here, before).astype(jnp.bfloat16)
            extra_tmp[pl.ds(j * 2, 2)] = jnp.where(lane2 >= lead_lanes, here2, before2)
            before, before2 = here, here2
        extra[there] = extra_tmp[...].astype(jnp.bfloat16)

        @pl.when(o < N_DP)
        def _():
            for copy in out_copies(o):
                copy.start()

        return 0

    lax.fori_loop(1, N_DP + 1, place_part, 0)
    arrived[dp] = canvas[dp]
    arrived_extra[dp] = extra[dp]

    def targets(length, width, offset, shape, dim):
        k = lax.broadcasted_iota(jnp.int32, shape, dim)
        found = jnp.full(shape, -1, jnp.int32)
        for d in range(N_DP):
            inside = k // width == d
            found = jnp.where(inside, first_rows[d] + k % width + offset, found)
        return k, found

    k, row_of = targets(N_DP * MAIN, MAIN, 0, (1, N_DP * MAIN), 1)
    pick = (lax.broadcasted_iota(jnp.int32, (GROUP_ROWS, N_DP * MAIN), 0) == row_of).astype(jnp.float32).astype(jnp.bfloat16)
    ke, row_e = targets(N_DP * EXTRA, EXTRA, MAIN, (1, N_DP * EXTRA), 1)
    ke = ke % EXTRA

    def wait_out(o, _):
        for copy in out_copies(o):
            copy.wait()
        return 0

    lax.fori_loop(1, N_DP, wait_out, 0)
    x_main = jnp.dot(pick, arrived[...].reshape(N_DP * MAIN, SLAB), preferred_element_type=jnp.float32)
    late = arrived_extra[...].reshape(N_DP * EXTRA, LANES)
    for j in range(4):
        row_j = jnp.where(ke // 2 == j, row_e - 2 * j, -1)
        pick_j = (lax.broadcasted_iota(jnp.int32, (GROUP_ROWS, N_DP * EXTRA), 0) == row_j).astype(jnp.float32).astype(jnp.bfloat16)
        cols = slice(j * LANES, (j + 1) * LANES)
        x_ref[:, cols] = (
            x_main[:, cols] + jnp.dot(pick_j, late, preferred_element_type=jnp.float32)
        ).astype(jnp.bfloat16)

    xr[x] = x_ref[...]
    xs[y] = x_ref[...]
    s1 = gather_start("col", xr)
    s2 = gather_start("row", xs)
    t1 = gather_pass("col", xr, s1)
    t2 = gather_pass("row", xs, s2)
    gather_end(t1)
    gather_end(t2)

    base = counter[0]
    counter[0] += 4

    def sib_message(i):
        rows = pl.ds(pl.multiple_of(i * HALF_ROWS, 16), HALF_ROWS)
        return message(to_sib.at[rows], from_sib.at[rows], dev_sib, slot=base + i)

    def gram_tile(half, i):
        left = xr[2 * half + i // 2, pl.ds(pl.multiple_of((i % 2) * HALF_ROWS, 16), HALF_ROWS)]
        return lax.dot_general(
            left, xs[...].reshape(BLOCK, SLAB), (((1,), (1,)), ((), ())), preferred_element_type=jnp.float32
        )

    def sib_step(i, _):
        rows = pl.ds(pl.multiple_of(i * HALF_ROWS, 16), HALF_ROWS)
        to_sib[rows] = gram_tile(1 - c, i).astype(jnp.bfloat16)
        sib_message(i).start()
        return 0

    lax.fori_loop(0, 4, sib_step, 0)

    def own_step(i, _):
        rows = pl.ds(pl.multiple_of(i * HALF_ROWS, 16), HALF_ROWS)
        own_f32[rows] = gram_tile(c, i)
        return 0

    lax.fori_loop(0, 4, own_step, 0)
    gh[pl.ds(CORE_ROWS, N_Z * SHARD - CORE_ROWS)] = jnp.zeros((N_Z * SHARD - CORE_ROWS, BLOCK), jnp.bfloat16)

    def join_step(i, _):
        rows = pl.ds(pl.multiple_of(i * HALF_ROWS, 16), HALF_ROWS)
        sib_message(i).wait()
        gh[rows] = (own_f32[rows] + from_sib[rows].astype(jnp.float32)).astype(jnp.bfloat16)
        return 0

    lax.fori_loop(0, 4, join_step, 0)

    def shard_rows(s):
        return pl.ds(pl.multiple_of(s * SHARD, 16), SHARD)

    f_cols, b_cols = pl.ds(0, FWD), pl.ds(FWD, BLOCK - FWD)
    f_copy = b_copy = None
    for t in range(N_Z - 1):
        sf, sb = (z + 7 - t + N_Z) % N_Z, (z + 1 + t) % N_Z
        if t == 0:
            f_src, b_src = gh.at[shard_rows(sf), f_cols], gh.at[shard_rows(sb), b_cols]
        else:
            f_copy.wait_recv()
            ring_f[t - 1] = (ring_f[t - 1].astype(jnp.float32) + gh[shard_rows(sf), f_cols].astype(jnp.float32)).astype(jnp.bfloat16)
            f_src, b_src = ring_f.at[t - 1], ring_b.at[t - 1]
        f_next = send(f_src, ring_f.at[t], dev_up)
        if t > 0:
            b_copy.wait_recv()
            ring_b[t - 1] = (ring_b[t - 1].astype(jnp.float32) + gh[shard_rows(sb), b_cols].astype(jnp.float32)).astype(jnp.bfloat16)
        b_next = send(b_src, ring_b.at[t], dev_down)
        f_copy, b_copy = f_next, b_next
    mine = shard_rows(z)
    f_copy.wait_recv()
    g_full[c, mine, f_cols] = (ring_f[N_Z - 2].astype(jnp.float32) + gh[mine, f_cols].astype(jnp.float32)).astype(jnp.bfloat16)
    b_copy.wait_recv()
    g_full[c, mine, b_cols] = (ring_b[N_Z - 2].astype(jnp.float32) + gh[mine, b_cols].astype(jnp.float32)).astype(jnp.bfloat16)

    pending = []

    def relay(rows, device):
        ref = g_full.at[c, rows]
        return send(ref, ref, device)

    up = relay(mine, dev_up)
    down = relay(mine, dev_down)
    pending.append(relay(mine, dev_sib))
    for step in range(1, 4):
        before, after = shard_rows((z + N_Z - step) % N_Z), shard_rows((z + step) % N_Z)
        if step == 3:
            before_next = pl.ds(pl.multiple_of(((z + N_Z - step) % N_Z) * SHARD, 16), HALF_SHARD)
            after_next = pl.ds(pl.multiple_of(((z + step) % N_Z) * SHARD + HALF_SHARD, 16), HALF_SHARD)
        else:
            before_next, after_next = before, after
        up.wait_recv()
        up = relay(before_next, dev_up)
        pending.append(relay(before, dev_sib))
        down.wait_recv()
        down = relay(after_next, dev_down)
        pending.append(relay(after, dev_sib))
    far = ((z + 4) % N_Z) * SHARD
    up.wait_recv()
    pending.append(relay(pl.ds(pl.multiple_of(far, 16), HALF_SHARD), dev_sib))
    down.wait_recv()
    pending.append(relay(pl.ds(pl.multiple_of(far + HALF_SHARD, 16), HALF_SHARD), dev_sib))
    for copy in pending:
        copy.wait_recv()

    def reduce4(axis, buf, cols, a_ref, b_ref, c_ref, d_ref, make):
        p = place[axis]
        right, left = near[axis]
        after, before, far = (p + 1) % RING, (p + 3) % RING, (p + 2) % RING
        make(far)
        a = send(buf.at[far, top], a_ref, right)
        b = send(buf.at[far, bottom], b_ref, left)
        make(after)
        c1 = send(buf.at[after, bottom], c_ref.at[bottom], right)
        make(before)
        d1 = send(buf.at[before, top], d_ref.at[top], left)
        a.wait_recv()
        buf[after, top] = (buf[after, top].astype(jnp.float32) + a_ref[...].astype(jnp.float32)).astype(jnp.bfloat16)
        c2 = send(buf.at[after, top], c_ref.at[top], right)
        b.wait_recv()
        buf[before, bottom] = (buf[before, bottom].astype(jnp.float32) + b_ref[...].astype(jnp.float32)).astype(jnp.bfloat16)
        d2 = send(buf.at[before, bottom], d_ref.at[bottom], left)
        return (c1, d1, c2, d2)

    def g_rows(q):
        return g_full[q // 2, pl.ds(pl.multiple_of((q % 2) * GROUP_ROWS, 16), GROUP_ROWS)]

    def make_y(q):
        part[q] = jnp.dot(g_rows(q), xs[...].reshape(BLOCK, SLAB), preferred_element_type=jnp.float32).astype(jnp.bfloat16)

    tail = reduce4("col", part, SLAB, got_a, got_b, got_c, got_d, make_y)
    y_f32[...] = jnp.dot(g_rows(x), xs[...].reshape(BLOCK, SLAB), preferred_element_type=jnp.float32)
    gather_end(tail)
    y_f32[...] = y_f32[...] + got_c[...].astype(jnp.float32) + got_d[...].astype(jnp.float32)
    ya[y] = y_f32[:, : SLAB // 2].astype(jnp.bfloat16)
    yb[x] = y_f32[:, SLAB // 2 :].astype(jnp.bfloat16)
    s1 = gather_start("row", ya)
    s2 = gather_start("col", yb)
    t1 = gather_pass("row", ya, s1)
    t2 = gather_pass("col", yb, s2)
    gather_end(t1)
    gather_end(t2)

    first, second = pl.ds(0, SLAB // 2), pl.ds(SLAB // 2, SLAB // 2)

    def make_za(q):
        part2[0, q] = jnp.dot(g_rows(q), ya[...].reshape(BLOCK, SLAB // 2), preferred_element_type=jnp.float32).astype(jnp.bfloat16)

    z_b[...] = jnp.zeros_like(z_b)
    for q in range(4):
        z_b[...] += lax.dot_general(
            g_full[q // 2, pl.ds((q % 2) * GROUP_ROWS, GROUP_ROWS)], yb[q], (((0,), (0,)), ((), ())),
            preferred_element_type=jnp.float32,
        )
    part2[1] = z_b[...].astype(jnp.bfloat16).reshape(4, GROUP_ROWS, SLAB // 2)

    ta = reduce4("col", part2.at[0], None, got_a.at[:, first], got_b.at[:, first], got_c.at[:, first], got_d.at[:, first], make_za)
    tb = reduce4("row", part2.at[1], None, got_a.at[:, second], got_b.at[:, second], got_c.at[:, second], got_d.at[:, second], lambda q: None)
    za_own = jnp.dot(g_rows(x), ya[...].reshape(BLOCK, SLAB // 2), preferred_element_type=jnp.float32)
    gather_end(ta)
    gather_end(tb)
    for cols, own in ((first, za_own), (second, z_b[pl.ds(pl.multiple_of(y * GROUP_ROWS, 8), GROUP_ROWS)])):
        z_val = own + got_c[:, cols].astype(jnp.float32) + got_d[:, cols].astype(jnp.float32)
        update[:, cols] = (
            SCALE * (LINEAR_COEF * x_ref[:, cols].astype(jnp.float32) + (CUBIC_COEF * y_f32[:, cols] + QUINTIC_COEF * z_val))
        ).astype(jnp.bfloat16)

    _, row_of = targets(N_DP * MAIN, MAIN, 0, (N_DP * MAIN, 1), 0)
    pick = (lax.broadcasted_iota(jnp.int32, (N_DP * MAIN, GROUP_ROWS), 1) == row_of).astype(jnp.float32).astype(jnp.bfloat16)
    canvas[...] = jnp.dot(pick, update[...], preferred_element_type=jnp.float32).astype(jnp.bfloat16).reshape(N_DP, MAIN, SLAB)
    ke, row_e = targets(N_DP * EXTRA, EXTRA, MAIN, (N_DP * EXTRA, 1), 0)
    ke = ke % EXTRA
    late = jnp.zeros((N_DP * EXTRA, LANES), jnp.float32)
    for j in range(4):
        row_j = jnp.where(ke // 2 == j, row_e - 2 * j, -1)
        pick_j = (lax.broadcasted_iota(jnp.int32, (N_DP * EXTRA, GROUP_ROWS), 1) == row_j).astype(jnp.float32).astype(jnp.bfloat16)
        late += jnp.dot(pick_j, update[:, j * LANES : (j + 1) * LANES], preferred_element_type=jnp.float32)
    extra[...] = late.astype(jnp.bfloat16).reshape(N_DP, EXTRA, LANES)

    def back_copies(o):
        there = (dp + o) % N_DP
        return exchange(o, 2 * N_DP, canvas.at[there], extra.at[there], returned.at[dp], returned_extra.at[dp], there)

    def send_back(o, _):
        for copy in back_copies(o):
            copy.start()
        return 0

    lax.fori_loop(1, N_DP, send_back, 0)
    returned[dp] = canvas[dp]
    returned_extra[dp] = extra[dp]

    def wait_back(o, _):
        for copy in back_copies(o):
            copy.wait()
        return 0

    lax.fori_loop(1, N_DP, wait_back, 0)

    def unpack(d, _):
        extra_tmp[...] = returned_extra[d].astype(jnp.float32)
        for j in range(4):
            back[pl.ds(d * 4 + j, MAIN, stride=CHUNKS)] = pltpu.roll(
                returned[d, :, pl.ds(j * LANES, LANES)].astype(jnp.float32), (LANES - lead_lanes) % LANES, 1)
            back[pl.ds(d * 4 + j + MAIN * CHUNKS, 2, stride=CHUNKS)] = pltpu.roll(
                extra_tmp[...], (LANES - lead_lanes) % LANES, 1)[2 * j : 2 * j + 2]
        return 0

    lax.fori_loop(0, N_DP, unpack, 0)
    back[pl.ds(34 * CHUNKS, 8)] = jnp.zeros((8, LANES), jnp.float32)

    def finish(i, _):
        here = back[pl.ds(i * STEP + lead_rows, STEP)]
        after = back[pl.ds(i * STEP + lead_rows + 1, STEP)]
        lane = lax.broadcasted_iota(jnp.int32, (STEP, LANES), 1)
        value = jnp.where(lane + lead_lanes < LANES, here, after)
        out_ref[pl.ds(pl.multiple_of(i * STEP, 8), STEP)] = jnp.where(slots(i) < my_length, value, 0.0)
        return 0

    lax.fori_loop(0, FLAT_ROWS // STEP, finish, 0)
    for copy in started:
        copy.wait_send()


def newton_schulz(lengths, flat):
    bf, f32 = jnp.bfloat16, jnp.float32
    vmem = pltpu.VMEM
    return pl.pallas_call(
        core_kernel,
        out_shape=jax.ShapeDtypeStruct((FLAT_ROWS, LANES), f32),
        in_specs=[pl.BlockSpec(memory_space=pltpu.SMEM), pl.BlockSpec(memory_space=pltpu.VMEM)],
        out_specs=pl.BlockSpec(memory_space=pltpu.VMEM),
        scratch_shapes=[
            vmem((LEAD + FLAT_ROWS + 88, LANES), f32),
            vmem((N_DP, MAIN, SLAB), bf),
            vmem((EXTRA, LANES), f32),
            vmem((N_DP, EXTRA, LANES), bf),
            vmem((N_DP, MAIN, SLAB), bf),
            vmem((N_DP, EXTRA, LANES), bf),
            vmem((34 * CHUNKS + 8, LANES), f32),
            vmem((GROUP_ROWS, SLAB), bf),
            vmem((RING, GROUP_ROWS, SLAB), bf),
            vmem((RING, GROUP_ROWS, SLAB), bf),
            vmem((CORE_ROWS, BLOCK), f32),
            vmem((CORE_ROWS, BLOCK), bf),
            vmem((CORE_ROWS, BLOCK), bf),
            vmem((N_Z * SHARD, BLOCK), bf),
            vmem((N_Z - 1, SHARD, FWD), bf),
            vmem((N_Z - 1, SHARD, BLOCK - FWD), bf),
            vmem((2, N_Z * SHARD, BLOCK), bf),
            vmem((RING, GROUP_ROWS, SLAB), bf),
            vmem((HALF_ROWS, SLAB), bf),
            vmem((HALF_ROWS, SLAB), bf),
            vmem((GROUP_ROWS, SLAB), bf),
            vmem((GROUP_ROWS, SLAB), bf),
            vmem((GROUP_ROWS, SLAB), f32),
            vmem((RING, GROUP_ROWS, SLAB // 2), bf),
            vmem((RING, GROUP_ROWS, SLAB // 2), bf),
            vmem((2, RING, GROUP_ROWS, SLAB // 2), bf),
            vmem((BLOCK, SLAB // 2), f32),
            vmem((GROUP_ROWS, SLAB), bf),
            vmem((N_DP, MAIN, SLAB), bf),
            vmem((N_DP, EXTRA, LANES), bf),
            pltpu.SemaphoreType.DMA((N_MESSAGES,)),
            pltpu.SemaphoreType.DMA((N_MESSAGES,)),
        ],
        compiler_params=pltpu.CompilerParams(
            collective_id=0, has_side_effects=True, vmem_limit_bytes=56 * 1024 * 1024
        ),
    )(lengths, flat)


def local(flat_iterate, lengths):
    flat = flat_iterate.astype(jnp.float32).reshape(FLAT_ROWS, LANES)
    return newton_schulz(lengths, flat).reshape(1, FLAT_ROWS * LANES).astype(jnp.bfloat16)


def solution(mesh):
    return jax.shard_map(
        local,
        mesh=mesh,
        in_specs=(P(("dp", "row", "col"), None), P()),
        out_specs=P(("dp", "row", "col"), None),
        check_vma=False,
    )
```

```python
import math

import jax
import jax.numpy as jnp
from jax import lax
from jax.experimental import pallas as pl
from jax.experimental.pallas import tpu as pltpu
from jax.sharding import PartitionSpec as P

COLS = 8192
ROWS = 5632


LINEAR_COEF = 3.4445
CUBIC_COEF = -4.775
QUINTIC_COEF = 2.0315

N_DP = 16
N_Z = 8
RING = 4
GROUP_ROWS = 352
HALF_ROWS = 176
SLAB = 512
BLOCK = 1408
CORE_ROWS = 704
SHARD = 48
PANEL = N_Z * SHARD
HALF_SLAB = SLAB // 2
LANES = 128
CHUNKS = COLS // LANES
FLAT_ROWS = 2112
MAIN = 32
EXTRA = 16
LEAD = 72
N_MESSAGES = 160
MESH = pl.DeviceIdType.MESH
SCALE = 0.2 * math.sqrt(max(ROWS, COLS))


def core_kernel(
    lengths_ref, flat_ref, out_ref, staged, canvas, extra_tmp, extra, arrived, arrived_extra, back, x_ref, xr, xs, own_f32, to_sib, from_sib, gh, ring_f, ring_b, g_full,
    part, got_a, got_b, got_c, got_d, y_f32, ya, yb, part2, z_b, z_f32, update, returned, returned_extra, send_sem, recv_sem,
):
    dp = lax.axis_index("dp")
    y = lax.axis_index("row")
    x = lax.axis_index("col")
    z, c = dp // 2, dp % 2
    sib_dp = z * 2 + 1 - c
    up_dp = ((z + 1) % N_Z) * 2 + c
    down_dp = ((z + 7) % N_Z) * 2 + c
    dev_sib = (sib_dp, y, x)
    dev_up = (up_dp, y, x)
    dev_down = (down_dp, y, x)
    near = {
        "col": ((dp, y, (x + 1) % RING), (dp, y, (x + 3) % RING)),
        "row": ((dp, (y + 1) % RING, x), (dp, (y + 3) % RING, x)),
    }
    place = {"col": x, "row": y}

    barrier = pltpu.get_barrier_semaphore()
    for peer in near["col"] + near["row"]:
        pl.semaphore_signal(barrier, inc=1, device_id=peer, device_id_type=MESH)

    def greet(o, _):
        pl.semaphore_signal(barrier, inc=1, device_id=((dp + o) % N_DP, y, x), device_id_type=MESH)
        return 0

    lax.fori_loop(1, N_DP, greet, 0)

    counter = [4 * N_DP]
    started = []

    def message(src, dst, device, slot=None):
        if slot is None:
            slot = counter[0]
            counter[0] += 1
        return pltpu.make_async_remote_copy(
            src_ref=src, dst_ref=dst, send_sem=send_sem.at[slot], recv_sem=recv_sem.at[slot],
            device_id=device, device_id_type=MESH,
        )

    def send(src, dst, device):
        copy = message(src, dst, device)
        copy.start()
        started.append(copy)
        return copy

    top, bottom = pl.ds(0, HALF_ROWS), pl.ds(HALF_ROWS, HALF_ROWS)

    def gather_start(axis, buf):
        p = place[axis]
        right, left = near[axis]
        a = [send(buf.at[p, h], buf.at[p, h], right) for h in (top, bottom)]
        b = [send(buf.at[p, h], buf.at[p, h], left) for h in (bottom, top)]
        return a, b

    def gather_pass(axis, buf, state):
        p = place[axis]
        right, left = near[axis]
        a, b = state
        before, after = (p + 3) % RING, (p + 1) % RING
        a[0].wait_recv()
        f = send(buf.at[before, top], buf.at[before, top], right)
        b[0].wait_recv()
        g = send(buf.at[after, bottom], buf.at[after, bottom], left)
        return a[1], b[1], f, g

    def gather_end(tail):
        for copy in tail:
            copy.wait_recv()

    group = y * RING + x
    my_start = jnp.int32(0)
    begin = jnp.int32(0)
    first_rows = []
    for d in range(N_DP):
        first_rows.append(begin // COLS)
        my_start = jnp.where(dp == d, begin, my_start)
        begin = begin + lengths_ref[group, d]
    my_length = lengths_ref[group, dp]
    lead = my_start % COLS
    lead_rows, lead_lanes = lead // LANES, lead % LANES
    staged[pl.ds(0, LEAD)] = jnp.zeros((LEAD, LANES), jnp.float32)
    tail_rows = staged.shape[0] - LEAD - FLAT_ROWS
    staged[pl.ds(LEAD + FLAT_ROWS, tail_rows)] = jnp.zeros((tail_rows, LANES), jnp.float32)
    STEP = 176

    def slots(i):
        return (
            i * (STEP * LANES)
            + lax.broadcasted_iota(jnp.int32, (STEP, LANES), 0) * LANES
            + lax.broadcasted_iota(jnp.int32, (STEP, LANES), 1)
        )

    def stage(i, _):
        rows = pl.ds(pl.multiple_of(i * STEP, 8), STEP)
        value = jnp.where(slots(i) < my_length, flat_ref[rows], 0.0)
        staged[pl.ds(pl.multiple_of(i * STEP + LEAD, 8), STEP)] = pltpu.roll(value, lead_lanes, 1)
        return 0

    lax.fori_loop(0, FLAT_ROWS // STEP, stage, 0)
    extra_tmp[...] = jnp.zeros_like(extra_tmp)

    def exchange(o, base, src, src_extra, dst, dst_extra, there):
        device = (there, y, x)
        return (
            message(src, dst, device, slot=base + o),
            message(src_extra, dst_extra, device, slot=base + N_DP + o),
        )

    def out_copies(o):
        there = (dp + o) % N_DP
        return exchange(o, 0, canvas.at[there], extra.at[there], arrived.at[dp], arrived_extra.at[dp], there)

    def place_part(o, _):
        there = (dp + o) % N_DP
        lane = lax.broadcasted_iota(jnp.int32, (MAIN, LANES), 1)
        lane2 = lax.broadcasted_iota(jnp.int32, (2, LANES), 1)
        start = LEAD - lead_rows + there * 4
        before = staged[pl.ds(start - 1, MAIN, stride=CHUNKS)]
        before2 = staged[pl.ds(start - 1 + MAIN * CHUNKS, 2, stride=CHUNKS)]
        for j in range(4):
            here = staged[pl.ds(start + j, MAIN, stride=CHUNKS)]
            here2 = staged[pl.ds(start + j + MAIN * CHUNKS, 2, stride=CHUNKS)]
            canvas[there, :, pl.ds(j * LANES, LANES)] = jnp.where(lane >= lead_lanes, here, before).astype(jnp.bfloat16)
            extra_tmp[pl.ds(j * 2, 2)] = jnp.where(lane2 >= lead_lanes, here2, before2)
            before, before2 = here, here2
        extra[there] = extra_tmp[...].astype(jnp.bfloat16)
        return 0

    lax.fori_loop(1, N_DP + 1, place_part, 0)
    pl.semaphore_wait(barrier, 4 + N_DP - 1)

    def send_out(o, _):
        for copy in out_copies(o):
            copy.start()
        return 0

    lax.fori_loop(1, N_DP, send_out, 0)
    arrived[dp] = canvas[dp]
    arrived_extra[dp] = extra[dp]

    def targets(length, width, offset, shape, dim):
        k = lax.broadcasted_iota(jnp.int32, shape, dim)
        found = jnp.full(shape, -1, jnp.int32)
        for d in range(N_DP):
            inside = k // width == d
            found = jnp.where(inside, first_rows[d] + k % width + offset, found)
        return k, found

    k, row_of = targets(N_DP * MAIN, MAIN, 0, (1, N_DP * MAIN), 1)
    pick = (lax.broadcasted_iota(jnp.int32, (GROUP_ROWS, N_DP * MAIN), 0) == row_of).astype(jnp.float32).astype(jnp.bfloat16)
    ke, row_e = targets(N_DP * EXTRA, EXTRA, MAIN, (1, N_DP * EXTRA), 1)
    ke = ke % EXTRA

    def wait_out(o, _):
        for copy in out_copies(o):
            copy.wait()
        return 0

    lax.fori_loop(1, N_DP, wait_out, 0)
    x_main = jnp.dot(pick, arrived[...].reshape(N_DP * MAIN, SLAB), preferred_element_type=jnp.float32)
    late = arrived_extra[...].reshape(N_DP * EXTRA, LANES)
    for j in range(4):
        row_j = jnp.where(ke // 2 == j, row_e - 2 * j, -1)
        pick_j = (lax.broadcasted_iota(jnp.int32, (GROUP_ROWS, N_DP * EXTRA), 0) == row_j).astype(jnp.float32).astype(jnp.bfloat16)
        cols = slice(j * LANES, (j + 1) * LANES)
        x_ref[:, cols] = (
            x_main[:, cols] + jnp.dot(pick_j, late, preferred_element_type=jnp.float32)
        ).astype(jnp.bfloat16)

    pad = pl.ds(GROUP_ROWS, PANEL - GROUP_ROWS)
    for q in range(RING):
        xr[q, pad] = jnp.zeros((PANEL - GROUP_ROWS, SLAB), jnp.bfloat16)
        yb[q, pad] = jnp.zeros((PANEL - GROUP_ROWS, HALF_SLAB), jnp.bfloat16)
    for p in range(2):
        gh[p, pad] = jnp.zeros((PANEL - GROUP_ROWS, BLOCK), jnp.bfloat16)
    xr[x, pl.ds(0, GROUP_ROWS)] = x_ref[...]
    xs[y] = x_ref[...]
    s1 = gather_start("col", xr)
    s2 = gather_start("row", xs)
    t1 = gather_pass("col", xr, s1)
    t2 = gather_pass("row", xs, s2)
    gather_end(t1)
    gather_end(t2)

    base = counter[0]
    counter[0] += 4

    def sib_message(i):
        rows = pl.ds(pl.multiple_of(i * HALF_ROWS, 16), HALF_ROWS)
        return message(to_sib.at[rows], from_sib.at[rows], dev_sib, slot=base + i)

    def gram_tile(half, i):
        left = xr[2 * half + i // 2, pl.ds(pl.multiple_of((i % 2) * HALF_ROWS, 16), HALF_ROWS)]
        return lax.dot_general(
            left, xs[...].reshape(BLOCK, SLAB), (((1,), (1,)), ((), ())), preferred_element_type=jnp.float32
        )

    def sib_step(i, _):
        rows = pl.ds(pl.multiple_of(i * HALF_ROWS, 16), HALF_ROWS)
        to_sib[rows] = gram_tile(1 - c, i).astype(jnp.bfloat16)
        sib_message(i).start()
        return 0

    lax.fori_loop(0, 4, sib_step, 0)

    def own_step(i, _):
        rows = pl.ds(pl.multiple_of(i * HALF_ROWS, 16), HALF_ROWS)
        own_f32[rows] = gram_tile(c, i)
        return 0

    lax.fori_loop(0, 4, own_step, 0)
    def join_step(i, _):
        rows = pl.ds(pl.multiple_of(i * HALF_ROWS, 16), HALF_ROWS)
        sib_message(i).wait()
        part_rows = pl.ds(pl.multiple_of((i % 2) * HALF_ROWS, 16), HALF_ROWS)
        gh[i // 2, part_rows] = (own_f32[rows] + from_sib[rows].astype(jnp.float32)).astype(jnp.bfloat16)
        return 0

    lax.fori_loop(0, 4, join_step, 0)

    def shard_rows(s):
        return pl.ds(pl.multiple_of(((s + N_Z) % N_Z) * SHARD, 16), SHARD)

    f32 = jnp.float32
    up_in, down_in = [], []
    for k in range(7):
        distance = 4 - (k + 1) // 2
        for upward in (True, False):
            panel = k % 2 if upward else 1 - k % 2
            rows = shard_rows(z + distance if upward else z - distance)
            arrivals, ring, device = (up_in, ring_f, dev_up) if upward else (down_in, ring_b, dev_down)
            if k < 2:
                src = gh.at[panel, rows]
            else:
                arrivals[k - 2].wait_recv()
                ring[k - 2] = (ring[k - 2].astype(f32) + gh[panel, rows].astype(f32)).astype(jnp.bfloat16)
                src = ring.at[k - 2]
            arrivals.append(send(src, ring.at[k], device))
    mine = shard_rows(z)
    for panel, k_up, k_down in ((0, 6, 5), (1, 5, 6)):
        up_in[k_up].wait_recv()
        down_in[k_down].wait_recv()
        g_full[2 * c + panel, mine] = (
            gh[panel, mine].astype(f32) + ring_f[k_up].astype(f32) + ring_b[k_down].astype(f32)
        ).astype(jnp.bfloat16)

    pending = []

    def relay(panel, rows, device):
        ref = g_full.at[2 * c + panel, rows]
        return send(ref, ref, device)

    up_in, down_in = [], []
    for k in range(9):
        back_by = k // 2
        up_part, down_part = (k % 2, shard_rows(z - back_by)), (1 - k % 2, shard_rows(z + back_by))
        if k >= 2:
            up_in[k - 2].wait_recv()
        if k < 7:
            up_in.append(relay(*up_part, dev_up))
        if k >= 2:
            down_in[k - 2].wait_recv()
        if k < 7:
            down_in.append(relay(*down_part, dev_down))
        pending.append(relay(*up_part, dev_sib))
        if k >= 2:
            pending.append(relay(*down_part, dev_sib))
    for copy in pending:
        copy.wait_recv()

    def reduce_start(axis, buf, a_ref, b_ref):
        p = place[axis]
        right, left = near[axis]
        far = (p + 2) % RING
        return (send(buf.at[far, top], a_ref, right), send(buf.at[far, bottom], b_ref, left))

    def reduce_near(axis, buf, c_ref, d_ref):
        p = place[axis]
        right, left = near[axis]
        after, before = (p + 1) % RING, (p + 3) % RING
        return (
            send(buf.at[after, bottom], c_ref.at[bottom], right),
            send(buf.at[before, top], d_ref.at[top], left),
        )

    def reduce_pass(axis, buf, a_ref, b_ref, c_ref, d_ref, state):
        p = place[axis]
        right, left = near[axis]
        after, before = (p + 1) % RING, (p + 3) % RING
        state[0].wait_recv()
        buf[after, top] = (buf[after, top].astype(f32) + a_ref[...].astype(f32)).astype(jnp.bfloat16)
        c2 = send(buf.at[after, top], c_ref.at[top], right)
        state[1].wait_recv()
        buf[before, bottom] = (buf[before, bottom].astype(f32) + b_ref[...].astype(f32)).astype(jnp.bfloat16)
        d2 = send(buf.at[before, bottom], d_ref.at[bottom], left)
        return (c2, d2)

    first, second = pl.ds(0, HALF_SLAB), pl.ds(HALF_SLAB, HALF_SLAB)

    def apply_gram(right_a, right_b, buf, total):
        def make(q):
            return jnp.dot(g_full[q, pl.ds(0, GROUP_ROWS)], right_a(), preferred_element_type=f32)

        far, after, before = (x + 2) % RING, (x + 1) % RING, (x + 3) % RING
        buf_a, buf_b = buf.at[0], buf.at[1]
        slots = [[r.at[i] for r in (got_a, got_b, got_c, got_d)] for i in range(2)]
        buf_a[far] = make(far).astype(jnp.bfloat16)
        sa = reduce_start("col", buf_a, *slots[0][:2])

        def columns(j, _):
            cols = pl.ds(pl.multiple_of(j * LANES, LANES), LANES)
            z_b[cols] = lax.dot_general(
                g_full[:, :, cols].reshape(RING * PANEL, LANES), right_b(), (((0,), (0,)), ((), ())),
                preferred_element_type=f32,
            )
            return 0

        lax.fori_loop(0, BLOCK // LANES, columns, 0)
        buf_b[...] = z_b[...].astype(jnp.bfloat16).reshape(RING, GROUP_ROWS, HALF_SLAB)
        sb = reduce_start("row", buf_b, *slots[1][:2])
        nb = reduce_near("row", buf_b, *slots[1][2:])
        buf_a[after] = make(after).astype(jnp.bfloat16)
        buf_a[before] = make(before).astype(jnp.bfloat16)
        na = reduce_near("col", buf_a, *slots[0][2:])
        pa = reduce_pass("col", buf_a, *slots[0], sa)
        pb = reduce_pass("row", buf_b, *slots[1], sb)
        total[:, first] = make(x)
        total[:, second] = z_b[pl.ds(pl.multiple_of(y * GROUP_ROWS, 8), GROUP_ROWS)]
        for i, (cols, tail) in enumerate(((first, na + pa), (second, nb + pb))):
            gather_end(tail)
            total[:, cols] = total[:, cols] + got_c[i].astype(f32) + got_d[i].astype(f32)

    apply_gram(
        lambda: xs[:, :, :HALF_SLAB].reshape(BLOCK, HALF_SLAB),
        lambda: xr[:, :, HALF_SLAB:].reshape(RING * PANEL, HALF_SLAB),
        part, y_f32,
    )
    ya[y] = y_f32[:, :HALF_SLAB].astype(jnp.bfloat16)
    yb[x, pl.ds(0, GROUP_ROWS)] = y_f32[:, HALF_SLAB:].astype(jnp.bfloat16)
    s1 = gather_start("row", ya)
    s2 = gather_start("col", yb)
    t1 = gather_pass("row", ya, s1)
    t2 = gather_pass("col", yb, s2)
    gather_end(t1)
    gather_end(t2)

    apply_gram(
        lambda: ya[...].reshape(BLOCK, HALF_SLAB),
        lambda: yb[...].reshape(RING * PANEL, HALF_SLAB),
        part2, z_f32,
    )
    update[...] = (
        SCALE * (LINEAR_COEF * x_ref[...].astype(f32) + (CUBIC_COEF * y_f32[...] + QUINTIC_COEF * z_f32[...]))
    ).astype(jnp.bfloat16)

    _, row_of = targets(N_DP * MAIN, MAIN, 0, (N_DP * MAIN, 1), 0)
    pick = (lax.broadcasted_iota(jnp.int32, (N_DP * MAIN, GROUP_ROWS), 1) == row_of).astype(jnp.float32).astype(jnp.bfloat16)
    canvas[...] = jnp.dot(pick, update[...], preferred_element_type=jnp.float32).astype(jnp.bfloat16).reshape(N_DP, MAIN, SLAB)
    ke, row_e = targets(N_DP * EXTRA, EXTRA, MAIN, (N_DP * EXTRA, 1), 0)
    ke = ke % EXTRA
    late = jnp.zeros((N_DP * EXTRA, LANES), jnp.float32)
    for j in range(4):
        row_j = jnp.where(ke // 2 == j, row_e - 2 * j, -1)
        pick_j = (lax.broadcasted_iota(jnp.int32, (N_DP * EXTRA, GROUP_ROWS), 1) == row_j).astype(jnp.float32).astype(jnp.bfloat16)
        late += jnp.dot(pick_j, update[:, j * LANES : (j + 1) * LANES], preferred_element_type=jnp.float32)
    extra[...] = late.astype(jnp.bfloat16).reshape(N_DP, EXTRA, LANES)

    def back_copies(o):
        there = (dp + o) % N_DP
        return exchange(o, 2 * N_DP, canvas.at[there], extra.at[there], returned.at[dp], returned_extra.at[dp], there)

    def send_back(o, _):
        for copy in back_copies(o):
            copy.start()
        return 0

    lax.fori_loop(1, N_DP, send_back, 0)
    returned[dp] = canvas[dp]
    returned_extra[dp] = extra[dp]

    def wait_back(o, _):
        for copy in back_copies(o):
            copy.wait()
        return 0

    lax.fori_loop(1, N_DP, wait_back, 0)

    def unpack(d, _):
        extra_tmp[...] = returned_extra[d].astype(jnp.float32)
        for j in range(4):
            back[pl.ds(d * 4 + j, MAIN, stride=CHUNKS)] = pltpu.roll(
                returned[d, :, pl.ds(j * LANES, LANES)].astype(jnp.float32), (LANES - lead_lanes) % LANES, 1)
            back[pl.ds(d * 4 + j + MAIN * CHUNKS, 2, stride=CHUNKS)] = pltpu.roll(
                extra_tmp[...], (LANES - lead_lanes) % LANES, 1)[2 * j : 2 * j + 2]
        return 0

    lax.fori_loop(0, N_DP, unpack, 0)
    back[pl.ds(34 * CHUNKS, 8)] = jnp.zeros((8, LANES), jnp.float32)

    def finish(i, _):
        here = back[pl.ds(i * STEP + lead_rows, STEP)]
        after = back[pl.ds(i * STEP + lead_rows + 1, STEP)]
        lane = lax.broadcasted_iota(jnp.int32, (STEP, LANES), 1)
        value = jnp.where(lane + lead_lanes < LANES, here, after)
        out_ref[pl.ds(pl.multiple_of(i * STEP, 8), STEP)] = jnp.where(slots(i) < my_length, value, 0.0)
        return 0

    lax.fori_loop(0, FLAT_ROWS // STEP, finish, 0)
    for copy in started:
        copy.wait_send()


def newton_schulz(lengths, flat):
    bf, f32 = jnp.bfloat16, jnp.float32
    vmem = pltpu.VMEM
    return pl.pallas_call(
        core_kernel,
        out_shape=jax.ShapeDtypeStruct((FLAT_ROWS, LANES), f32),
        in_specs=[pl.BlockSpec(memory_space=pltpu.SMEM), pl.BlockSpec(memory_space=pltpu.VMEM)],
        out_specs=pl.BlockSpec(memory_space=pltpu.VMEM),
        scratch_shapes=[
            vmem((LEAD + FLAT_ROWS + 88, LANES), f32),
            vmem((N_DP, MAIN, SLAB), bf),
            vmem((EXTRA, LANES), f32),
            vmem((N_DP, EXTRA, LANES), bf),
            vmem((N_DP, MAIN, SLAB), bf),
            vmem((N_DP, EXTRA, LANES), bf),
            vmem((34 * CHUNKS + 8, LANES), f32),
            vmem((GROUP_ROWS, SLAB), bf),
            vmem((RING, PANEL, SLAB), bf),
            vmem((RING, GROUP_ROWS, SLAB), bf),
            vmem((CORE_ROWS, BLOCK), f32),
            vmem((CORE_ROWS, BLOCK), bf),
            vmem((CORE_ROWS, BLOCK), bf),
            vmem((2, PANEL, BLOCK), bf),
            vmem((7, SHARD, BLOCK), bf),
            vmem((7, SHARD, BLOCK), bf),
            vmem((RING, PANEL, BLOCK), bf),
            vmem((2, RING, GROUP_ROWS, HALF_SLAB), bf),
            vmem((2, HALF_ROWS, HALF_SLAB), bf),
            vmem((2, HALF_ROWS, HALF_SLAB), bf),
            vmem((2, GROUP_ROWS, HALF_SLAB), bf),
            vmem((2, GROUP_ROWS, HALF_SLAB), bf),
            vmem((GROUP_ROWS, SLAB), f32),
            vmem((RING, GROUP_ROWS, HALF_SLAB), bf),
            vmem((RING, PANEL, HALF_SLAB), bf),
            vmem((2, RING, GROUP_ROWS, HALF_SLAB), bf),
            vmem((BLOCK, HALF_SLAB), f32),
            vmem((GROUP_ROWS, SLAB), f32),
            vmem((GROUP_ROWS, SLAB), bf),
            vmem((N_DP, MAIN, SLAB), bf),
            vmem((N_DP, EXTRA, LANES), bf),
            pltpu.SemaphoreType.DMA((N_MESSAGES,)),
            pltpu.SemaphoreType.DMA((N_MESSAGES,)),
        ],
        compiler_params=pltpu.CompilerParams(
            collective_id=0, has_side_effects=True, vmem_limit_bytes=56 * 1024 * 1024
        ),
    )(lengths, flat)


def local(flat_iterate, lengths):
    flat = flat_iterate.astype(jnp.float32).reshape(FLAT_ROWS, LANES)
    new_flat = newton_schulz(lengths, flat).reshape(1, FLAT_ROWS * LANES)
    return lax.optimization_barrier(new_flat).astype(jnp.bfloat16)


def solution(mesh):
    return jax.shard_map(
        local,
        mesh=mesh,
        in_specs=(P(("dp", "row", "col"), None), P()),
        out_specs=P(("dp", "row", "col"), None),
        check_vma=False,
    )
```

```python
import math

import jax
import jax.numpy as jnp
from jax import lax
from jax.experimental import pallas as pl
from jax.experimental.pallas import tpu as pltpu
from jax.sharding import PartitionSpec as P

COLS = 8192
ROWS = 5632


LINEAR_COEF = 3.4445
CUBIC_COEF = -4.775
QUINTIC_COEF = 2.0315

N_DP = 16
N_Z = 8
RING = 4
GROUP_ROWS = 352
HALF_ROWS = 176
SLAB = 512
BLOCK = 1408
CORE_ROWS = 704
SHARD = 48
PANEL = N_Z * SHARD
HALF_SLAB = SLAB // 2
LANES = 128
CHUNKS = COLS // LANES
FLAT_ROWS = 2112
MAIN = 32
EXTRA = 16
LEAD = 72
N_MESSAGES = 256
MESH = pl.DeviceIdType.MESH
SCALE = 0.2 * math.sqrt(max(ROWS, COLS))


def core_kernel(
    lengths_ref, flat_ref, out_ref, staged, canvas, outgoing, extra_tmp, extra, arrived, arrived_extra, back, x_ref, xr, xs, own_f32, sib_f32, to_sib, from_sib, gh, ring_f, ring_b, g_full,
    part, got_a, got_b, got_c, got_d, y_f32, ya, yb, part2, z_b, z_f32, update, returned, returned_extra, send_sem, recv_sem,
):
    dp = lax.axis_index("dp")
    y = lax.axis_index("row")
    x = lax.axis_index("col")
    z, c = dp // 2, dp % 2
    sib_dp = z * 2 + 1 - c
    up_dp = ((z + 1) % N_Z) * 2 + c
    down_dp = ((z + 7) % N_Z) * 2 + c
    dev_sib = (sib_dp, y, x)
    dev_up = (up_dp, y, x)
    dev_down = (down_dp, y, x)
    near = {
        "col": ((dp, y, (x + 1) % RING), (dp, y, (x + 3) % RING)),
        "row": ((dp, (y + 1) % RING, x), (dp, (y + 3) % RING, x)),
    }
    place = {"col": x, "row": y}

    barrier = pltpu.get_barrier_semaphore()
    for peer in near["col"] + near["row"]:
        pl.semaphore_signal(barrier, inc=1, device_id=peer, device_id_type=MESH)

    def greet(o, _):
        pl.semaphore_signal(barrier, inc=1, device_id=((dp + o) % N_DP, y, x), device_id_type=MESH)
        return 0

    lax.fori_loop(1, N_DP, greet, 0)

    counter = [5 * N_DP]
    started = []

    def message(src, dst, device, slot=None):
        if slot is None:
            slot = counter[0]
            counter[0] += 1
        return pltpu.make_async_remote_copy(
            src_ref=src, dst_ref=dst, send_sem=send_sem.at[slot], recv_sem=recv_sem.at[slot],
            device_id=device, device_id_type=MESH,
        )

    def send(src, dst, device):
        copy = message(src, dst, device)
        copy.start()
        started.append(copy)
        return copy

    top, bottom = pl.ds(0, HALF_ROWS), pl.ds(HALF_ROWS, HALF_ROWS)

    def gather_start(axis, buf, cols):
        p = place[axis]
        right, left = near[axis]
        a = [send(buf.at[p, h, cols], buf.at[p, h, cols], right) for h in (top, bottom)]
        b = [send(buf.at[p, h, cols], buf.at[p, h, cols], left) for h in (bottom, top)]
        return a, b

    def gather_pass(axis, buf, state, cols):
        p = place[axis]
        right, left = near[axis]
        a, b = state
        before, after = (p + 3) % RING, (p + 1) % RING
        a[0].wait_recv()
        f = send(buf.at[before, top, cols], buf.at[before, top, cols], right)
        b[0].wait_recv()
        g = send(buf.at[after, bottom, cols], buf.at[after, bottom, cols], left)
        return a[1], b[1], f, g

    def gather_end(tail):
        for copy in tail:
            copy.wait_recv()

    group = y * RING + x
    my_start = jnp.int32(0)
    begin = jnp.int32(0)
    first_rows = []
    for d in range(N_DP):
        first_rows.append(begin // COLS)
        my_start = jnp.where(dp == d, begin, my_start)
        begin = begin + lengths_ref[group, d]
    my_length = lengths_ref[group, dp]
    lead = my_start % COLS
    lead_rows, lead_lanes = lead // LANES, lead % LANES
    staged[pl.ds(0, LEAD)] = jnp.zeros((LEAD, LANES), jnp.float32)
    tail_rows = staged.shape[0] - LEAD - FLAT_ROWS
    staged[pl.ds(LEAD + FLAT_ROWS, tail_rows)] = jnp.zeros((tail_rows, LANES), jnp.float32)
    STEP = 176

    def slots(i):
        return (
            i * (STEP * LANES)
            + lax.broadcasted_iota(jnp.int32, (STEP, LANES), 0) * LANES
            + lax.broadcasted_iota(jnp.int32, (STEP, LANES), 1)
        )

    def stage(i, _):
        value = flat_ref[:, pl.ds(pl.multiple_of(i * STEP * LANES, LANES), STEP * LANES)].astype(jnp.float32).reshape(STEP, LANES)
        value = jnp.where(slots(i) < my_length, value, 0.0)
        staged[pl.ds(pl.multiple_of(i * STEP + LEAD, 8), STEP)] = pltpu.roll(value, lead_lanes, 1)
        return 0

    lax.fori_loop(0, FLAT_ROWS // STEP, stage, 0)
    extra_tmp[...] = jnp.zeros_like(extra_tmp)

    def out_copies(o):
        there = (dp + o) % N_DP
        device = (there, y, x)
        return (
            message(extra.at[there], arrived_extra.at[dp], device, slot=o),
            message(canvas.at[0, there], arrived.at[0, dp], device, slot=N_DP + o),
            message(canvas.at[1, there], arrived.at[1, dp], device, slot=2 * N_DP + o),
        )

    def place_part(o, _):
        there = (dp + o) % N_DP
        lane = lax.broadcasted_iota(jnp.int32, (MAIN, LANES), 1)
        lane2 = lax.broadcasted_iota(jnp.int32, (2, LANES), 1)
        start = LEAD - lead_rows + there * 4
        before = staged[pl.ds(start - 1, MAIN, stride=CHUNKS)]
        before2 = staged[pl.ds(start - 1 + MAIN * CHUNKS, 2, stride=CHUNKS)]
        for j in range(4):
            here = staged[pl.ds(start + j, MAIN, stride=CHUNKS)]
            here2 = staged[pl.ds(start + j + MAIN * CHUNKS, 2, stride=CHUNKS)]
            canvas[j // 2, there, :, pl.ds(j % 2 * LANES, LANES)] = jnp.where(lane >= lead_lanes, here, before).astype(jnp.bfloat16)
            extra_tmp[pl.ds(j * 2, 2)] = jnp.where(lane2 >= lead_lanes, here2, before2)
            before, before2 = here, here2
        extra[there] = extra_tmp[...].astype(jnp.bfloat16)
        return 0

    lax.fori_loop(1, N_DP + 1, place_part, 0)
    pl.semaphore_wait(barrier, 4 + N_DP - 1)

    def send_out(o, _):
        for copy in out_copies(o)[:2]:
            copy.start()
        return 0

    def send_out_more(o, _):
        out_copies(o)[2].start()
        return 0

    lax.fori_loop(1, N_DP, send_out, 0)
    lax.fori_loop(1, N_DP, send_out_more, 0)
    for h in range(2):
        arrived[h, dp] = canvas[h, dp]
    arrived_extra[dp] = extra[dp]

    def targets(length, width, offset, shape, dim):
        k = lax.broadcasted_iota(jnp.int32, shape, dim)
        found = jnp.full(shape, -1, jnp.int32)
        for d in range(N_DP):
            inside = k // width == d
            found = jnp.where(inside, first_rows[d] + k % width + offset, found)
        return k, found

    k, row_of = targets(N_DP * MAIN, MAIN, 0, (1, N_DP * MAIN), 1)
    pick = (lax.broadcasted_iota(jnp.int32, (GROUP_ROWS, N_DP * MAIN), 0) == row_of).astype(jnp.float32).astype(jnp.bfloat16)
    ke, row_e = targets(N_DP * EXTRA, EXTRA, MAIN, (1, N_DP * EXTRA), 1)
    ke = ke % EXTRA

    def land(h):
        def wait_out(o, _):
            for copy in out_copies(o)[2 * h : 2 + h]:
                copy.wait()
            return 0

        lax.fori_loop(1, N_DP, wait_out, 0)
        value = jnp.dot(pick, arrived[h].reshape(N_DP * MAIN, HALF_SLAB), preferred_element_type=jnp.float32)
        late = arrived_extra[...].reshape(N_DP * EXTRA, LANES)
        parts = []
        for j in (2 * h, 2 * h + 1):
            row_j = jnp.where(ke // 2 == j, row_e - 2 * j, -1)
            pick_j = (lax.broadcasted_iota(jnp.int32, (GROUP_ROWS, N_DP * EXTRA), 0) == row_j).astype(jnp.float32).astype(jnp.bfloat16)
            parts.append(jnp.dot(pick_j, late, preferred_element_type=jnp.float32))
        value = (value + jnp.concatenate(parts, axis=1)).astype(jnp.bfloat16)
        cols = halves[h]
        x_ref[:, cols] = value
        xr[x, group_rows, cols] = value
        xs[y, :, cols] = value

    halves = (pl.ds(0, HALF_SLAB), pl.ds(HALF_SLAB, HALF_SLAB))
    group_rows = pl.ds(0, GROUP_ROWS)
    pad = pl.ds(GROUP_ROWS, PANEL - GROUP_ROWS)
    for q in range(RING):
        xr[q, pad] = jnp.zeros((PANEL - GROUP_ROWS, SLAB), jnp.bfloat16)
        yb[q, pad] = jnp.zeros((PANEL - GROUP_ROWS, HALF_SLAB), jnp.bfloat16)
    for p in range(2):
        to_sib[p, pad] = jnp.zeros((PANEL - GROUP_ROWS, BLOCK), jnp.bfloat16)
        own_f32[p, pad] = jnp.zeros((PANEL - GROUP_ROWS, BLOCK), jnp.float32)

    def gram(core, h, store):
        def tile(i, _):
            rows = pl.ds(pl.multiple_of((i % 2) * HALF_ROWS, 16), HALF_ROWS)
            value = lax.dot_general(
                xr[2 * core + i // 2, rows, halves[h]], xs[:, :, halves[h]].reshape(BLOCK, HALF_SLAB),
                (((1,), (1,)), ((), ())), preferred_element_type=jnp.float32,
            )
            store(i // 2, rows, value)
            return 0

        lax.fori_loop(0, 4, tile, 0)

    def keep_own(p, rows, value):
        own_f32[p, rows] = value

    def keep_sib(p, rows, value):
        sib_f32[p, rows] = value

    def add_own(p, rows, value):
        own_f32[p, rows] += value

    def add_sib(p, rows, value):
        to_sib[p, rows] = (sib_f32[p, rows] + value).astype(jnp.bfloat16)

    land(0)
    s1 = gather_start("col", xr, halves[0])
    s2 = gather_start("row", xs, halves[0])
    t1 = gather_pass("col", xr, s1, halves[0])
    t2 = gather_pass("row", xs, s2, halves[0])
    land(1)
    s1 = gather_start("col", xr, halves[1])
    s2 = gather_start("row", xs, halves[1])
    gather_end(t1)
    gather_end(t2)
    gram(1 - c, 0, keep_sib)
    gram(c, 0, keep_own)
    t1 = gather_pass("col", xr, s1, halves[1])
    t2 = gather_pass("row", xs, s2, halves[1])
    gather_end(t1)
    gather_end(t2)
    gram(1 - c, 1, add_sib)

    def shard_rows(s):
        return pl.ds(pl.multiple_of(((s + N_Z) % N_Z) * SHARD, 16), SHARD)

    f32 = jnp.float32
    plan = []
    for k in range(8):
        distance = 4 - (k + 1) // 2
        plan.append((True, k % 2, distance))
        plan.append((False, 1 - k % 2, distance))
    sib_in = []
    for upward, panel, distance in plan:
        rows = shard_rows(z + distance if upward else z - distance)
        sib_in.append(send(to_sib.at[panel, rows], from_sib.at[panel, rows], dev_sib))
    gram(c, 1, add_own)

    up_in, down_in = [], []
    for (upward, panel, distance), arrival in zip(plan, sib_in):
        rows = shard_rows(z + distance if upward else z - distance)
        arrival.wait_recv()
        term = own_f32[panel, rows] + from_sib[panel, rows].astype(f32)
        if distance == 0:
            up, down = (6, 5) if panel == 0 else (5, 6)
            up_in[up].wait_recv()
            down_in[down].wait_recv()
            term = term + ring_f[up].astype(f32) + ring_b[down].astype(f32)
            g_full[2 * c + panel, rows] = term.astype(jnp.bfloat16)
            continue
        arrivals, ring, device = (up_in, ring_f, dev_up) if upward else (down_in, ring_b, dev_down)
        k = len(arrivals)
        if k < 2:
            src = gh.at[2 * k + int(upward)]
        else:
            arrivals[k - 2].wait_recv()
            src = ring.at[k - 2]
            term = term + ring[k - 2].astype(f32)
        src[...] = term.astype(jnp.bfloat16)
        arrivals.append(send(src, ring.at[k], device))
    mine = shard_rows(z)

    pending = []

    def relay(panel, rows, device):
        ref = g_full.at[2 * c + panel, rows]
        return send(ref, ref, device)

    up_in, down_in = [], []
    for k in range(9):
        back_by = k // 2
        up_part, down_part = (k % 2, shard_rows(z - back_by)), (1 - k % 2, shard_rows(z + back_by))
        if k >= 2:
            up_in[k - 2].wait_recv()
        if k < 7:
            up_in.append(relay(*up_part, dev_up))
        if k >= 2:
            down_in[k - 2].wait_recv()
        if k < 7:
            down_in.append(relay(*down_part, dev_down))
        pending.append(relay(*up_part, dev_sib))
        if k >= 2:
            pending.append(relay(*down_part, dev_sib))
    for copy in pending:
        copy.wait_recv()

    def reduce_start(axis, buf, a_ref, b_ref):
        p = place[axis]
        right, left = near[axis]
        far = (p + 2) % RING
        return (send(buf.at[far, top], a_ref, right), send(buf.at[far, bottom], b_ref, left))

    def reduce_near(axis, buf, c_ref, d_ref):
        p = place[axis]
        right, left = near[axis]
        after, before = (p + 1) % RING, (p + 3) % RING
        return (
            send(buf.at[after, bottom], c_ref.at[bottom], right),
            send(buf.at[before, top], d_ref.at[top], left),
        )

    def reduce_pass(axis, buf, a_ref, b_ref, c_ref, d_ref, state):
        p = place[axis]
        right, left = near[axis]
        after, before = (p + 1) % RING, (p + 3) % RING
        state[0].wait_recv()
        buf[after, top] = (buf[after, top].astype(f32) + a_ref[...].astype(f32)).astype(jnp.bfloat16)
        c2 = send(buf.at[after, top], c_ref.at[top], right)
        state[1].wait_recv()
        buf[before, bottom] = (buf[before, bottom].astype(f32) + b_ref[...].astype(f32)).astype(jnp.bfloat16)
        d2 = send(buf.at[before, bottom], d_ref.at[bottom], left)
        return (c2, d2)

    first, second = pl.ds(0, HALF_SLAB), pl.ds(HALF_SLAB, HALF_SLAB)

    def apply_gram(right_a, right_b, buf, total):
        def make(q):
            return jnp.dot(g_full[q, pl.ds(0, GROUP_ROWS)], right_a(), preferred_element_type=f32)

        far, after, before = (x + 2) % RING, (x + 1) % RING, (x + 3) % RING
        buf_a, buf_b = buf.at[0], buf.at[1]
        slots = [[r.at[i] for r in (got_a, got_b, got_c, got_d)] for i in range(2)]
        buf_a[far] = make(far).astype(jnp.bfloat16)
        sa = reduce_start("col", buf_a, *slots[0][:2])

        def columns(j, _):
            cols = pl.ds(pl.multiple_of(j * LANES, LANES), LANES)
            z_b[cols] = lax.dot_general(
                g_full[:, :, cols].reshape(RING * PANEL, LANES), right_b(), (((0,), (0,)), ((), ())),
                preferred_element_type=f32,
            )
            return 0

        lax.fori_loop(0, BLOCK // LANES, columns, 0)
        buf_b[...] = z_b[...].astype(jnp.bfloat16).reshape(RING, GROUP_ROWS, HALF_SLAB)
        sb = reduce_start("row", buf_b, *slots[1][:2])
        nb = reduce_near("row", buf_b, *slots[1][2:])
        buf_a[after] = make(after).astype(jnp.bfloat16)
        buf_a[before] = make(before).astype(jnp.bfloat16)
        na = reduce_near("col", buf_a, *slots[0][2:])
        pa = reduce_pass("col", buf_a, *slots[0], sa)
        pb = reduce_pass("row", buf_b, *slots[1], sb)
        total[:, first] = make(x)
        total[:, second] = z_b[pl.ds(pl.multiple_of(y * GROUP_ROWS, 8), GROUP_ROWS)]
        for i, (cols, tail) in enumerate(((first, na + pa), (second, nb + pb))):
            gather_end(tail)
            total[:, cols] = total[:, cols] + got_c[i].astype(f32) + got_d[i].astype(f32)

    apply_gram(
        lambda: xs[:, :, :HALF_SLAB].reshape(BLOCK, HALF_SLAB),
        lambda: xr[:, :, HALF_SLAB:].reshape(RING * PANEL, HALF_SLAB),
        part, y_f32,
    )
    ya[y] = y_f32[:, :HALF_SLAB].astype(jnp.bfloat16)
    yb[x, pl.ds(0, GROUP_ROWS)] = y_f32[:, HALF_SLAB:].astype(jnp.bfloat16)
    s1 = gather_start("row", ya, first)
    s2 = gather_start("col", yb, first)
    t1 = gather_pass("row", ya, s1, first)
    t2 = gather_pass("col", yb, s2, first)
    gather_end(t1)
    gather_end(t2)

    apply_gram(
        lambda: ya[...].reshape(BLOCK, HALF_SLAB),
        lambda: yb[...].reshape(RING * PANEL, HALF_SLAB),
        part2, z_f32,
    )
    update[...] = (
        SCALE * (LINEAR_COEF * x_ref[...].astype(f32) + (CUBIC_COEF * y_f32[...] + QUINTIC_COEF * z_f32[...]))
    ).astype(jnp.bfloat16)

    _, row_of = targets(N_DP * MAIN, MAIN, 0, (N_DP * MAIN, 1), 0)
    pick = (lax.broadcasted_iota(jnp.int32, (N_DP * MAIN, GROUP_ROWS), 1) == row_of).astype(jnp.float32).astype(jnp.bfloat16)
    outgoing[...] = jnp.dot(pick, update[...], preferred_element_type=jnp.float32).astype(jnp.bfloat16).reshape(N_DP, MAIN, SLAB)
    ke, row_e = targets(N_DP * EXTRA, EXTRA, MAIN, (N_DP * EXTRA, 1), 0)
    ke = ke % EXTRA
    late = jnp.zeros((N_DP * EXTRA, LANES), jnp.float32)
    for j in range(4):
        row_j = jnp.where(ke // 2 == j, row_e - 2 * j, -1)
        pick_j = (lax.broadcasted_iota(jnp.int32, (N_DP * EXTRA, GROUP_ROWS), 1) == row_j).astype(jnp.float32).astype(jnp.bfloat16)
        late += jnp.dot(pick_j, update[:, j * LANES : (j + 1) * LANES], preferred_element_type=jnp.float32)
    extra[...] = late.astype(jnp.bfloat16).reshape(N_DP, EXTRA, LANES)

    def back_copies(o):
        there = (dp + o) % N_DP
        device = (there, y, x)
        return (
            message(outgoing.at[there], returned.at[dp], device, slot=3 * N_DP + o),
            message(extra.at[there], returned_extra.at[dp], device, slot=4 * N_DP + o),
        )

    def send_back(o, _):
        for copy in back_copies(o):
            copy.start()
        return 0

    lax.fori_loop(1, N_DP, send_back, 0)
    returned[dp] = outgoing[dp]
    returned_extra[dp] = extra[dp]

    def wait_back(o, _):
        for copy in back_copies(o):
            copy.wait()
        return 0

    lax.fori_loop(1, N_DP, wait_back, 0)

    def unpack(d, _):
        extra_tmp[...] = returned_extra[d].astype(jnp.float32)
        for j in range(4):
            back[pl.ds(d * 4 + j, MAIN, stride=CHUNKS)] = pltpu.roll(
                returned[d, :, pl.ds(j * LANES, LANES)].astype(jnp.float32), (LANES - lead_lanes) % LANES, 1)
            back[pl.ds(d * 4 + j + MAIN * CHUNKS, 2, stride=CHUNKS)] = pltpu.roll(
                extra_tmp[...], (LANES - lead_lanes) % LANES, 1)[2 * j : 2 * j + 2]
        return 0

    lax.fori_loop(0, N_DP, unpack, 0)
    back[pl.ds(34 * CHUNKS, 8)] = jnp.zeros((8, LANES), jnp.float32)

    def finish(i, _):
        here = back[pl.ds(i * STEP + lead_rows, STEP)]
        after = back[pl.ds(i * STEP + lead_rows + 1, STEP)]
        lane = lax.broadcasted_iota(jnp.int32, (STEP, LANES), 1)
        value = jnp.where(lane + lead_lanes < LANES, here, after)
        value = jnp.where(slots(i) < my_length, value, 0.0).reshape(1, STEP * LANES)
        out_ref[:, pl.ds(pl.multiple_of(i * STEP * LANES, LANES), STEP * LANES)] = value.astype(jnp.bfloat16)
        return 0

    lax.fori_loop(0, FLAT_ROWS // STEP, finish, 0)
    for copy in started:
        copy.wait_send()


def newton_schulz(lengths, flat):
    bf, f32 = jnp.bfloat16, jnp.float32
    vmem = pltpu.VMEM
    return pl.pallas_call(
        core_kernel,
        out_shape=jax.ShapeDtypeStruct((1, FLAT_ROWS * LANES), bf),
        in_specs=[pl.BlockSpec(memory_space=pltpu.SMEM), pl.BlockSpec(memory_space=pltpu.VMEM)],
        out_specs=pl.BlockSpec(memory_space=pltpu.VMEM),
        scratch_shapes=[
            vmem((LEAD + FLAT_ROWS + 88, LANES), f32),
            vmem((2, N_DP, MAIN, HALF_SLAB), bf),
            vmem((N_DP, MAIN, SLAB), bf),
            vmem((EXTRA, LANES), f32),
            vmem((N_DP, EXTRA, LANES), bf),
            vmem((2, N_DP, MAIN, HALF_SLAB), bf),
            vmem((N_DP, EXTRA, LANES), bf),
            vmem((34 * CHUNKS + 8, LANES), f32),
            vmem((GROUP_ROWS, SLAB), bf),
            vmem((RING, PANEL, SLAB), bf),
            vmem((RING, GROUP_ROWS, SLAB), bf),
            vmem((2, PANEL, BLOCK), f32),
            vmem((2, PANEL, BLOCK), f32),
            vmem((2, PANEL, BLOCK), bf),
            vmem((2, PANEL, BLOCK), bf),
            vmem((4, SHARD, BLOCK), bf),
            vmem((7, SHARD, BLOCK), bf),
            vmem((7, SHARD, BLOCK), bf),
            vmem((RING, PANEL, BLOCK), bf),
            vmem((2, RING, GROUP_ROWS, HALF_SLAB), bf),
            vmem((2, HALF_ROWS, HALF_SLAB), bf),
            vmem((2, HALF_ROWS, HALF_SLAB), bf),
            vmem((2, GROUP_ROWS, HALF_SLAB), bf),
            vmem((2, GROUP_ROWS, HALF_SLAB), bf),
            vmem((GROUP_ROWS, SLAB), f32),
            vmem((RING, GROUP_ROWS, HALF_SLAB), bf),
            vmem((RING, PANEL, HALF_SLAB), bf),
            vmem((2, RING, GROUP_ROWS, HALF_SLAB), bf),
            vmem((BLOCK, HALF_SLAB), f32),
            vmem((GROUP_ROWS, SLAB), f32),
            vmem((GROUP_ROWS, SLAB), bf),
            vmem((N_DP, MAIN, SLAB), bf),
            vmem((N_DP, EXTRA, LANES), bf),
            pltpu.SemaphoreType.DMA((N_MESSAGES,)),
            pltpu.SemaphoreType.DMA((N_MESSAGES,)),
        ],
        compiler_params=pltpu.CompilerParams(
            collective_id=0, has_side_effects=True, vmem_limit_bytes=56 * 1024 * 1024
        ),
    )(lengths, flat)


def local(flat_iterate, lengths):
    return newton_schulz(lengths, flat_iterate)


def solution(mesh):
    return jax.shard_map(
        local,
        mesh=mesh,
        in_specs=(P(("dp", "row", "col"), None), P()),
        out_specs=P(("dp", "row", "col"), None),
        check_vma=False,
    )
```

```python
import math

import jax
import jax.numpy as jnp
from jax import lax
from jax.experimental import pallas as pl
from jax.experimental.pallas import tpu as pltpu
from jax.sharding import PartitionSpec as P

COLS = 8192
ROWS = 5632


LINEAR_COEF = 3.4445
CUBIC_COEF = -4.775
QUINTIC_COEF = 2.0315

N_DP = 16
N_Z = 8
RING = 4
GROUP_ROWS = 352
HALF_ROWS = 176
SLAB = 512
BLOCK = 1408
CORE_ROWS = 704
SHARD = 48
PANEL = N_Z * SHARD
HALF_SLAB = SLAB // 2
LANES = 128
CHUNKS = COLS // LANES
FLAT_ROWS = 2112
MAIN = 32
EXTRA = 16
LEAD = 72
STEP = 176
N_MESSAGES = 256
MESH = pl.DeviceIdType.MESH
SCALE = 0.2 * math.sqrt(max(ROWS, COLS))


def slots(i):
    return (
        i * (STEP * LANES)
        + lax.broadcasted_iota(jnp.int32, (STEP, LANES), 0) * LANES
        + lax.broadcasted_iota(jnp.int32, (STEP, LANES), 1)
    )


def core_kernel(
    lengths_ref, flat_ref, returned, returned_extra, staged, canvas, outgoing, extra_tmp, extra, arrived, arrived_extra, x_ref, xr, xs, own_f32, sib_f32, to_sib, from_sib, gh, ring_f, ring_b, g_full,
    part, got_a, got_b, got_c, got_d, y_f32, ya, yb, part2, z_b, z_f32, update, send_sem, recv_sem,
):
    dp = lax.axis_index("dp")
    y = lax.axis_index("row")
    x = lax.axis_index("col")
    z, c = dp // 2, dp % 2
    sib_dp = z * 2 + 1 - c
    up_dp = ((z + 1) % N_Z) * 2 + c
    down_dp = ((z + 7) % N_Z) * 2 + c
    dev_sib = (sib_dp, y, x)
    dev_up = (up_dp, y, x)
    dev_down = (down_dp, y, x)
    near = {
        "col": ((dp, y, (x + 1) % RING), (dp, y, (x + 3) % RING)),
        "row": ((dp, (y + 1) % RING, x), (dp, (y + 3) % RING, x)),
    }
    place = {"col": x, "row": y}

    barrier = pltpu.get_barrier_semaphore()
    for peer in near["col"] + near["row"]:
        pl.semaphore_signal(barrier, inc=1, device_id=peer, device_id_type=MESH)

    def greet(o, _):
        pl.semaphore_signal(barrier, inc=1, device_id=((dp + o) % N_DP, y, x), device_id_type=MESH)
        return 0

    lax.fori_loop(1, N_DP, greet, 0)

    counter = [6 * N_DP]
    started = []

    def message(src, dst, device, slot=None):
        if slot is None:
            slot = counter[0]
            counter[0] += 1
        return pltpu.make_async_remote_copy(
            src_ref=src, dst_ref=dst, send_sem=send_sem.at[slot], recv_sem=recv_sem.at[slot],
            device_id=device, device_id_type=MESH,
        )

    def send(src, dst, device):
        copy = message(src, dst, device)
        copy.start()
        started.append(copy)
        return copy

    top, bottom = pl.ds(0, HALF_ROWS), pl.ds(HALF_ROWS, HALF_ROWS)

    def gather_start(axis, buf):
        p = place[axis]
        right, left = near[axis]
        a = [send(buf.at[p, h], buf.at[p, h], right) for h in (top, bottom)]
        b = [send(buf.at[p, h], buf.at[p, h], left) for h in (bottom, top)]
        return a, b

    def gather_pass(axis, buf, state):
        p = place[axis]
        right, left = near[axis]
        a, b = state
        before, after = (p + 3) % RING, (p + 1) % RING
        a[0].wait_recv()
        f = send(buf.at[before, top], buf.at[before, top], right)
        b[0].wait_recv()
        g = send(buf.at[after, bottom], buf.at[after, bottom], left)
        return a[1], b[1], f, g

    def gather_end(tail):
        for copy in tail:
            copy.wait_recv()

    group = y * RING + x
    my_start = jnp.int32(0)
    begin = jnp.int32(0)
    first_rows = []
    for d in range(N_DP):
        first_rows.append(begin // COLS)
        my_start = jnp.where(dp == d, begin, my_start)
        begin = begin + lengths_ref[group, d]
    my_length = lengths_ref[group, dp]
    lead = my_start % COLS
    lead_rows, lead_lanes = lead // LANES, lead % LANES
    staged[pl.ds(0, LEAD)] = jnp.zeros((LEAD, LANES), jnp.float32)
    tail_rows = staged.shape[0] - LEAD - FLAT_ROWS
    staged[pl.ds(LEAD + FLAT_ROWS, tail_rows)] = jnp.zeros((tail_rows, LANES), jnp.float32)

    def stage(i, _):
        value = flat_ref[:, pl.ds(pl.multiple_of(i * STEP * LANES, LANES), STEP * LANES)].astype(jnp.float32).reshape(STEP, LANES)
        value = jnp.where(slots(i) < my_length, value, 0.0)
        staged[pl.ds(pl.multiple_of(i * STEP + LEAD, 8), STEP)] = pltpu.roll(value, lead_lanes, 1)
        return 0

    lax.fori_loop(0, FLAT_ROWS // STEP, stage, 0)
    extra_tmp[...] = jnp.zeros_like(extra_tmp)

    def out_copies(o):
        there = (dp + o) % N_DP
        device = (there, y, x)
        return (
            message(extra.at[there], arrived_extra.at[dp], device, slot=o),
            message(canvas.at[0, there], arrived.at[0, dp], device, slot=N_DP + o),
            message(canvas.at[1, there], arrived.at[1, dp], device, slot=2 * N_DP + o),
        )

    def place_part(o, _):
        there = (dp + o) % N_DP
        lane = lax.broadcasted_iota(jnp.int32, (MAIN, LANES), 1)
        lane2 = lax.broadcasted_iota(jnp.int32, (2, LANES), 1)
        start = LEAD - lead_rows + there * 4
        before = staged[pl.ds(start - 1, MAIN, stride=CHUNKS)]
        before2 = staged[pl.ds(start - 1 + MAIN * CHUNKS, 2, stride=CHUNKS)]
        for j in range(4):
            here = staged[pl.ds(start + j, MAIN, stride=CHUNKS)]
            here2 = staged[pl.ds(start + j + MAIN * CHUNKS, 2, stride=CHUNKS)]
            canvas[j // 2, there, :, pl.ds(j % 2 * LANES, LANES)] = jnp.where(lane >= lead_lanes, here, before).astype(jnp.bfloat16)
            extra_tmp[pl.ds(j * 2, 2)] = jnp.where(lane2 >= lead_lanes, here2, before2)
            before, before2 = here, here2
        extra[there] = extra_tmp[...].astype(jnp.bfloat16)
        return 0

    lax.fori_loop(1, N_DP + 1, place_part, 0)
    pl.semaphore_wait(barrier, 4 + N_DP - 1)

    def send_out(o, _):
        for copy in out_copies(o)[:2]:
            copy.start()
        return 0

    def send_out_more(o, _):
        out_copies(o)[2].start()
        return 0

    lax.fori_loop(1, N_DP, send_out, 0)
    lax.fori_loop(1, N_DP, send_out_more, 0)
    for h in range(2):
        arrived[h, dp] = canvas[h, dp]
    arrived_extra[dp] = extra[dp]

    def targets(length, width, offset, shape, dim):
        k = lax.broadcasted_iota(jnp.int32, shape, dim)
        found = jnp.full(shape, -1, jnp.int32)
        for d in range(N_DP):
            inside = k // width == d
            found = jnp.where(inside, first_rows[d] + k % width + offset, found)
        return k, found

    k, row_of = targets(N_DP * MAIN, MAIN, 0, (1, N_DP * MAIN), 1)
    pick = (lax.broadcasted_iota(jnp.int32, (GROUP_ROWS, N_DP * MAIN), 0) == row_of).astype(jnp.float32).astype(jnp.bfloat16)
    ke, row_e = targets(N_DP * EXTRA, EXTRA, MAIN, (1, N_DP * EXTRA), 1)
    ke = ke % EXTRA

    def land(h):
        def wait_out(o, _):
            for copy in out_copies(o)[2 * h : 2 + h]:
                copy.wait()
            return 0

        lax.fori_loop(1, N_DP, wait_out, 0)
        value = jnp.dot(pick, arrived[h].reshape(N_DP * MAIN, HALF_SLAB), preferred_element_type=jnp.float32)
        late = arrived_extra[...].reshape(N_DP * EXTRA, LANES)
        parts = []
        for j in (2 * h, 2 * h + 1):
            row_j = jnp.where(ke // 2 == j, row_e - 2 * j, -1)
            pick_j = (lax.broadcasted_iota(jnp.int32, (GROUP_ROWS, N_DP * EXTRA), 0) == row_j).astype(jnp.float32).astype(jnp.bfloat16)
            parts.append(jnp.dot(pick_j, late, preferred_element_type=jnp.float32))
        value = (value + jnp.concatenate(parts, axis=1)).astype(jnp.bfloat16)
        x_ref[:, halves[h]] = value
        xr[h, x, group_rows] = value
        xs[h, y] = value

    halves = (pl.ds(0, HALF_SLAB), pl.ds(HALF_SLAB, HALF_SLAB))
    group_rows = pl.ds(0, GROUP_ROWS)
    pad = pl.ds(GROUP_ROWS, PANEL - GROUP_ROWS)
    for q in range(RING):
        for h in range(2):
            xr[h, q, pad] = jnp.zeros((PANEL - GROUP_ROWS, HALF_SLAB), jnp.bfloat16)
        yb[q, pad] = jnp.zeros((PANEL - GROUP_ROWS, HALF_SLAB), jnp.bfloat16)
    for p in range(2):
        to_sib[p, pad] = jnp.zeros((PANEL - GROUP_ROWS, BLOCK), jnp.bfloat16)
        own_f32[p, pad] = jnp.zeros((PANEL - GROUP_ROWS, BLOCK), jnp.float32)

    def gram(core, h, store):
        def tile(i, _):
            rows = pl.ds(pl.multiple_of((i % 2) * HALF_ROWS, 16), HALF_ROWS)
            value = lax.dot_general(
                xr[h, 2 * core + i // 2, rows], xs[h].reshape(BLOCK, HALF_SLAB),
                (((1,), (1,)), ((), ())), preferred_element_type=jnp.float32,
            )
            store(i // 2, rows, value)
            return 0

        lax.fori_loop(0, 4, tile, 0)

    def keep_own(p, rows, value):
        own_f32[p, rows] = value

    def keep_sib(p, rows, value):
        sib_f32[p, rows] = value

    def add_own(p, rows, value):
        own_f32[p, rows] += value

    def add_sib(p, rows, value):
        to_sib[p, rows] = (sib_f32[p, rows] + value).astype(jnp.bfloat16)

    land(0)
    a0 = gather_start("col", xr.at[0])
    b0 = gather_start("row", xs.at[0])
    a0 = gather_pass("col", xr.at[0], a0)
    b0 = gather_pass("row", xs.at[0], b0)
    land(1)
    a1 = gather_start("col", xr.at[1])
    b1 = gather_start("row", xs.at[1])
    gather_end(a0 + b0)
    gram(1 - c, 0, keep_sib)
    a1 = gather_pass("col", xr.at[1], a1)
    b1 = gather_pass("row", xs.at[1], b1)
    gram(c, 0, keep_own)
    gather_end(a1 + b1)
    gram(1 - c, 1, add_sib)

    def shard_rows(s):
        return pl.ds(pl.multiple_of(((s + N_Z) % N_Z) * SHARD, 16), SHARD)

    f32 = jnp.float32
    plan = []
    for k in range(8):
        distance = 4 - (k + 1) // 2
        plan.append((True, k % 2, distance))
        plan.append((False, 1 - k % 2, distance))
    sib_in = []
    for upward, panel, distance in plan:
        rows = shard_rows(z + distance if upward else z - distance)
        sib_in.append(send(to_sib.at[panel, rows], from_sib.at[panel, rows], dev_sib))
    gram(c, 1, add_own)

    up_in, down_in = [], []
    for (upward, panel, distance), arrival in zip(plan, sib_in):
        rows = shard_rows(z + distance if upward else z - distance)
        arrival.wait_recv()
        term = own_f32[panel, rows] + from_sib[panel, rows].astype(f32)
        if distance == 0:
            up, down = (6, 5) if panel == 0 else (5, 6)
            up_in[up].wait_recv()
            down_in[down].wait_recv()
            term = term + ring_f[up].astype(f32) + ring_b[down].astype(f32)
            g_full[2 * c + panel, rows] = term.astype(jnp.bfloat16)
            continue
        arrivals, ring, device = (up_in, ring_f, dev_up) if upward else (down_in, ring_b, dev_down)
        k = len(arrivals)
        if k < 2:
            src = gh.at[2 * k + int(upward)]
        else:
            arrivals[k - 2].wait_recv()
            src = ring.at[k - 2]
            term = term + ring[k - 2].astype(f32)
        src[...] = term.astype(jnp.bfloat16)
        arrivals.append(send(src, ring.at[k], device))
    mine = shard_rows(z)

    pending = []

    def relay(panel, rows, device):
        ref = g_full.at[2 * c + panel, rows]
        return send(ref, ref, device)

    up_in, down_in = [], []
    for k in range(9):
        back_by = k // 2
        up_part, down_part = (k % 2, shard_rows(z - back_by)), (1 - k % 2, shard_rows(z + back_by))
        if k >= 2:
            up_in[k - 2].wait_recv()
        if k < 7:
            up_in.append(relay(*up_part, dev_up))
        if k >= 2:
            down_in[k - 2].wait_recv()
        if k < 7:
            down_in.append(relay(*down_part, dev_down))
        pending.append(relay(*up_part, dev_sib))
        if k >= 2:
            pending.append(relay(*down_part, dev_sib))
    for copy in pending:
        copy.wait_recv()

    def reduce_start(axis, buf, a_ref, b_ref):
        p = place[axis]
        right, left = near[axis]
        far = (p + 2) % RING
        return (send(buf.at[far, top], a_ref, right), send(buf.at[far, bottom], b_ref, left))

    def reduce_near(axis, buf, c_ref, d_ref):
        p = place[axis]
        right, left = near[axis]
        after, before = (p + 1) % RING, (p + 3) % RING
        return (
            send(buf.at[after, bottom], c_ref.at[bottom], right),
            send(buf.at[before, top], d_ref.at[top], left),
        )

    def reduce_pass(axis, buf, a_ref, b_ref, c_ref, d_ref, state):
        p = place[axis]
        right, left = near[axis]
        after, before = (p + 1) % RING, (p + 3) % RING
        state[0].wait_recv()
        buf[after, top] = (buf[after, top].astype(f32) + a_ref[...].astype(f32)).astype(jnp.bfloat16)
        c2 = send(buf.at[after, top], c_ref.at[top], right)
        state[1].wait_recv()
        buf[before, bottom] = (buf[before, bottom].astype(f32) + b_ref[...].astype(f32)).astype(jnp.bfloat16)
        d2 = send(buf.at[before, bottom], d_ref.at[bottom], left)
        return (c2, d2)

    first, second = pl.ds(0, HALF_SLAB), pl.ds(HALF_SLAB, HALF_SLAB)
    slots_a, slots_b, slots_a2, slots_b2 = [[r.at[i] for r in (got_a, got_b, got_c, got_d)] for i in range(4)]
    far, after, before = (x + 2) % RING, (x + 1) % RING, (x + 3) % RING

    def times(q, right):
        return jnp.dot(g_full[q, group_rows], right, preferred_element_type=f32)

    def open_a(buf, right, slots):
        buf[far] = times(far, right()).astype(jnp.bfloat16)
        state = reduce_start("col", buf, *slots[:2])
        buf[after] = times(after, right()).astype(jnp.bfloat16)
        buf[before] = times(before, right()).astype(jnp.bfloat16)
        near_copies = reduce_near("col", buf, *slots[2:])
        return state, near_copies

    def open_b(buf, right, slots):
        def columns(j, _):
            cols = pl.ds(pl.multiple_of(j * LANES, LANES), LANES)
            z_b[cols] = lax.dot_general(
                g_full[:, :, cols].reshape(RING * PANEL, LANES), right, (((0,), (0,)), ((), ())),
                preferred_element_type=f32,
            )
            return 0

        lax.fori_loop(0, BLOCK // LANES, columns, 0)
        buf[...] = z_b[...].astype(jnp.bfloat16).reshape(RING, GROUP_ROWS, HALF_SLAB)
        state = reduce_start("row", buf, *slots[:2])
        return state, reduce_near("row", buf, *slots[2:])

    def pass_on(axis, buf, slots, opened):
        return opened[1] + reduce_pass(axis, buf, *slots, opened[0])

    def close(tail, slots, total, cols):
        gather_end(tail)
        total[:, cols] = total[:, cols] + slots[2][...].astype(f32) + slots[3][...].astype(f32)

    def own_b(total):
        total[:, second] = z_b[pl.ds(pl.multiple_of(y * GROUP_ROWS, 8), GROUP_ROWS)]

    oa = open_a(part.at[0], lambda: xs[0].reshape(BLOCK, HALF_SLAB), slots_a)
    ob = open_b(part.at[1], xr[1].reshape(RING * PANEL, HALF_SLAB), slots_b)
    y_f32[:, first] = times(x, xs[0].reshape(BLOCK, HALF_SLAB))
    own_b(y_f32)
    oa = pass_on("col", part.at[0], slots_a, oa)
    ob = pass_on("row", part.at[1], slots_b, ob)
    close(oa, slots_a, y_f32, first)
    ya[y] = y_f32[:, first].astype(jnp.bfloat16)
    sa = gather_start("row", ya)
    close(ob, slots_b, y_f32, second)
    yb[x, group_rows] = y_f32[:, second].astype(jnp.bfloat16)
    sb = gather_start("col", yb)
    sa = gather_pass("row", ya, sa)
    sb = gather_pass("col", yb, sb)
    gather_end(sa)

    oa = open_a(part2.at[0], lambda: ya[...].reshape(BLOCK, HALF_SLAB), slots_a2)
    gather_end(sb)
    ob = open_b(part2.at[1], yb[...].reshape(RING * PANEL, HALF_SLAB), slots_b2)
    z_f32[:, first] = times(x, ya[...].reshape(BLOCK, HALF_SLAB))
    own_b(z_f32)
    oa = pass_on("col", part2.at[0], slots_a2, oa)
    ob = pass_on("row", part2.at[1], slots_b2, ob)

    _, row_of = targets(N_DP * MAIN, MAIN, 0, (N_DP * MAIN, 1), 0)
    pick = (lax.broadcasted_iota(jnp.int32, (N_DP * MAIN, GROUP_ROWS), 1) == row_of).astype(f32).astype(jnp.bfloat16)
    ke, row_e = targets(N_DP * EXTRA, EXTRA, MAIN, (N_DP * EXTRA, 1), 0)
    ke = ke % EXTRA

    def back_copies(o):
        there = (dp + o) % N_DP
        device = (there, y, x)
        return (
            message(outgoing.at[0, there], returned.at[0, dp], device, slot=3 * N_DP + o),
            message(outgoing.at[1, there], returned.at[1, dp], device, slot=4 * N_DP + o),
            message(extra.at[there], returned_extra.at[dp], device, slot=5 * N_DP + o),
        )

    def leave(h, cols):
        update[:, cols] = (
            SCALE * (LINEAR_COEF * x_ref[:, cols].astype(f32) + (CUBIC_COEF * y_f32[:, cols] + QUINTIC_COEF * z_f32[:, cols]))
        ).astype(jnp.bfloat16)
        outgoing[h] = (
            jnp.dot(pick, update[:, cols], preferred_element_type=f32).astype(jnp.bfloat16).reshape(N_DP, MAIN, HALF_SLAB)
        )

        def send_back(o, _):
            back_copies(o)[h].start()
            return 0

        lax.fori_loop(1, N_DP, send_back, 0)
        returned[h, dp] = outgoing[h, dp]

    close(oa, slots_a2, z_f32, first)
    leave(0, first)
    close(ob, slots_b2, z_f32, second)
    leave(1, second)
    late = jnp.zeros((N_DP * EXTRA, LANES), f32)
    for j in range(4):
        row_j = jnp.where(ke // 2 == j, row_e - 2 * j, -1)
        pick_j = (lax.broadcasted_iota(jnp.int32, (N_DP * EXTRA, GROUP_ROWS), 1) == row_j).astype(f32).astype(jnp.bfloat16)
        late += jnp.dot(pick_j, update[:, j * LANES : (j + 1) * LANES], preferred_element_type=f32)
    extra[...] = late.astype(jnp.bfloat16).reshape(N_DP, EXTRA, LANES)

    def send_extra(o, _):
        back_copies(o)[2].start()
        return 0

    lax.fori_loop(1, N_DP, send_extra, 0)
    returned_extra[dp] = extra[dp]

    def wait_back(o, _):
        for copy in back_copies(o):
            copy.wait()
        return 0

    lax.fori_loop(1, N_DP, wait_back, 0)
    for copy in started:
        copy.wait_send()


def finish_kernel(lengths_ref, returned, returned_extra, out_ref, back, extra_tmp):
    dp = lax.axis_index("dp")
    group = lax.axis_index("row") * RING + lax.axis_index("col")
    my_start = jnp.int32(0)
    for d in range(N_DP):
        my_start = my_start + jnp.where(d < dp, lengths_ref[group, d], 0)
    my_length = lengths_ref[group, dp]
    lead = my_start % COLS
    lead_rows, lead_lanes = lead // LANES, lead % LANES
    turn = (LANES - lead_lanes) % LANES

    def unpack(d, _):
        extra_tmp[...] = pltpu.roll(returned_extra[d].astype(jnp.float32), turn, 1)
        for j in range(4):
            back[pl.ds(d * 4 + j, MAIN, stride=CHUNKS)] = pltpu.roll(
                returned[j // 2, d, :, pl.ds(j % 2 * LANES, LANES)].astype(jnp.float32), turn, 1)
            back[pl.ds(d * 4 + j + MAIN * CHUNKS, 2, stride=CHUNKS)] = extra_tmp[2 * j : 2 * j + 2]
        return 0

    lax.fori_loop(0, N_DP, unpack, 0)
    back[pl.ds(34 * CHUNKS, 8)] = jnp.zeros((8, LANES), jnp.float32)

    def finish(i, _):
        here = back[pl.ds(i * STEP + lead_rows, STEP)]
        after = back[pl.ds(i * STEP + lead_rows + 1, STEP)]
        lane = lax.broadcasted_iota(jnp.int32, (STEP, LANES), 1)
        value = jnp.where(lane + lead_lanes < LANES, here, after)
        value = jnp.where(slots(i) < my_length, value, 0.0).reshape(1, STEP * LANES)
        out_ref[:, pl.ds(pl.multiple_of(i * STEP * LANES, LANES), STEP * LANES)] = value.astype(jnp.bfloat16)
        return 0

    lax.fori_loop(0, FLAT_ROWS // STEP, finish, 0)


def newton_schulz(lengths, flat):
    bf, f32 = jnp.bfloat16, jnp.float32
    vmem = pltpu.VMEM
    returned, returned_extra = pl.pallas_call(
        core_kernel,
        out_shape=(
            jax.ShapeDtypeStruct((2, N_DP, MAIN, HALF_SLAB), bf),
            jax.ShapeDtypeStruct((N_DP, EXTRA, LANES), bf),
        ),
        in_specs=[pl.BlockSpec(memory_space=pltpu.SMEM), pl.BlockSpec(memory_space=pltpu.VMEM)],
        out_specs=[pl.BlockSpec(memory_space=pltpu.VMEM)] * 2,
        scratch_shapes=[
            vmem((LEAD + FLAT_ROWS + 88, LANES), f32),
            vmem((2, N_DP, MAIN, HALF_SLAB), bf),
            vmem((2, N_DP, MAIN, HALF_SLAB), bf),
            vmem((EXTRA, LANES), f32),
            vmem((N_DP, EXTRA, LANES), bf),
            vmem((2, N_DP, MAIN, HALF_SLAB), bf),
            vmem((N_DP, EXTRA, LANES), bf),
            vmem((GROUP_ROWS, SLAB), bf),
            vmem((2, RING, PANEL, HALF_SLAB), bf),
            vmem((2, RING, GROUP_ROWS, HALF_SLAB), bf),
            vmem((2, PANEL, BLOCK), f32),
            vmem((2, PANEL, BLOCK), f32),
            vmem((2, PANEL, BLOCK), bf),
            vmem((2, PANEL, BLOCK), bf),
            vmem((4, SHARD, BLOCK), bf),
            vmem((7, SHARD, BLOCK), bf),
            vmem((7, SHARD, BLOCK), bf),
            vmem((RING, PANEL, BLOCK), bf),
            vmem((2, RING, GROUP_ROWS, HALF_SLAB), bf),
            vmem((4, HALF_ROWS, HALF_SLAB), bf),
            vmem((4, HALF_ROWS, HALF_SLAB), bf),
            vmem((4, GROUP_ROWS, HALF_SLAB), bf),
            vmem((4, GROUP_ROWS, HALF_SLAB), bf),
            vmem((GROUP_ROWS, SLAB), f32),
            vmem((RING, GROUP_ROWS, HALF_SLAB), bf),
            vmem((RING, PANEL, HALF_SLAB), bf),
            vmem((2, RING, GROUP_ROWS, HALF_SLAB), bf),
            vmem((BLOCK, HALF_SLAB), f32),
            vmem((GROUP_ROWS, SLAB), f32),
            vmem((GROUP_ROWS, SLAB), bf),
            pltpu.SemaphoreType.DMA((N_MESSAGES,)),
            pltpu.SemaphoreType.DMA((N_MESSAGES,)),
        ],
        compiler_params=pltpu.CompilerParams(
            collective_id=0, has_side_effects=True, vmem_limit_bytes=56 * 1024 * 1024
        ),
    )(lengths, flat)
    return pl.pallas_call(
        finish_kernel,
        out_shape=jax.ShapeDtypeStruct((1, FLAT_ROWS * LANES), bf),
        in_specs=[pl.BlockSpec(memory_space=pltpu.SMEM)] + [pl.BlockSpec(memory_space=pltpu.VMEM)] * 2,
        out_specs=pl.BlockSpec(memory_space=pltpu.VMEM),
        scratch_shapes=[vmem((34 * CHUNKS + 8, LANES), f32), vmem((EXTRA, LANES), f32)],
        compiler_params=pltpu.CompilerParams(vmem_limit_bytes=32 * 1024 * 1024),
    )(lengths, returned, returned_extra)


def local(flat_iterate, lengths):
    return newton_schulz(lengths, flat_iterate)


def solution(mesh):
    return jax.shard_map(
        local,
        mesh=mesh,
        in_specs=(P(("dp", "row", "col"), None), P()),
        out_specs=P(("dp", "row", "col"), None),
        check_vma=False,
    )
```

```python
import math

import jax
import jax.numpy as jnp
from jax import lax
from jax.experimental import pallas as pl
from jax.experimental.pallas import tpu as pltpu
from jax.sharding import PartitionSpec as P

COLS = 8192
ROWS = 5632


LINEAR_COEF = 3.4445
CUBIC_COEF = -4.775
QUINTIC_COEF = 2.0315

N_DP = 16
N_Z = 8
RING = 4
GROUP_ROWS = 352
HALF_ROWS = 176
SLAB = 512
BLOCK = 1408
CORE_ROWS = 704
SHARD = 48
PANEL = N_Z * SHARD
HALF_SLAB = SLAB // 2
LANES = 128
CHUNKS = COLS // LANES
FLAT_ROWS = 2112
MAIN = 32
EXTRA = 16
LEAD = 72
STEP = 176
N_MESSAGES = 320
MESH = pl.DeviceIdType.MESH
SCALE = 0.2 * math.sqrt(max(ROWS, COLS))


def slots(i):
    return (
        i * (STEP * LANES)
        + lax.broadcasted_iota(jnp.int32, (STEP, LANES), 0) * LANES
        + lax.broadcasted_iota(jnp.int32, (STEP, LANES), 1)
    )


def core_kernel(
    lengths_ref, flat_ref, returned, returned_extra, staged, canvas, outgoing, extra_tmp, extra, arrived, arrived_extra, x_ref, xr, xs, own_f32, sib_f32, to_sib, from_sib, gh, ring_f, ring_b, g_full,
    part, got_a, got_b, got_c, got_d, y_f32, ya, yb, y_tmp, y_out, y_in, y_own, z_b, z_f32, update, send_sem, recv_sem,
):
    dp = lax.axis_index("dp")
    y = lax.axis_index("row")
    x = lax.axis_index("col")
    z, c = dp // 2, dp % 2
    sib_dp = z * 2 + 1 - c
    up_dp = ((z + 1) % N_Z) * 2 + c
    down_dp = ((z + 7) % N_Z) * 2 + c
    dev_sib = (sib_dp, y, x)
    dev_up = (up_dp, y, x)
    dev_down = (down_dp, y, x)
    near = {
        "col": ((dp, y, (x + 1) % RING), (dp, y, (x + 3) % RING)),
        "row": ((dp, (y + 1) % RING, x), (dp, (y + 3) % RING, x)),
    }
    place = {"col": x, "row": y}

    barrier = pltpu.get_barrier_semaphore()
    for peer in near["col"] + near["row"]:
        pl.semaphore_signal(barrier, inc=1, device_id=peer, device_id_type=MESH)

    def greet(o, _):
        pl.semaphore_signal(barrier, inc=1, device_id=((dp + o) % N_DP, y, x), device_id_type=MESH)
        return 0

    lax.fori_loop(1, N_DP, greet, 0)

    def by_distance(i):
        return N_DP // 2 + (i + 1) // 2 * (1 - 2 * (i % 2))

    counter = [6 * N_DP]
    started = []

    def message(src, dst, device, slot=None):
        if slot is None:
            slot = counter[0]
            counter[0] += 1
        return pltpu.make_async_remote_copy(
            src_ref=src, dst_ref=dst, send_sem=send_sem.at[slot], recv_sem=recv_sem.at[slot],
            device_id=device, device_id_type=MESH,
        )

    def send(src, dst, device):
        copy = message(src, dst, device)
        copy.start()
        started.append(copy)
        return copy

    top, bottom = pl.ds(0, HALF_ROWS), pl.ds(HALF_ROWS, HALF_ROWS)

    def gather_start(axis, buf):
        p = place[axis]
        right, left = near[axis]
        a = [send(buf.at[p, h], buf.at[p, h], right) for h in (top, bottom)]
        b = [send(buf.at[p, h], buf.at[p, h], left) for h in (bottom, top)]
        return a, b

    def gather_pass(axis, buf, state):
        p = place[axis]
        right, left = near[axis]
        a, b = state
        before, after = (p + 3) % RING, (p + 1) % RING
        a[0].wait_recv()
        f = send(buf.at[before, top], buf.at[before, top], right)
        b[0].wait_recv()
        g = send(buf.at[after, bottom], buf.at[after, bottom], left)
        return a[1], b[1], f, g

    def gather_end(tail):
        for copy in tail:
            copy.wait_recv()

    group = y * RING + x
    my_start = jnp.int32(0)
    begin = jnp.int32(0)
    first_rows = []
    for d in range(N_DP):
        first_rows.append(begin // COLS)
        my_start = jnp.where(dp == d, begin, my_start)
        begin = begin + lengths_ref[group, d]
    my_length = lengths_ref[group, dp]
    lead = my_start % COLS
    lead_rows, lead_lanes = lead // LANES, lead % LANES
    staged[pl.ds(0, LEAD)] = jnp.zeros((LEAD, LANES), jnp.float32)
    tail_rows = staged.shape[0] - LEAD - FLAT_ROWS
    staged[pl.ds(LEAD + FLAT_ROWS, tail_rows)] = jnp.zeros((tail_rows, LANES), jnp.float32)

    def stage(i, _):
        value = flat_ref[:, pl.ds(pl.multiple_of(i * STEP * LANES, LANES), STEP * LANES)].astype(jnp.float32).reshape(STEP, LANES)
        value = jnp.where(slots(i) < my_length, value, 0.0)
        staged[pl.ds(pl.multiple_of(i * STEP + LEAD, 8), STEP)] = pltpu.roll(value, lead_lanes, 1)
        return 0

    lax.fori_loop(0, FLAT_ROWS // STEP, stage, 0)
    extra_tmp[...] = jnp.zeros_like(extra_tmp)

    def out_copies(o):
        there = (dp + o) % N_DP
        device = (there, y, x)
        return (
            message(extra.at[there], arrived_extra.at[dp], device, slot=o),
            message(canvas.at[0, there], arrived.at[0, dp], device, slot=N_DP + o),
            message(canvas.at[1, there], arrived.at[1, dp], device, slot=2 * N_DP + o),
        )

    def place_part(o, _):
        there = (dp + o) % N_DP
        lane = lax.broadcasted_iota(jnp.int32, (MAIN, LANES), 1)
        lane2 = lax.broadcasted_iota(jnp.int32, (2, LANES), 1)
        start = LEAD - lead_rows + there * 4
        before = staged[pl.ds(start - 1, MAIN, stride=CHUNKS)]
        before2 = staged[pl.ds(start - 1 + MAIN * CHUNKS, 2, stride=CHUNKS)]
        for j in range(4):
            here = staged[pl.ds(start + j, MAIN, stride=CHUNKS)]
            here2 = staged[pl.ds(start + j + MAIN * CHUNKS, 2, stride=CHUNKS)]
            canvas[j // 2, there, :, pl.ds(j % 2 * LANES, LANES)] = jnp.where(lane >= lead_lanes, here, before).astype(jnp.bfloat16)
            extra_tmp[pl.ds(j * 2, 2)] = jnp.where(lane2 >= lead_lanes, here2, before2)
            before, before2 = here, here2
        extra[there] = extra_tmp[...].astype(jnp.bfloat16)
        return 0

    lax.fori_loop(1, N_DP + 1, place_part, 0)
    pl.semaphore_wait(barrier, 4 + N_DP - 1)

    def send_out(i, _):
        for copy in out_copies(by_distance(i))[:2]:
            copy.start()
        return 0

    def send_out_more(i, _):
        out_copies(by_distance(i))[2].start()
        return 0

    lax.fori_loop(0, N_DP - 1, send_out, 0)
    lax.fori_loop(0, N_DP - 1, send_out_more, 0)
    for h in range(2):
        arrived[h, dp] = canvas[h, dp]
    arrived_extra[dp] = extra[dp]

    def targets(length, width, offset, shape, dim):
        k = lax.broadcasted_iota(jnp.int32, shape, dim)
        found = jnp.full(shape, -1, jnp.int32)
        for d in range(N_DP):
            inside = k // width == d
            found = jnp.where(inside, first_rows[d] + k % width + offset, found)
        return k, found

    k, row_of = targets(N_DP * MAIN, MAIN, 0, (1, N_DP * MAIN), 1)
    pick = (lax.broadcasted_iota(jnp.int32, (GROUP_ROWS, N_DP * MAIN), 0) == row_of).astype(jnp.float32).astype(jnp.bfloat16)
    ke, row_e = targets(N_DP * EXTRA, EXTRA, MAIN, (1, N_DP * EXTRA), 1)
    ke = ke % EXTRA

    def land(h):
        def wait_out(o, _):
            for copy in out_copies(o)[2 * h : 2 + h]:
                copy.wait()
            return 0

        lax.fori_loop(1, N_DP, wait_out, 0)
        value = jnp.dot(pick, arrived[h].reshape(N_DP * MAIN, HALF_SLAB), preferred_element_type=jnp.float32)
        late = arrived_extra[...].reshape(N_DP * EXTRA, LANES)
        parts = []
        for j in (2 * h, 2 * h + 1):
            row_j = jnp.where(ke // 2 == j, row_e - 2 * j, -1)
            pick_j = (lax.broadcasted_iota(jnp.int32, (GROUP_ROWS, N_DP * EXTRA), 0) == row_j).astype(jnp.float32).astype(jnp.bfloat16)
            parts.append(jnp.dot(pick_j, late, preferred_element_type=jnp.float32))
        value = (value + jnp.concatenate(parts, axis=1)).astype(jnp.bfloat16)
        x_ref[:, halves[h]] = value
        xr[h, x, group_rows] = value
        xs[h, y] = value

    halves = (pl.ds(0, HALF_SLAB), pl.ds(HALF_SLAB, HALF_SLAB))
    group_rows = pl.ds(0, GROUP_ROWS)
    pad = pl.ds(GROUP_ROWS, PANEL - GROUP_ROWS)
    for q in range(RING):
        for h in range(2):
            xr[h, q, pad] = jnp.zeros((PANEL - GROUP_ROWS, HALF_SLAB), jnp.bfloat16)
    for p in range(2):
        to_sib[p, pad] = jnp.zeros((PANEL - GROUP_ROWS, BLOCK), jnp.bfloat16)
        own_f32[p, pad] = jnp.zeros((PANEL - GROUP_ROWS, BLOCK), jnp.float32)

    def gram(core, h, store):
        def tile(i, _):
            rows = pl.ds(pl.multiple_of((i % 2) * HALF_ROWS, 16), HALF_ROWS)
            value = lax.dot_general(
                xr[h, 2 * core + i // 2, rows], xs[h].reshape(BLOCK, HALF_SLAB),
                (((1,), (1,)), ((), ())), preferred_element_type=jnp.float32,
            )
            store(i // 2, rows, value)
            return 0

        lax.fori_loop(0, 4, tile, 0)

    def keep_own(p, rows, value):
        own_f32[p, rows] = value

    def keep_sib(p, rows, value):
        sib_f32[p, rows] = value

    def add_own(p, rows, value):
        own_f32[p, rows] += value

    def add_sib(p, rows, value):
        to_sib[p, rows] = (sib_f32[p, rows] + value).astype(jnp.bfloat16)

    land(0)
    a0 = gather_start("col", xr.at[0])
    b0 = gather_start("row", xs.at[0])
    land(1)
    a1 = gather_start("col", xr.at[1])
    b1 = gather_start("row", xs.at[1])
    a0 = gather_pass("col", xr.at[0], a0)
    b0 = gather_pass("row", xs.at[0], b0)
    a1 = gather_pass("col", xr.at[1], a1)
    b1 = gather_pass("row", xs.at[1], b1)
    gather_end(a0 + b0)
    gram(1 - c, 0, keep_sib)
    gram(c, 0, keep_own)
    gather_end(a1 + b1)
    gram(1 - c, 1, add_sib)

    def shard_rows(s):
        return pl.ds(pl.multiple_of(((s + N_Z) % N_Z) * SHARD, 16), SHARD)

    f32 = jnp.float32
    plan = []
    for k in range(8):
        distance = 4 - (k + 1) // 2
        plan.append((True, k % 2, distance))
        plan.append((False, 1 - k % 2, distance))
    sib_in = []
    for upward, panel, distance in plan:
        rows = shard_rows(z + distance if upward else z - distance)
        sib_in.append(send(to_sib.at[panel, rows], from_sib.at[panel, rows], dev_sib))
    gram(c, 1, add_own)

    up_in, down_in = [], []
    for (upward, panel, distance), arrival in zip(plan, sib_in):
        rows = shard_rows(z + distance if upward else z - distance)
        arrival.wait_recv()
        term = own_f32[panel, rows] + from_sib[panel, rows].astype(f32)
        if distance == 0:
            up, down = (6, 5) if panel == 0 else (5, 6)
            up_in[up].wait_recv()
            down_in[down].wait_recv()
            term = term + ring_f[up].astype(f32) + ring_b[down].astype(f32)
            g_full[2 * c + panel, rows] = term.astype(jnp.bfloat16)
            continue
        arrivals, ring, device = (up_in, ring_f, dev_up) if upward else (down_in, ring_b, dev_down)
        k = len(arrivals)
        if k < 2:
            src = gh.at[2 * k + int(upward)]
        else:
            arrivals[k - 2].wait_recv()
            src = ring.at[k - 2]
            term = term + ring[k - 2].astype(f32)
        src[...] = term.astype(jnp.bfloat16)
        arrivals.append(send(src, ring.at[k], device))
    mine = shard_rows(z)

    sib_parts = {}

    def relay(panel, rows, device):
        ref = g_full.at[2 * c + panel, rows]
        return send(ref, ref, device)

    y_sums, y_left, y_right = {}, [], []
    order = (0, -1, 1, -2, 2, -3, 3, 4)

    def multiply(shift):
        i, rows = order.index(shift), shard_rows(z + shift)
        for copy in sib_parts[shift]:
            copy.wait_recv()
        left = g_full[:, rows, :].reshape(RING * SHARD, BLOCK)
        for h in range(2):
            value = jnp.dot(left, xs[h].reshape(BLOCK, HALF_SLAB), preferred_element_type=f32)
            y_tmp[:, :, halves[h]] = value.reshape(RING, SHARD, HALF_SLAB)
        y_out[i] = y_tmp[...].astype(jnp.bfloat16)
        y_sums[shift] = [
            send(y_out.at[i, (x + o) % RING], y_in.at[i, o - 1], (dp, y, (x + o) % RING)) for o in (2, 1, 3)
        ]
        y_own[i] = y_tmp[x]

    def add_up(shift):
        i, rows = order.index(shift), shard_rows(z + shift)
        for copy in y_sums[shift]:
            copy.wait_recv()
        value = y_own[i] + y_in[i, 0].astype(f32) + y_in[i, 1].astype(f32) + y_in[i, 2].astype(f32)
        y_f32[rows] = value
        ya[y, rows] = value[:, :HALF_SLAB].astype(jnp.bfloat16)
        yb[x, rows] = value[:, HALF_SLAB:].astype(jnp.bfloat16)
        for o in (2, 1, 3):
            y_left.append(send(ya.at[y, rows], ya.at[y, rows], (dp, (y + o) % RING, x)))
            y_right.append(send(yb.at[x, rows], yb.at[x, rows], (dp, y, (x + o) % RING)))

    up_in, down_in = [], []
    for k in range(9):
        back_by = k // 2
        up_part, down_part = (k % 2, shard_rows(z - back_by)), (1 - k % 2, shard_rows(z + back_by))
        if k >= 2:
            up_in[k - 2].wait_recv()
        if k < 7:
            up_in.append(relay(*up_part, dev_up))
        if k >= 2:
            down_in[k - 2].wait_recv()
        if k < 7:
            down_in.append(relay(*down_part, dev_down))
        sib_parts.setdefault(4 if k == 8 else -back_by, []).append(relay(*up_part, dev_sib))
        if k >= 2:
            sib_parts.setdefault(back_by, []).append(relay(*down_part, dev_sib))
        for shift in {2: (0,), 4: (-1, 1), 6: (-2, 2), 7: (-3, 3), 8: (4,)}.get(k, ()):
            multiply(shift)
        for shift in {5: (0,), 6: (-1, 1), 8: (-2, 2, -3, 3, 4)}.get(k, ()):
            add_up(shift)

    def reduce_start(axis, buf, a_ref, b_ref):
        p = place[axis]
        right, left = near[axis]
        far = (p + 2) % RING
        return (send(buf.at[far, top], a_ref, right), send(buf.at[far, bottom], b_ref, left))

    def reduce_near(axis, buf, c_ref, d_ref):
        p = place[axis]
        right, left = near[axis]
        after, before = (p + 1) % RING, (p + 3) % RING
        return (
            send(buf.at[after, bottom], c_ref.at[bottom], right),
            send(buf.at[before, top], d_ref.at[top], left),
        )

    def reduce_pass(axis, buf, a_ref, b_ref, c_ref, d_ref, state):
        p = place[axis]
        right, left = near[axis]
        after, before = (p + 1) % RING, (p + 3) % RING
        state[0].wait_recv()
        buf[after, top] = (buf[after, top].astype(f32) + a_ref[...].astype(f32)).astype(jnp.bfloat16)
        c2 = send(buf.at[after, top], c_ref.at[top], right)
        state[1].wait_recv()
        buf[before, bottom] = (buf[before, bottom].astype(f32) + b_ref[...].astype(f32)).astype(jnp.bfloat16)
        d2 = send(buf.at[before, bottom], d_ref.at[bottom], left)
        return (c2, d2)

    first, second = pl.ds(0, HALF_SLAB), pl.ds(HALF_SLAB, HALF_SLAB)
    slots_a, slots_b = [[r.at[i] for r in (got_a, got_b, got_c, got_d)] for i in range(2)]
    far, after, before = (x + 2) % RING, (x + 1) % RING, (x + 3) % RING

    def times(q, right):
        return jnp.dot(g_full[q, group_rows], right, preferred_element_type=f32)

    def open_a(buf, right, slots):
        buf[far] = times(far, right()).astype(jnp.bfloat16)
        state = reduce_start("col", buf, *slots[:2])
        buf[after] = times(after, right()).astype(jnp.bfloat16)
        buf[before] = times(before, right()).astype(jnp.bfloat16)
        near_copies = reduce_near("col", buf, *slots[2:])
        return state, near_copies

    def open_b(buf, right, slots):
        def columns(j, _):
            cols = pl.ds(pl.multiple_of(j * LANES, LANES), LANES)
            z_b[cols] = lax.dot_general(
                g_full[:, :, cols].reshape(RING * PANEL, LANES), right, (((0,), (0,)), ((), ())),
                preferred_element_type=f32,
            )
            return 0

        lax.fori_loop(0, BLOCK // LANES, columns, 0)
        buf[...] = z_b[...].astype(jnp.bfloat16).reshape(RING, GROUP_ROWS, HALF_SLAB)
        state = reduce_start("row", buf, *slots[:2])
        return state, reduce_near("row", buf, *slots[2:])

    def pass_on(axis, buf, slots, opened):
        return opened[1] + reduce_pass(axis, buf, *slots, opened[0])

    def close(tail, slots, total, cols):
        gather_end(tail)
        total[:, cols] = total[:, cols] + slots[2][...].astype(f32) + slots[3][...].astype(f32)

    def own_b(total):
        total[:, second] = z_b[pl.ds(pl.multiple_of(y * GROUP_ROWS, 8), GROUP_ROWS)]

    gather_end(y_left)
    oa = open_a(part.at[0], lambda: ya[:, :GROUP_ROWS].reshape(BLOCK, HALF_SLAB), slots_a)
    gather_end(y_right)
    ob = open_b(part.at[1], yb[...].reshape(RING * PANEL, HALF_SLAB), slots_b)
    z_f32[:, first] = times(x, ya[:, :GROUP_ROWS].reshape(BLOCK, HALF_SLAB))
    own_b(z_f32)
    oa = pass_on("col", part.at[0], slots_a, oa)
    ob = pass_on("row", part.at[1], slots_b, ob)

    _, row_of = targets(N_DP * MAIN, MAIN, 0, (N_DP * MAIN, 1), 0)
    pick = (lax.broadcasted_iota(jnp.int32, (N_DP * MAIN, GROUP_ROWS), 1) == row_of).astype(f32).astype(jnp.bfloat16)
    ke, row_e = targets(N_DP * EXTRA, EXTRA, MAIN, (N_DP * EXTRA, 1), 0)
    ke = ke % EXTRA

    def back_copies(o):
        there = (dp + o) % N_DP
        device = (there, y, x)
        return (
            message(outgoing.at[0, there], returned.at[0, dp], device, slot=3 * N_DP + o),
            message(outgoing.at[1, there], returned.at[1, dp], device, slot=4 * N_DP + o),
            message(extra.at[there], returned_extra.at[dp], device, slot=5 * N_DP + o),
        )

    def leave(h, cols):
        update[:, cols] = (
            SCALE * (LINEAR_COEF * x_ref[:, cols].astype(f32) + (CUBIC_COEF * y_f32[group_rows, cols] + QUINTIC_COEF * z_f32[:, cols]))
        ).astype(jnp.bfloat16)
        outgoing[h] = (
            jnp.dot(pick, update[:, cols], preferred_element_type=f32).astype(jnp.bfloat16).reshape(N_DP, MAIN, HALF_SLAB)
        )

        def send_back(i, _):
            back_copies(by_distance(i))[h].start()
            return 0

        lax.fori_loop(0, N_DP - 1, send_back, 0)
        returned[h, dp] = outgoing[h, dp]

    close(oa, slots_a, z_f32, first)
    leave(0, first)
    close(ob, slots_b, z_f32, second)
    leave(1, second)
    late = jnp.zeros((N_DP * EXTRA, LANES), f32)
    for j in range(4):
        row_j = jnp.where(ke // 2 == j, row_e - 2 * j, -1)
        pick_j = (lax.broadcasted_iota(jnp.int32, (N_DP * EXTRA, GROUP_ROWS), 1) == row_j).astype(f32).astype(jnp.bfloat16)
        late += jnp.dot(pick_j, update[:, j * LANES : (j + 1) * LANES], preferred_element_type=f32)
    extra[...] = late.astype(jnp.bfloat16).reshape(N_DP, EXTRA, LANES)

    def send_extra(o, _):
        back_copies(o)[2].start()
        return 0

    lax.fori_loop(1, N_DP, send_extra, 0)
    returned_extra[dp] = extra[dp]

    def wait_back(o, _):
        for copy in back_copies(o):
            copy.wait()
        return 0

    lax.fori_loop(1, N_DP, wait_back, 0)
    for copy in started:
        copy.wait_send()


def finish_kernel(lengths_ref, returned, returned_extra, out_ref, back, extra_tmp):
    dp = lax.axis_index("dp")
    group = lax.axis_index("row") * RING + lax.axis_index("col")
    my_start = jnp.int32(0)
    for d in range(N_DP):
        my_start = my_start + jnp.where(d < dp, lengths_ref[group, d], 0)
    my_length = lengths_ref[group, dp]
    lead = my_start % COLS
    lead_rows, lead_lanes = lead // LANES, lead % LANES
    turn = (LANES - lead_lanes) % LANES

    def unpack(d, _):
        extra_tmp[...] = pltpu.roll(returned_extra[d].astype(jnp.float32), turn, 1)
        for j in range(4):
            back[pl.ds(d * 4 + j, MAIN, stride=CHUNKS)] = pltpu.roll(
                returned[j // 2, d, :, pl.ds(j % 2 * LANES, LANES)].astype(jnp.float32), turn, 1)
            back[pl.ds(d * 4 + j + MAIN * CHUNKS, 2, stride=CHUNKS)] = extra_tmp[2 * j : 2 * j + 2]
        return 0

    lax.fori_loop(0, N_DP, unpack, 0)
    back[pl.ds(34 * CHUNKS, 8)] = jnp.zeros((8, LANES), jnp.float32)

    def finish(i, _):
        here = back[pl.ds(i * STEP + lead_rows, STEP)]
        after = back[pl.ds(i * STEP + lead_rows + 1, STEP)]
        lane = lax.broadcasted_iota(jnp.int32, (STEP, LANES), 1)
        value = jnp.where(lane + lead_lanes < LANES, here, after)
        value = jnp.where(slots(i) < my_length, value, 0.0).reshape(1, STEP * LANES)
        out_ref[:, pl.ds(pl.multiple_of(i * STEP * LANES, LANES), STEP * LANES)] = value.astype(jnp.bfloat16)
        return 0

    lax.fori_loop(0, FLAT_ROWS // STEP, finish, 0)


def newton_schulz(lengths, flat):
    bf, f32 = jnp.bfloat16, jnp.float32
    vmem = pltpu.VMEM
    returned, returned_extra = pl.pallas_call(
        core_kernel,
        out_shape=(
            jax.ShapeDtypeStruct((2, N_DP, MAIN, HALF_SLAB), bf),
            jax.ShapeDtypeStruct((N_DP, EXTRA, LANES), bf),
        ),
        in_specs=[pl.BlockSpec(memory_space=pltpu.SMEM), pl.BlockSpec(memory_space=pltpu.VMEM)],
        out_specs=[pl.BlockSpec(memory_space=pltpu.VMEM)] * 2,
        scratch_shapes=[
            vmem((LEAD + FLAT_ROWS + 88, LANES), f32),
            vmem((2, N_DP, MAIN, HALF_SLAB), bf),
            vmem((2, N_DP, MAIN, HALF_SLAB), bf),
            vmem((EXTRA, LANES), f32),
            vmem((N_DP, EXTRA, LANES), bf),
            vmem((2, N_DP, MAIN, HALF_SLAB), bf),
            vmem((N_DP, EXTRA, LANES), bf),
            vmem((GROUP_ROWS, SLAB), bf),
            vmem((2, RING, PANEL, HALF_SLAB), bf),
            vmem((2, RING, GROUP_ROWS, HALF_SLAB), bf),
            vmem((2, PANEL, BLOCK), f32),
            vmem((2, PANEL, BLOCK), f32),
            vmem((2, PANEL, BLOCK), bf),
            vmem((2, PANEL, BLOCK), bf),
            vmem((4, SHARD, BLOCK), bf),
            vmem((7, SHARD, BLOCK), bf),
            vmem((7, SHARD, BLOCK), bf),
            vmem((RING, PANEL, BLOCK), bf),
            vmem((2, RING, GROUP_ROWS, HALF_SLAB), bf),
            vmem((2, HALF_ROWS, HALF_SLAB), bf),
            vmem((2, HALF_ROWS, HALF_SLAB), bf),
            vmem((2, GROUP_ROWS, HALF_SLAB), bf),
            vmem((2, GROUP_ROWS, HALF_SLAB), bf),
            vmem((PANEL, SLAB), f32),
            vmem((RING, PANEL, HALF_SLAB), bf),
            vmem((RING, PANEL, HALF_SLAB), bf),
            vmem((RING, SHARD, SLAB), f32),
            vmem((N_Z, RING, SHARD, SLAB), bf),
            vmem((N_Z, RING - 1, SHARD, SLAB), bf),
            vmem((N_Z, SHARD, SLAB), f32),
            vmem((BLOCK, HALF_SLAB), f32),
            vmem((GROUP_ROWS, SLAB), f32),
            vmem((GROUP_ROWS, SLAB), bf),
            pltpu.SemaphoreType.DMA((N_MESSAGES,)),
            pltpu.SemaphoreType.DMA((N_MESSAGES,)),
        ],
        compiler_params=pltpu.CompilerParams(
            collective_id=0, has_side_effects=True, vmem_limit_bytes=56 * 1024 * 1024
        ),
    )(lengths, flat)
    return pl.pallas_call(
        finish_kernel,
        out_shape=jax.ShapeDtypeStruct((1, FLAT_ROWS * LANES), bf),
        in_specs=[pl.BlockSpec(memory_space=pltpu.SMEM)] + [pl.BlockSpec(memory_space=pltpu.VMEM)] * 2,
        out_specs=pl.BlockSpec(memory_space=pltpu.VMEM),
        scratch_shapes=[vmem((34 * CHUNKS + 8, LANES), f32), vmem((EXTRA, LANES), f32)],
        compiler_params=pltpu.CompilerParams(vmem_limit_bytes=32 * 1024 * 1024),
    )(lengths, returned, returned_extra)


def local(flat_iterate, lengths):
    return newton_schulz(lengths, flat_iterate)


def solution(mesh):
    return jax.shard_map(
        local,
        mesh=mesh,
        in_specs=(P(("dp", "row", "col"), None), P()),
        out_specs=P(("dp", "row", "col"), None),
        check_vma=False,
    )
```

```python
import math

import jax
import jax.numpy as jnp
from jax import lax
from jax.experimental import pallas as pl
from jax.experimental.pallas import tpu as pltpu
from jax.sharding import PartitionSpec as P

COLS = 8192
ROWS = 5632


LINEAR_COEF = 3.4445
CUBIC_COEF = -4.775
QUINTIC_COEF = 2.0315

N_DP = 16
N_Z = 8
RING = 4
GROUP_ROWS = 352
HALF_ROWS = 176
SLAB = 512
BLOCK = 1408
CORE_ROWS = 704
SHARD = 48
PANEL = N_Z * SHARD
HALF_SLAB = SLAB // 2
LANES = 128
CHUNKS = COLS // LANES
FLAT_ROWS = 2112
MAIN = 32
EXTRA = 16
LEAD = 72
STEP = 176
PEERS = N_DP - 1
BACK_GROUP = 5
(
    OUT_0, OUT_1, OUT_EXTRA, BACK_0, BACK_1, BACK_EXTRA, X_R0, X_R1, X_S0, X_S1,
    TO_SIB, RING_UP, RING_DOWN, G_UP, G_DOWN, G_SIB, Y_SUM, Y_GATHER, Z_A, Z_B, N_SENT,
) = range(21)
N_RECEIVED = 128
MESH = pl.DeviceIdType.MESH
SCALE = 0.2 * math.sqrt(max(ROWS, COLS))


def slots(i):
    return (
        i * (STEP * LANES)
        + lax.broadcasted_iota(jnp.int32, (STEP, LANES), 0) * LANES
        + lax.broadcasted_iota(jnp.int32, (STEP, LANES), 1)
    )


def core_kernel(
    lengths_ref, flat_ref, out_ref, staged, canvas, outgoing, extra_tmp, extra, arrived, arrived_extra, x_ref, xr, xs, own_f32, sib_f32, to_sib, from_sib, gh, ring_f, ring_b, g_full,
    part, got_a, got_b, got_c, got_d, y_f32, ya, yb, y_tmp, y_out, y_in, y_own, z_b, z_f32, update, outgoing_extra, returned, returned_extra, back, send_sem, recv_sem,
):
    dp = lax.axis_index("dp")
    y = lax.axis_index("row")
    x = lax.axis_index("col")
    z, c = dp // 2, dp % 2
    sib_dp = z * 2 + 1 - c
    up_dp = ((z + 1) % N_Z) * 2 + c
    down_dp = ((z + 7) % N_Z) * 2 + c
    dev_sib = (sib_dp, y, x)
    dev_up = (up_dp, y, x)
    dev_down = (down_dp, y, x)
    near = {
        "col": ((dp, y, (x + 1) % RING), (dp, y, (x + 3) % RING)),
        "row": ((dp, (y + 1) % RING, x), (dp, (y + 3) % RING, x)),
    }
    place = {"col": x, "row": y}

    barrier = pltpu.get_barrier_semaphore()
    for peer in near["col"] + near["row"]:
        pl.semaphore_signal(barrier, inc=1, device_id=peer, device_id_type=MESH)

    def greet(o, _):
        pl.semaphore_signal(barrier, inc=1, device_id=((dp + o) % N_DP, y, x), device_id_type=MESH)
        return 0

    lax.fori_loop(1, N_DP, greet, 0)

    def by_distance(i):
        return N_DP // 2 + (i + 1) // 2 * (1 - 2 * (i % 2))

    counter = [10]

    def message(src, dst, device, group, slot):
        return pltpu.make_async_remote_copy(
            src_ref=src, dst_ref=dst, send_sem=send_sem.at[group], recv_sem=recv_sem.at[slot],
            device_id=device, device_id_type=MESH,
        )

    def new_slot():
        counter[0] += 1
        return counter[0] - 1

    def send(src, dst, device, group, slot=None):
        copy = message(src, dst, device, group, new_slot() if slot is None else slot)
        copy.start()
        return copy

    def all_sent(ref, group):
        message(ref, ref, dev_sib, group, 0).wait_send()

    def all_received(ref, slot):
        message(ref, ref, dev_sib, 0, slot).wait_recv()

    top, bottom = pl.ds(0, HALF_ROWS), pl.ds(HALF_ROWS, HALF_ROWS)

    def gather_start(axis, buf, group):
        p = place[axis]
        right, left = near[axis]
        a = [send(buf.at[p, h], buf.at[p, h], right, group) for h in (top, bottom)]
        b = [send(buf.at[p, h], buf.at[p, h], left, group) for h in (bottom, top)]
        return a, b

    def gather_pass(axis, buf, state, group):
        p = place[axis]
        right, left = near[axis]
        a, b = state
        before, after = (p + 3) % RING, (p + 1) % RING
        a[0].wait_recv()
        f = send(buf.at[before, top], buf.at[before, top], right, group)
        b[0].wait_recv()
        g = send(buf.at[after, bottom], buf.at[after, bottom], left, group)
        return a[1], b[1], f, g

    def gather_end(tail):
        for copy in tail:
            copy.wait_recv()

    group = y * RING + x
    my_start = jnp.int32(0)
    begin = jnp.int32(0)
    first_rows = []
    for d in range(N_DP):
        first_rows.append(begin // COLS)
        my_start = jnp.where(dp == d, begin, my_start)
        begin = begin + lengths_ref[group, d]
    my_length = lengths_ref[group, dp]
    lead = my_start % COLS
    lead_rows, lead_lanes = lead // LANES, lead % LANES
    staged[pl.ds(0, LEAD)] = jnp.zeros((LEAD, LANES), jnp.float32)
    tail_rows = staged.shape[0] - LEAD - FLAT_ROWS
    staged[pl.ds(LEAD + FLAT_ROWS, tail_rows)] = jnp.zeros((tail_rows, LANES), jnp.float32)

    def stage(i, _):
        value = flat_ref[:, pl.ds(pl.multiple_of(i * STEP * LANES, LANES), STEP * LANES)].astype(jnp.float32).reshape(STEP, LANES)
        value = jnp.where(slots(i) < my_length, value, 0.0)
        staged[pl.ds(pl.multiple_of(i * STEP + LEAD, 8), STEP)] = pltpu.roll(value, lead_lanes, 1)
        return 0

    lax.fori_loop(0, FLAT_ROWS // STEP, stage, 0)
    extra_tmp[...] = jnp.zeros_like(extra_tmp)

    def partner(i):
        there = (dp + by_distance(i)) % N_DP
        return there, (there, y, x)

    def out_copies(i):
        there, device = partner(i)
        return (
            message(extra.at[there], arrived_extra.at[i], device, OUT_EXTRA, 0),
            message(canvas.at[0, there], arrived.at[0, i], device, OUT_0, 1),
            message(canvas.at[1, there], arrived.at[1, i], device, OUT_1, 2),
        )

    def place_part(o, _):
        there = (dp + o) % N_DP
        lane = lax.broadcasted_iota(jnp.int32, (MAIN, LANES), 1)
        lane2 = lax.broadcasted_iota(jnp.int32, (2, LANES), 1)
        start = LEAD - lead_rows + there * 4
        before = staged[pl.ds(start - 1, MAIN, stride=CHUNKS)]
        before2 = staged[pl.ds(start - 1 + MAIN * CHUNKS, 2, stride=CHUNKS)]
        for j in range(4):
            here = staged[pl.ds(start + j, MAIN, stride=CHUNKS)]
            here2 = staged[pl.ds(start + j + MAIN * CHUNKS, 2, stride=CHUNKS)]
            canvas[j // 2, there, :, pl.ds(j % 2 * LANES, LANES)] = jnp.where(lane >= lead_lanes, here, before).astype(jnp.bfloat16)
            extra_tmp[pl.ds(j * 2, 2)] = jnp.where(lane2 >= lead_lanes, here2, before2)
            before, before2 = here, here2
        extra[there] = extra_tmp[...].astype(jnp.bfloat16)
        return 0

    lax.fori_loop(1, N_DP + 1, place_part, 0)
    pl.semaphore_wait(barrier, 4 + N_DP - 1)

    def send_out(i, _):
        for copy in out_copies(i)[:2]:
            copy.start()
        return 0

    def send_out_more(i, _):
        out_copies(i)[2].start()
        return 0

    lax.fori_loop(0, PEERS, send_out, 0)
    lax.fori_loop(0, PEERS, send_out_more, 0)
    for h in range(2):
        arrived[h, PEERS] = canvas[h, dp]
    arrived_extra[PEERS] = extra[dp]

    def targets(length, width, offset, shape, dim, slot_of):
        k = lax.broadcasted_iota(jnp.int32, shape, dim)
        found = jnp.full(shape, -1, jnp.int32)
        for d in range(N_DP):
            inside = k // width == slot_of(d)
            found = jnp.where(inside, first_rows[d] + k % width + offset, found)
        return k, found

    def arrival_slot(d):
        ahead = (dp - d + N_DP) % N_DP - N_DP // 2
        return jnp.where(ahead >= 0, 2 * ahead, -2 * ahead - 1)

    k, row_of = targets(N_DP * MAIN, MAIN, 0, (1, N_DP * MAIN), 1, arrival_slot)
    pick = (lax.broadcasted_iota(jnp.int32, (GROUP_ROWS, N_DP * MAIN), 0) == row_of).astype(jnp.float32).astype(jnp.bfloat16)
    ke, row_e = targets(N_DP * EXTRA, EXTRA, MAIN, (1, N_DP * EXTRA), 1, arrival_slot)
    ke = ke % EXTRA

    def land(h):
        remote = pl.ds(0, PEERS)
        if h == 0:
            all_received(arrived_extra.at[remote], 0)
        all_received(arrived.at[h, remote], 1 + h)
        value = jnp.dot(pick, arrived[h].reshape(N_DP * MAIN, HALF_SLAB), preferred_element_type=jnp.float32)
        late = arrived_extra[...].reshape(N_DP * EXTRA, LANES)
        parts = []
        for j in (2 * h, 2 * h + 1):
            row_j = jnp.where(ke // 2 == j, row_e - 2 * j, -1)
            pick_j = (lax.broadcasted_iota(jnp.int32, (GROUP_ROWS, N_DP * EXTRA), 0) == row_j).astype(jnp.float32).astype(jnp.bfloat16)
            parts.append(jnp.dot(pick_j, late, preferred_element_type=jnp.float32))
        value = (value + jnp.concatenate(parts, axis=1)).astype(jnp.bfloat16)
        x_ref[:, halves[h]] = value
        xr[h, x, group_rows] = value
        xs[h, y] = value

    halves = (pl.ds(0, HALF_SLAB), pl.ds(HALF_SLAB, HALF_SLAB))
    group_rows = pl.ds(0, GROUP_ROWS)
    pad = pl.ds(GROUP_ROWS, PANEL - GROUP_ROWS)
    for q in range(RING):
        for h in range(2):
            xr[h, q, pad] = jnp.zeros((PANEL - GROUP_ROWS, HALF_SLAB), jnp.bfloat16)
    for p in range(2):
        to_sib[p, pad] = jnp.zeros((PANEL - GROUP_ROWS, BLOCK), jnp.bfloat16)
        own_f32[p, pad] = jnp.zeros((PANEL - GROUP_ROWS, BLOCK), jnp.float32)

    def gram(core, h, store):
        def tile(i, _):
            rows = pl.ds(pl.multiple_of((i % 2) * HALF_ROWS, 16), HALF_ROWS)
            value = lax.dot_general(
                xr[h, 2 * core + i // 2, rows], xs[h].reshape(BLOCK, HALF_SLAB),
                (((1,), (1,)), ((), ())), preferred_element_type=jnp.float32,
            )
            store(i // 2, rows, value)
            return 0

        lax.fori_loop(0, 4, tile, 0)

    def keep_own(p, rows, value):
        own_f32[p, rows] = value

    def keep_sib(p, rows, value):
        sib_f32[p, rows] = value

    def add_own(p, rows, value):
        own_f32[p, rows] += value

    def add_sib(p, rows, value):
        to_sib[p, rows] = (sib_f32[p, rows] + value).astype(jnp.bfloat16)

    land(0)
    a0 = gather_start("col", xr.at[0], X_R0)
    b0 = gather_start("row", xs.at[0], X_S0)
    land(1)
    a1 = gather_start("col", xr.at[1], X_R1)
    b1 = gather_start("row", xs.at[1], X_S1)
    a0 = gather_pass("col", xr.at[0], a0, X_R0)
    b0 = gather_pass("row", xs.at[0], b0, X_S0)
    a1 = gather_pass("col", xr.at[1], a1, X_R1)
    b1 = gather_pass("row", xs.at[1], b1, X_S1)
    gather_end(a0 + b0)
    gram(1 - c, 0, keep_sib)
    gram(c, 0, keep_own)
    gather_end(a1 + b1)
    gram(1 - c, 1, add_sib)

    def shard_rows(s):
        return pl.ds(pl.multiple_of(((s + N_Z) % N_Z) * SHARD, 16), SHARD)

    f32 = jnp.float32
    plan = []
    for k in range(8):
        distance = 4 - (k + 1) // 2
        plan.append((True, k % 2, distance))
        plan.append((False, 1 - k % 2, distance))
    sib_in = []
    for upward, panel, distance in plan:
        rows = shard_rows(z + distance if upward else z - distance)
        sib_in.append(send(to_sib.at[panel, rows], from_sib.at[panel, rows], dev_sib, TO_SIB))
    gram(c, 1, add_own)

    up_in, down_in = [], []
    for (upward, panel, distance), arrival in zip(plan, sib_in):
        rows = shard_rows(z + distance if upward else z - distance)
        arrival.wait_recv()
        term = own_f32[panel, rows] + from_sib[panel, rows].astype(f32)
        if distance == 0:
            up, down = (6, 5) if panel == 0 else (5, 6)
            up_in[up].wait_recv()
            down_in[down].wait_recv()
            term = term + ring_f[up].astype(f32) + ring_b[down].astype(f32)
            g_full[2 * c + panel, rows] = term.astype(jnp.bfloat16)
            continue
        arrivals, ring, device = (up_in, ring_f, dev_up) if upward else (down_in, ring_b, dev_down)
        k = len(arrivals)
        if k < 2:
            src = gh.at[2 * k + int(upward)]
        else:
            arrivals[k - 2].wait_recv()
            src = ring.at[k - 2]
            term = term + ring[k - 2].astype(f32)
        src[...] = term.astype(jnp.bfloat16)
        arrivals.append(send(src, ring.at[k], device, RING_UP if upward else RING_DOWN))
    mine = shard_rows(z)

    sib_slots = {shift: new_slot() for shift in (0, -1, 1, -2, 2, -3, 3, 4)}

    def relay(panel, rows, device, group, slot=None):
        ref = g_full.at[2 * c + panel, rows]
        return send(ref, ref, device, group, slot)

    y_slots = [new_slot() for _ in range(N_Z)]
    y_left, y_right = new_slot(), new_slot()
    order = (0, -1, 1, -2, 2, -3, 3, 4)

    def multiply(shift):
        i, rows = order.index(shift), shard_rows(z + shift)
        all_received(g_full.at[pl.ds(2 * (1 - c), 2), rows], sib_slots[shift])
        left = g_full[:, rows, :].reshape(RING * SHARD, BLOCK)
        for h in range(2):
            value = jnp.dot(left, xs[h].reshape(BLOCK, HALF_SLAB), preferred_element_type=f32)
            y_tmp[:, :, halves[h]] = value.reshape(RING, SHARD, HALF_SLAB)
        y_out[i] = y_tmp[...].astype(jnp.bfloat16)
        for o in (2, 1, 3):
            there = (x + o) % RING
            send(y_out.at[i, there], y_in.at[i, o - 1], (dp, y, there), Y_SUM, y_slots[i])
        y_own[i] = y_tmp[x]

    def add_up(shift):
        i, rows = order.index(shift), shard_rows(z + shift)
        all_received(y_in.at[i], y_slots[i])
        value = y_own[i] + y_in[i, 0].astype(f32) + y_in[i, 1].astype(f32) + y_in[i, 2].astype(f32)
        y_f32[rows] = value
        ya[y, rows] = value[:, :HALF_SLAB].astype(jnp.bfloat16)
        yb[x, rows] = value[:, HALF_SLAB:].astype(jnp.bfloat16)
        for o in (2, 1, 3):
            send(ya.at[y, rows], ya.at[y, rows], (dp, (y + o) % RING, x), Y_GATHER, y_left)
            send(yb.at[x, rows], yb.at[x, rows], (dp, y, (x + o) % RING), Y_GATHER, y_right)

    up_in, down_in = [], []
    for k in range(9):
        back_by = k // 2
        up_part, down_part = (k % 2, shard_rows(z - back_by)), (1 - k % 2, shard_rows(z + back_by))
        if k >= 2:
            up_in[k - 2].wait_recv()
        if k < 7:
            up_in.append(relay(*up_part, dev_up, G_UP))
        if k >= 2:
            down_in[k - 2].wait_recv()
        if k < 7:
            down_in.append(relay(*down_part, dev_down, G_DOWN))
        relay(*up_part, dev_sib, G_SIB, sib_slots[4 if k == 8 else -back_by])
        if k >= 2:
            relay(*down_part, dev_sib, G_SIB, sib_slots[back_by])
        for shift in {1: (0,), 3: (-1, 1), 5: (-2, 2), 7: (-3, 3), 8: (4,)}.get(k, ()):
            multiply(shift)
        for shift in {3: (0,), 6: (-1, 1), 8: (-2, 2, -3, 3, 4)}.get(k, ()):
            add_up(shift)

    def reduce_start(axis, buf, a_ref, b_ref, group):
        p = place[axis]
        right, left = near[axis]
        far = (p + 2) % RING
        return (send(buf.at[far, top], a_ref, right, group), send(buf.at[far, bottom], b_ref, left, group))

    def reduce_near(axis, buf, c_ref, d_ref, group):
        p = place[axis]
        right, left = near[axis]
        after, before = (p + 1) % RING, (p + 3) % RING
        return (
            send(buf.at[after, bottom], c_ref.at[bottom], right, group),
            send(buf.at[before, top], d_ref.at[top], left, group),
        )

    def reduce_pass(axis, buf, a_ref, b_ref, c_ref, d_ref, state, group):
        p = place[axis]
        right, left = near[axis]
        after, before = (p + 1) % RING, (p + 3) % RING
        state[0].wait_recv()
        buf[after, top] = (buf[after, top].astype(f32) + a_ref[...].astype(f32)).astype(jnp.bfloat16)
        c2 = send(buf.at[after, top], c_ref.at[top], right, group)
        state[1].wait_recv()
        buf[before, bottom] = (buf[before, bottom].astype(f32) + b_ref[...].astype(f32)).astype(jnp.bfloat16)
        d2 = send(buf.at[before, bottom], d_ref.at[bottom], left, group)
        return (c2, d2)

    first, second = pl.ds(0, HALF_SLAB), pl.ds(HALF_SLAB, HALF_SLAB)
    slots_a, slots_b = [[r.at[i] for r in (got_a, got_b, got_c, got_d)] for i in range(2)]
    far, after, before = (x + 2) % RING, (x + 1) % RING, (x + 3) % RING

    def times(q, right):
        return jnp.dot(g_full[q, group_rows], right, preferred_element_type=f32)

    def open_a(buf, right, slots):
        buf[far] = times(far, right()).astype(jnp.bfloat16)
        state = reduce_start("col", buf, *slots[:2], Z_A)
        buf[after] = times(after, right()).astype(jnp.bfloat16)
        buf[before] = times(before, right()).astype(jnp.bfloat16)
        near_copies = reduce_near("col", buf, *slots[2:], Z_A)
        return state, near_copies

    def open_b(buf, right, slots):
        def columns(j, _):
            cols = pl.ds(pl.multiple_of(j * LANES, LANES), LANES)
            z_b[cols] = lax.dot_general(
                g_full[:, :, cols].reshape(RING * PANEL, LANES), right, (((0,), (0,)), ((), ())),
                preferred_element_type=f32,
            )
            return 0

        lax.fori_loop(0, BLOCK // LANES, columns, 0)
        buf[...] = z_b[...].astype(jnp.bfloat16).reshape(RING, GROUP_ROWS, HALF_SLAB)
        state = reduce_start("row", buf, *slots[:2], Z_B)
        return state, reduce_near("row", buf, *slots[2:], Z_B)

    def pass_on(axis, buf, slots, opened):
        return opened[1] + reduce_pass(axis, buf, *slots, opened[0], Z_A if axis == "col" else Z_B)

    def close(tail, slots, total, cols):
        gather_end(tail)
        total[:, cols] = total[:, cols] + slots[2][...].astype(f32) + slots[3][...].astype(f32)

    def own_b(total):
        total[:, second] = z_b[pl.ds(pl.multiple_of(y * GROUP_ROWS, 8), GROUP_ROWS)]

    three = pl.ds(0, RING - 1)
    all_received(ya.at[three], y_left)
    oa = open_a(part.at[0], lambda: ya[:, :GROUP_ROWS].reshape(BLOCK, HALF_SLAB), slots_a)
    all_received(yb.at[three], y_right)
    ob = open_b(part.at[1], yb[...].reshape(RING * PANEL, HALF_SLAB), slots_b)
    z_f32[:, first] = times(x, ya[:, :GROUP_ROWS].reshape(BLOCK, HALF_SLAB))
    own_b(z_f32)
    oa = pass_on("col", part.at[0], slots_a, oa)
    ob = pass_on("row", part.at[1], slots_b, ob)

    _, row_of = targets(N_DP * MAIN, MAIN, 0, (N_DP * MAIN, 1), 0, lambda d: d)
    pick = (lax.broadcasted_iota(jnp.int32, (N_DP * MAIN, GROUP_ROWS), 1) == row_of).astype(f32).astype(jnp.bfloat16)
    ke, row_e = targets(N_DP * EXTRA, EXTRA, MAIN, (N_DP * EXTRA, 1), 0, lambda d: d)
    ke = ke % EXTRA
    late_picks = []
    for j in range(4):
        row_j = jnp.where(ke // 2 == j, row_e - 2 * j, -1)
        pick_j = lax.broadcasted_iota(jnp.int32, (N_DP * EXTRA, GROUP_ROWS), 1) == row_j
        late_picks.append(pick_j.astype(f32).astype(jnp.bfloat16))

    def back_copies(i):
        there, device = partner(i)
        group = i // BACK_GROUP
        return (
            message(outgoing.at[0, there], returned.at[0, i], device, BACK_0, 3 + group),
            message(outgoing.at[1, there], returned.at[1, i], device, BACK_1, 6 + group),
            message(outgoing_extra.at[there], returned_extra.at[i], device, BACK_EXTRA, 9),
        )

    def send_back(n):
        def step(i, _):
            back_copies(i)[n].start()
            return 0

        lax.fori_loop(0, PEERS, step, 0)

    def late_rows(h):
        return sum(
            jnp.dot(late_picks[j], update[:, j * LANES : (j + 1) * LANES], preferred_element_type=f32)
            for j in (2 * h, 2 * h + 1)
        )

    def leave(h, cols):
        update[:, cols] = (
            SCALE * (LINEAR_COEF * x_ref[:, cols].astype(f32) + (CUBIC_COEF * y_f32[group_rows, cols] + QUINTIC_COEF * z_f32[:, cols]))
        ).astype(jnp.bfloat16)
        outgoing[h] = (
            jnp.dot(pick, update[:, cols], preferred_element_type=f32).astype(jnp.bfloat16).reshape(N_DP, MAIN, HALF_SLAB)
        )
        send_back(h)
        returned[h, PEERS] = outgoing[h, dp]

    close(oa, slots_a, z_f32, first)
    leave(0, first)
    late = late_rows(0)
    close(ob, slots_b, z_f32, second)
    leave(1, second)
    outgoing_extra[...] = (late + late_rows(1)).astype(jnp.bfloat16).reshape(N_DP, EXTRA, LANES)
    send_back(2)
    returned_extra[PEERS] = outgoing_extra[dp]

    turn = (LANES - lead_lanes) % LANES

    def unpack(h, i):
        d = (dp - by_distance(i) + N_DP) % N_DP
        for j in range(2):
            back[pl.ds(d * 4 + 2 * h + j, MAIN, stride=CHUNKS)] = pltpu.roll(
                returned[h, i, :, pl.ds(j * LANES, LANES)].astype(f32), turn, 1)

    def unpack_late(i, _):
        d = (dp - by_distance(i) + N_DP) % N_DP
        extra_tmp[...] = pltpu.roll(returned_extra[i].astype(f32), turn, 1)
        for j in range(4):
            back[pl.ds(d * 4 + j + MAIN * CHUNKS, 2, stride=CHUNKS)] = extra_tmp[2 * j : 2 * j + 2]
        return 0

    def unpack_step(h):
        def step(i, _):
            unpack(h, i)
            return 0

        return step

    back[pl.ds(34 * CHUNKS, 8)] = jnp.zeros((8, LANES), f32)
    for h in range(2):
        unpack(h, jnp.int32(PEERS))
    for h in range(2):
        for group in range(3):
            all_received(returned.at[h, pl.ds(group * BACK_GROUP, BACK_GROUP)], 3 + 3 * h + group)
            lax.fori_loop(group * BACK_GROUP, (group + 1) * BACK_GROUP, unpack_step(h), 0)
    all_received(returned_extra.at[pl.ds(0, PEERS)], 9)
    lax.fori_loop(0, N_DP, unpack_late, 0)

    def finish(i, _):
        here = back[pl.ds(i * STEP + lead_rows, STEP)]
        after_rows = back[pl.ds(i * STEP + lead_rows + 1, STEP)]
        lane = lax.broadcasted_iota(jnp.int32, (STEP, LANES), 1)
        value = jnp.where(lane + lead_lanes < LANES, here, after_rows)
        value = jnp.where(slots(i) < my_length, value, 0.0).reshape(1, STEP * LANES)
        out_ref[:, pl.ds(pl.multiple_of(i * STEP * LANES, LANES), STEP * LANES)] = value.astype(jnp.bfloat16)
        return 0

    lax.fori_loop(0, FLAT_ROWS // STEP, finish, 0)

    remote = pl.ds(0, PEERS)
    halves_of_three = xs.at[0, pl.ds(0, RING - 1)]
    for ref, groups in (
        (arrived.at[0, remote], (OUT_0, OUT_1, BACK_0, BACK_1)),
        (arrived_extra.at[remote], (OUT_EXTRA, BACK_EXTRA)),
        (halves_of_three, (X_R0, X_R1, X_S0, X_S1, Z_A, Z_B)),
        (to_sib, (TO_SIB, G_SIB)),
        (ring_f, (RING_UP, RING_DOWN, G_UP, G_DOWN)),
        (y_in, (Y_SUM, Y_GATHER)),
    ):
        for group in groups:
            all_sent(ref, group)


def hand_on_kernel(value_ref, out_ref, sem):
    copy = pltpu.make_async_copy(value_ref, out_ref, sem)
    copy.start()
    copy.wait()


def newton_schulz(lengths, flat):
    bf, f32 = jnp.bfloat16, jnp.float32
    vmem = pltpu.VMEM
    value = pl.pallas_call(
        core_kernel,
        out_shape=jax.ShapeDtypeStruct((1, FLAT_ROWS * LANES), bf),
        in_specs=[pl.BlockSpec(memory_space=pltpu.SMEM), pl.BlockSpec(memory_space=pltpu.VMEM)],
        out_specs=pl.BlockSpec(memory_space=pltpu.VMEM),
        scratch_shapes=[
            vmem((LEAD + FLAT_ROWS + 88, LANES), f32),
            vmem((2, N_DP, MAIN, HALF_SLAB), bf),
            vmem((2, N_DP, MAIN, HALF_SLAB), bf),
            vmem((EXTRA, LANES), f32),
            vmem((N_DP, EXTRA, LANES), bf),
            vmem((2, N_DP, MAIN, HALF_SLAB), bf),
            vmem((N_DP, EXTRA, LANES), bf),
            vmem((GROUP_ROWS, SLAB), bf),
            vmem((2, RING, PANEL, HALF_SLAB), bf),
            vmem((2, RING, GROUP_ROWS, HALF_SLAB), bf),
            vmem((2, PANEL, BLOCK), f32),
            vmem((2, PANEL, BLOCK), f32),
            vmem((2, PANEL, BLOCK), bf),
            vmem((2, PANEL, BLOCK), bf),
            vmem((4, SHARD, BLOCK), bf),
            vmem((7, SHARD, BLOCK), bf),
            vmem((7, SHARD, BLOCK), bf),
            vmem((RING, PANEL, BLOCK), bf),
            vmem((2, RING, GROUP_ROWS, HALF_SLAB), bf),
            vmem((2, HALF_ROWS, HALF_SLAB), bf),
            vmem((2, HALF_ROWS, HALF_SLAB), bf),
            vmem((2, GROUP_ROWS, HALF_SLAB), bf),
            vmem((2, GROUP_ROWS, HALF_SLAB), bf),
            vmem((PANEL, SLAB), f32),
            vmem((RING, PANEL, HALF_SLAB), bf),
            vmem((RING, PANEL, HALF_SLAB), bf),
            vmem((RING, SHARD, SLAB), f32),
            vmem((N_Z, RING, SHARD, SLAB), bf),
            vmem((N_Z, RING - 1, SHARD, SLAB), bf),
            vmem((N_Z, SHARD, SLAB), f32),
            vmem((BLOCK, HALF_SLAB), f32),
            vmem((GROUP_ROWS, SLAB), f32),
            vmem((GROUP_ROWS, SLAB), bf),
            vmem((N_DP, EXTRA, LANES), bf),
            vmem((2, N_DP, MAIN, HALF_SLAB), bf),
            vmem((N_DP, EXTRA, LANES), bf),
            vmem((34 * CHUNKS + 8, LANES), f32),
            pltpu.SemaphoreType.DMA((N_SENT,)),
            pltpu.SemaphoreType.DMA((N_RECEIVED,)),
        ],
        compiler_params=pltpu.CompilerParams(
            collective_id=0, has_side_effects=True, vmem_limit_bytes=56 * 1024 * 1024
        ),
    )(lengths, flat)
    return pl.pallas_call(
        hand_on_kernel,
        out_shape=jax.ShapeDtypeStruct((1, FLAT_ROWS * LANES), bf),
        in_specs=[pl.BlockSpec(memory_space=pl.ANY)],
        out_specs=pl.BlockSpec(memory_space=pl.ANY),
        scratch_shapes=[pltpu.SemaphoreType.DMA],
        compiler_params=pltpu.CompilerParams(vmem_limit_bytes=60 * 1024 * 1024),
    )(value)


def local(flat_iterate, lengths):
    return newton_schulz(lengths, flat_iterate)


def solution(mesh):
    return jax.shard_map(
        local,
        mesh=mesh,
        in_specs=(P(("dp", "row", "col"), None), P()),
        out_specs=P(("dp", "row", "col"), None),
        check_vma=False,
    )
```

```python
import math

import jax
import jax.numpy as jnp
from jax import lax
from jax.experimental import pallas as pl
from jax.experimental.pallas import tpu as pltpu
from jax.sharding import PartitionSpec as P

COLS = 8192
ROWS = 5632


LINEAR_COEF = 3.4445
CUBIC_COEF = -4.775
QUINTIC_COEF = 2.0315

N_DP = 16
N_Z = 8
RING = 4
GROUP_ROWS = 352
HALF_ROWS = 176
SLAB = 512
BLOCK = 1408
CORE_ROWS = 704
SHARD = 48
PANEL = N_Z * SHARD
HALF_SLAB = SLAB // 2
LANES = 128
CHUNKS = COLS // LANES
FLAT_ROWS = 2112
MAIN = 32
EXTRA = 16
LEAD = 72
STEP = 176
PEERS = N_DP - 1
BACK_GROUP = 5
(
    OUT_0, OUT_1, OUT_EXTRA, BACK_0, BACK_1, BACK_EXTRA, X_R0, X_R1, X_S0, X_S1,
    TO_SIB, RING_UP, RING_DOWN, G_UP, G_DOWN, G_SIB, Y_SUM, Y_GATHER, Z_A, Z_B, N_SENT,
) = range(21)
N_RECEIVED = 128
MESH = pl.DeviceIdType.MESH
SCALE = 0.2 * math.sqrt(max(ROWS, COLS))


def slots(i):
    return (
        i * (STEP * LANES)
        + lax.broadcasted_iota(jnp.int32, (STEP, LANES), 0) * LANES
        + lax.broadcasted_iota(jnp.int32, (STEP, LANES), 1)
    )


def core_kernel(
    lengths_ref, flat_ref, out_ref, staged, canvas, outgoing, extra_tmp, extra, arrived, arrived_extra, x_ref, xr, xs, own_f32, sib_f32, to_sib, from_sib, gh, ring_f, ring_b, g_full,
    part, got_a, got_b, got_c, got_d, y_f32, ya, yb, y_tmp, y_out, y_in, y_own, z_b, z_f32, update, outgoing_extra, returned, returned_extra, back, send_sem, recv_sem,
):
    dp = lax.axis_index("dp")
    y = lax.axis_index("row")
    x = lax.axis_index("col")
    z, c = dp // 2, dp % 2
    sib_dp = z * 2 + 1 - c
    up_dp = ((z + 1) % N_Z) * 2 + c
    down_dp = ((z + 7) % N_Z) * 2 + c
    dev_sib = (sib_dp, y, x)
    dev_up = (up_dp, y, x)
    dev_down = (down_dp, y, x)
    near = {
        "col": ((dp, y, (x + 1) % RING), (dp, y, (x + 3) % RING)),
        "row": ((dp, (y + 1) % RING, x), (dp, (y + 3) % RING, x)),
    }
    place = {"col": x, "row": y}

    barrier = pltpu.get_barrier_semaphore()
    for peer in near["col"] + near["row"]:
        pl.semaphore_signal(barrier, inc=1, device_id=peer, device_id_type=MESH)

    def greet(o, _):
        pl.semaphore_signal(barrier, inc=1, device_id=((dp + o) % N_DP, y, x), device_id_type=MESH)
        return 0

    lax.fori_loop(1, N_DP, greet, 0)

    def by_distance(i):
        return N_DP // 2 + (i + 1) // 2 * (1 - 2 * (i % 2))

    counter = [10]

    def message(src, dst, device, group, slot):
        return pltpu.make_async_remote_copy(
            src_ref=src, dst_ref=dst, send_sem=send_sem.at[group], recv_sem=recv_sem.at[slot],
            device_id=device, device_id_type=MESH,
        )

    def new_slot():
        counter[0] += 1
        return counter[0] - 1

    def send(src, dst, device, group, slot=None):
        copy = message(src, dst, device, group, new_slot() if slot is None else slot)
        copy.start()
        return copy

    def all_sent(ref, group):
        message(ref, ref, dev_sib, group, 0).wait_send()

    def all_received(ref, slot):
        message(ref, ref, dev_sib, 0, slot).wait_recv()

    top, bottom = pl.ds(0, HALF_ROWS), pl.ds(HALF_ROWS, HALF_ROWS)

    def gather_start(axis, buf, group):
        p = place[axis]
        right, left = near[axis]
        a = [send(buf.at[p, h], buf.at[p, h], right, group) for h in (top, bottom)]
        b = [send(buf.at[p, h], buf.at[p, h], left, group) for h in (bottom, top)]
        return a, b

    def gather_pass(axis, buf, state, group):
        p = place[axis]
        right, left = near[axis]
        a, b = state
        before, after = (p + 3) % RING, (p + 1) % RING
        a[0].wait_recv()
        f = send(buf.at[before, top], buf.at[before, top], right, group)
        b[0].wait_recv()
        g = send(buf.at[after, bottom], buf.at[after, bottom], left, group)
        return a[1], b[1], f, g

    def gather_end(tail):
        for copy in tail:
            copy.wait_recv()

    group = y * RING + x
    my_start = jnp.int32(0)
    begin = jnp.int32(0)
    first_rows = []
    for d in range(N_DP):
        first_rows.append(begin // COLS)
        my_start = jnp.where(dp == d, begin, my_start)
        begin = begin + lengths_ref[group, d]
    my_length = lengths_ref[group, dp]
    lead = my_start % COLS
    lead_rows, lead_lanes = lead // LANES, lead % LANES
    staged[pl.ds(0, LEAD)] = jnp.zeros((LEAD, LANES), jnp.float32)
    tail_rows = staged.shape[0] - LEAD - FLAT_ROWS
    staged[pl.ds(LEAD + FLAT_ROWS, tail_rows)] = jnp.zeros((tail_rows, LANES), jnp.float32)

    def stage(i, _):
        value = flat_ref[:, pl.ds(pl.multiple_of(i * STEP * LANES, LANES), STEP * LANES)].astype(jnp.float32).reshape(STEP, LANES)
        value = jnp.where(slots(i) < my_length, value, 0.0)
        staged[pl.ds(pl.multiple_of(i * STEP + LEAD, 8), STEP)] = pltpu.roll(value, lead_lanes, 1)
        return 0

    lax.fori_loop(0, FLAT_ROWS // STEP, stage, 0)
    extra_tmp[...] = jnp.zeros_like(extra_tmp)

    def partner(i):
        there = (dp + by_distance(i)) % N_DP
        return there, (there, y, x)

    def out_copies(i):
        there, device = partner(i)
        return (
            message(extra.at[there], arrived_extra.at[i], device, OUT_EXTRA, 0),
            message(canvas.at[0, there], arrived.at[0, i], device, OUT_0, 1),
            message(canvas.at[1, there], arrived.at[1, i], device, OUT_1, 2),
        )

    def place_part(o, _):
        there = (dp + o) % N_DP
        lane = lax.broadcasted_iota(jnp.int32, (MAIN, LANES), 1)
        lane2 = lax.broadcasted_iota(jnp.int32, (2, LANES), 1)
        start = LEAD - lead_rows + there * 4
        before = staged[pl.ds(start - 1, MAIN, stride=CHUNKS)]
        before2 = staged[pl.ds(start - 1 + MAIN * CHUNKS, 2, stride=CHUNKS)]
        for j in range(4):
            here = staged[pl.ds(start + j, MAIN, stride=CHUNKS)]
            here2 = staged[pl.ds(start + j + MAIN * CHUNKS, 2, stride=CHUNKS)]
            canvas[j // 2, there, :, pl.ds(j % 2 * LANES, LANES)] = jnp.where(lane >= lead_lanes, here, before).astype(jnp.bfloat16)
            extra_tmp[pl.ds(j * 2, 2)] = jnp.where(lane2 >= lead_lanes, here2, before2)
            before, before2 = here, here2
        extra[there] = extra_tmp[...].astype(jnp.bfloat16)
        return 0

    lax.fori_loop(1, N_DP + 1, place_part, 0)
    pl.semaphore_wait(barrier, 4 + N_DP - 1)

    def send_out(i, _):
        for copy in out_copies(i)[:2]:
            copy.start()
        return 0

    def send_out_more(i, _):
        out_copies(i)[2].start()
        return 0

    lax.fori_loop(0, PEERS, send_out, 0)
    lax.fori_loop(0, PEERS, send_out_more, 0)
    for h in range(2):
        arrived[h, PEERS] = canvas[h, dp]
    arrived_extra[PEERS] = extra[dp]

    def targets(length, width, offset, shape, dim, slot_of):
        k = lax.broadcasted_iota(jnp.int32, shape, dim)
        found = jnp.full(shape, -1, jnp.int32)
        for d in range(N_DP):
            inside = k // width == slot_of(d)
            found = jnp.where(inside, first_rows[d] + k % width + offset, found)
        return k, found

    def arrival_slot(d):
        ahead = (dp - d + N_DP) % N_DP - N_DP // 2
        return jnp.where(ahead >= 0, 2 * ahead, -2 * ahead - 1)

    k, row_of = targets(N_DP * MAIN, MAIN, 0, (1, N_DP * MAIN), 1, arrival_slot)
    pick = (lax.broadcasted_iota(jnp.int32, (GROUP_ROWS, N_DP * MAIN), 0) == row_of).astype(jnp.float32).astype(jnp.bfloat16)
    ke, row_e = targets(N_DP * EXTRA, EXTRA, MAIN, (1, N_DP * EXTRA), 1, arrival_slot)
    ke = ke % EXTRA

    def land(h):
        remote = pl.ds(0, PEERS)
        if h == 0:
            all_received(arrived_extra.at[remote], 0)
        all_received(arrived.at[h, remote], 1 + h)
        value = jnp.dot(pick, arrived[h].reshape(N_DP * MAIN, HALF_SLAB), preferred_element_type=jnp.float32)
        late = arrived_extra[...].reshape(N_DP * EXTRA, LANES)
        parts = []
        for j in (2 * h, 2 * h + 1):
            row_j = jnp.where(ke // 2 == j, row_e - 2 * j, -1)
            pick_j = (lax.broadcasted_iota(jnp.int32, (GROUP_ROWS, N_DP * EXTRA), 0) == row_j).astype(jnp.float32).astype(jnp.bfloat16)
            parts.append(jnp.dot(pick_j, late, preferred_element_type=jnp.float32))
        value = (value + jnp.concatenate(parts, axis=1)).astype(jnp.bfloat16)
        x_ref[:, halves[h]] = value
        xr[h, x, group_rows] = value
        xs[h, y] = value

    halves = (pl.ds(0, HALF_SLAB), pl.ds(HALF_SLAB, HALF_SLAB))
    group_rows = pl.ds(0, GROUP_ROWS)
    pad = pl.ds(GROUP_ROWS, PANEL - GROUP_ROWS)
    for q in range(RING):
        for h in range(2):
            xr[h, q, pad] = jnp.zeros((PANEL - GROUP_ROWS, HALF_SLAB), jnp.bfloat16)
    for p in range(2):
        to_sib[p, pad] = jnp.zeros((PANEL - GROUP_ROWS, BLOCK), jnp.bfloat16)
        own_f32[p, pad] = jnp.zeros((PANEL - GROUP_ROWS, BLOCK), jnp.float32)

    def gram(core, h, store):
        def tile(i, _):
            rows = pl.ds(pl.multiple_of((i % 2) * HALF_ROWS, 16), HALF_ROWS)
            value = lax.dot_general(
                xr[h, 2 * core + i // 2, rows], xs[h].reshape(BLOCK, HALF_SLAB),
                (((1,), (1,)), ((), ())), preferred_element_type=jnp.float32,
            )
            store(i // 2, rows, value)
            return 0

        lax.fori_loop(0, 4, tile, 0)

    def keep_own(p, rows, value):
        own_f32[p, rows] = value

    def keep_sib(p, rows, value):
        sib_f32[p, rows] = value

    def add_own(p, rows, value):
        own_f32[p, rows] += value

    def add_sib(p, rows, value):
        to_sib[p, rows] = (sib_f32[p, rows] + value).astype(jnp.bfloat16)

    land(0)
    a0 = gather_start("col", xr.at[0], X_R0)
    b0 = gather_start("row", xs.at[0], X_S0)
    land(1)
    a1 = gather_start("col", xr.at[1], X_R1)
    b1 = gather_start("row", xs.at[1], X_S1)
    a0 = gather_pass("col", xr.at[0], a0, X_R0)
    b0 = gather_pass("row", xs.at[0], b0, X_S0)
    a1 = gather_pass("col", xr.at[1], a1, X_R1)
    b1 = gather_pass("row", xs.at[1], b1, X_S1)
    gather_end(a0 + b0)
    gram(1 - c, 0, keep_sib)
    gram(c, 0, keep_own)
    gather_end(a1 + b1)
    gram(1 - c, 1, add_sib)

    def shard_rows(s):
        return pl.ds(pl.multiple_of(((s + N_Z) % N_Z) * SHARD, 16), SHARD)

    f32 = jnp.float32
    plan = []
    for k in range(8):
        distance = 4 - (k + 1) // 2
        plan.append((True, k % 2, distance))
        plan.append((False, 1 - k % 2, distance))
    sib_in = []
    for upward, panel, distance in plan:
        rows = shard_rows(z + distance if upward else z - distance)
        sib_in.append(send(to_sib.at[panel, rows], from_sib.at[panel, rows], dev_sib, TO_SIB))
    gram(c, 1, add_own)

    up_in, down_in = [], []
    for (upward, panel, distance), arrival in zip(plan, sib_in):
        rows = shard_rows(z + distance if upward else z - distance)
        arrival.wait_recv()
        term = own_f32[panel, rows] + from_sib[panel, rows].astype(f32)
        if distance == 0:
            up, down = (6, 5) if panel == 0 else (5, 6)
            up_in[up].wait_recv()
            down_in[down].wait_recv()
            term = term + ring_f[up].astype(f32) + ring_b[down].astype(f32)
            g_full[2 * c + panel, rows] = term.astype(jnp.bfloat16)
            continue
        arrivals, ring, device = (up_in, ring_f, dev_up) if upward else (down_in, ring_b, dev_down)
        k = len(arrivals)
        if k < 2:
            src = gh.at[2 * k + int(upward)]
        else:
            arrivals[k - 2].wait_recv()
            src = ring.at[k - 2]
            term = term + ring[k - 2].astype(f32)
        src[...] = term.astype(jnp.bfloat16)
        arrivals.append(send(src, ring.at[k], device, RING_UP if upward else RING_DOWN))
    mine = shard_rows(z)

    sib_slots = {shift: new_slot() for shift in (0, -1, 1, -2, 2, -3, 3, 4)}

    def relay(panel, rows, device, group, slot=None):
        ref = g_full.at[2 * c + panel, rows]
        return send(ref, ref, device, group, slot)

    y_slots = [new_slot() for _ in range(N_Z)]
    y_left, y_right = new_slot(), new_slot()
    order = (0, -1, 1, -2, 2, -3, 3, 4)

    def multiply(shift):
        i, rows = order.index(shift), shard_rows(z + shift)
        all_received(g_full.at[pl.ds(2 * (1 - c), 2), rows], sib_slots[shift])
        left = g_full[:, rows, :].reshape(RING * SHARD, BLOCK)
        for h in range(2):
            value = jnp.dot(left, xs[h].reshape(BLOCK, HALF_SLAB), preferred_element_type=f32)
            y_tmp[:, :, halves[h]] = value.reshape(RING, SHARD, HALF_SLAB)
        y_out[i] = y_tmp[...].astype(jnp.bfloat16)
        for o in (2, 1, 3):
            there = (x + o) % RING
            send(y_out.at[i, there], y_in.at[i, o - 1], (dp, y, there), Y_SUM, y_slots[i])
        y_own[i] = y_tmp[x]

    def add_up(shift):
        i, rows = order.index(shift), shard_rows(z + shift)
        all_received(y_in.at[i], y_slots[i])
        value = y_own[i] + y_in[i, 0].astype(f32) + y_in[i, 1].astype(f32) + y_in[i, 2].astype(f32)
        y_f32[rows] = value
        ya[y, rows] = value[:, :HALF_SLAB].astype(jnp.bfloat16)
        yb[x, rows] = value[:, HALF_SLAB:].astype(jnp.bfloat16)
        for o in (2, 1, 3):
            send(ya.at[y, rows], ya.at[y, rows], (dp, (y + o) % RING, x), Y_GATHER, y_left)
            send(yb.at[x, rows], yb.at[x, rows], (dp, y, (x + o) % RING), Y_GATHER, y_right)

    up_in, down_in = [], []
    for k in range(9):
        back_by = k // 2
        up_part, down_part = (k % 2, shard_rows(z - back_by)), (1 - k % 2, shard_rows(z + back_by))
        if k >= 2:
            up_in[k - 2].wait_recv()
        if k < 7:
            up_in.append(relay(*up_part, dev_up, G_UP))
        if k >= 2:
            down_in[k - 2].wait_recv()
        if k < 7:
            down_in.append(relay(*down_part, dev_down, G_DOWN))
        relay(*up_part, dev_sib, G_SIB, sib_slots[4 if k == 8 else -back_by])
        if k >= 2:
            relay(*down_part, dev_sib, G_SIB, sib_slots[back_by])
        for shift in {1: (0,), 3: (-1, 1), 5: (-2, 2), 7: (-3, 3), 8: (4,)}.get(k, ()):
            multiply(shift)
        for shift in {3: (0,), 6: (-1, 1), 8: (-2, 2, -3, 3, 4)}.get(k, ()):
            add_up(shift)

    def reduce_start(axis, buf, a_ref, b_ref, group):
        p = place[axis]
        right, left = near[axis]
        far = (p + 2) % RING
        return (send(buf.at[far, top], a_ref, right, group), send(buf.at[far, bottom], b_ref, left, group))

    def reduce_near(axis, buf, c_ref, d_ref, group):
        p = place[axis]
        right, left = near[axis]
        after, before = (p + 1) % RING, (p + 3) % RING
        return (
            send(buf.at[after, bottom], c_ref.at[bottom], right, group),
            send(buf.at[before, top], d_ref.at[top], left, group),
        )

    def reduce_pass(axis, buf, a_ref, b_ref, c_ref, d_ref, state, group):
        p = place[axis]
        right, left = near[axis]
        after, before = (p + 1) % RING, (p + 3) % RING
        state[0].wait_recv()
        buf[after, top] = (buf[after, top].astype(f32) + a_ref[...].astype(f32)).astype(jnp.bfloat16)
        c2 = send(buf.at[after, top], c_ref.at[top], right, group)
        state[1].wait_recv()
        buf[before, bottom] = (buf[before, bottom].astype(f32) + b_ref[...].astype(f32)).astype(jnp.bfloat16)
        d2 = send(buf.at[before, bottom], d_ref.at[bottom], left, group)
        return (c2, d2)

    first, second = pl.ds(0, HALF_SLAB), pl.ds(HALF_SLAB, HALF_SLAB)
    slots_a, slots_b = [[r.at[i] for r in (got_a, got_b, got_c, got_d)] for i in range(2)]
    far, after, before = (x + 2) % RING, (x + 1) % RING, (x + 3) % RING

    def times(q, right):
        return jnp.dot(g_full[q, group_rows], right, preferred_element_type=f32)

    def open_a(buf, right, slots):
        buf[far] = times(far, right()).astype(jnp.bfloat16)
        state = reduce_start("col", buf, *slots[:2], Z_A)
        buf[after] = times(after, right()).astype(jnp.bfloat16)
        buf[before] = times(before, right()).astype(jnp.bfloat16)
        near_copies = reduce_near("col", buf, *slots[2:], Z_A)
        return state, near_copies

    def open_b(buf, right, slots):
        def columns(j, _):
            cols = pl.ds(pl.multiple_of(j * LANES, LANES), LANES)
            z_b[cols] = lax.dot_general(
                g_full[:, :, cols].reshape(RING * PANEL, LANES), right, (((0,), (0,)), ((), ())),
                preferred_element_type=f32,
            )
            return 0

        lax.fori_loop(0, BLOCK // LANES, columns, 0)
        buf[...] = z_b[...].astype(jnp.bfloat16).reshape(RING, GROUP_ROWS, HALF_SLAB)
        state = reduce_start("row", buf, *slots[:2], Z_B)
        return state, reduce_near("row", buf, *slots[2:], Z_B)

    def pass_on(axis, buf, slots, opened):
        return opened[1] + reduce_pass(axis, buf, *slots, opened[0], Z_A if axis == "col" else Z_B)

    def close(tail, slots, total, cols):
        gather_end(tail)
        total[:, cols] = total[:, cols] + slots[2][...].astype(f32) + slots[3][...].astype(f32)

    def own_b(total):
        total[:, second] = z_b[pl.ds(pl.multiple_of(y * GROUP_ROWS, 8), GROUP_ROWS)]

    three = pl.ds(0, RING - 1)
    all_received(ya.at[three], y_left)
    oa = open_a(part.at[0], lambda: ya[:, :GROUP_ROWS].reshape(BLOCK, HALF_SLAB), slots_a)
    all_received(yb.at[three], y_right)
    ob = open_b(part.at[1], yb[...].reshape(RING * PANEL, HALF_SLAB), slots_b)
    z_f32[:, first] = times(x, ya[:, :GROUP_ROWS].reshape(BLOCK, HALF_SLAB))
    own_b(z_f32)
    oa = pass_on("col", part.at[0], slots_a, oa)
    ob = pass_on("row", part.at[1], slots_b, ob)

    _, row_of = targets(N_DP * MAIN, MAIN, 0, (N_DP * MAIN, 1), 0, lambda d: d)
    pick = (lax.broadcasted_iota(jnp.int32, (N_DP * MAIN, GROUP_ROWS), 1) == row_of).astype(f32).astype(jnp.bfloat16)
    ke, row_e = targets(N_DP * EXTRA, EXTRA, MAIN, (N_DP * EXTRA, 1), 0, lambda d: d)
    ke = ke % EXTRA
    late_picks = []
    for j in range(4):
        row_j = jnp.where(ke // 2 == j, row_e - 2 * j, -1)
        pick_j = lax.broadcasted_iota(jnp.int32, (N_DP * EXTRA, GROUP_ROWS), 1) == row_j
        late_picks.append(pick_j.astype(f32).astype(jnp.bfloat16))

    def back_copies(i):
        there, device = partner(i)
        group = i // BACK_GROUP
        return (
            message(outgoing.at[0, there], returned.at[0, i], device, BACK_0, 3 + group),
            message(outgoing.at[1, there], returned.at[1, i], device, BACK_1, 6 + group),
            message(outgoing_extra.at[there], returned_extra.at[i], device, BACK_EXTRA, 9),
        )

    def send_back(n):
        def step(i, _):
            back_copies(i)[n].start()
            return 0

        lax.fori_loop(0, PEERS, step, 0)

    def late_rows(h):
        return sum(
            jnp.dot(late_picks[j], update[:, j * LANES : (j + 1) * LANES], preferred_element_type=f32)
            for j in (2 * h, 2 * h + 1)
        )

    def leave(h, cols):
        update[:, cols] = (
            SCALE * (LINEAR_COEF * x_ref[:, cols].astype(f32) + (CUBIC_COEF * y_f32[group_rows, cols] + QUINTIC_COEF * z_f32[:, cols]))
        ).astype(jnp.bfloat16)
        outgoing[h] = (
            jnp.dot(pick, update[:, cols], preferred_element_type=f32).astype(jnp.bfloat16).reshape(N_DP, MAIN, HALF_SLAB)
        )
        send_back(h)
        returned[h, PEERS] = outgoing[h, dp]

    close(oa, slots_a, z_f32, first)
    leave(0, first)
    late = late_rows(0)
    close(ob, slots_b, z_f32, second)
    leave(1, second)
    outgoing_extra[...] = (late + late_rows(1)).astype(jnp.bfloat16).reshape(N_DP, EXTRA, LANES)
    send_back(2)
    returned_extra[PEERS] = outgoing_extra[dp]

    turn = (LANES - lead_lanes) % LANES

    def unpack(h, i):
        d = (dp - by_distance(i) + N_DP) % N_DP
        for j in range(2):
            back[pl.ds(d * 4 + 2 * h + j, MAIN, stride=CHUNKS)] = pltpu.roll(
                returned[h, i, :, pl.ds(j * LANES, LANES)].astype(f32), turn, 1)

    def unpack_late(i, _):
        d = (dp - by_distance(i) + N_DP) % N_DP
        extra_tmp[...] = pltpu.roll(returned_extra[i].astype(f32), turn, 1)
        for j in range(4):
            back[pl.ds(d * 4 + j + MAIN * CHUNKS, 2, stride=CHUNKS)] = extra_tmp[2 * j : 2 * j + 2]
        return 0

    def unpack_step(h):
        def step(i, _):
            unpack(h, i)
            return 0

        return step

    back[pl.ds(34 * CHUNKS, 8)] = jnp.zeros((8, LANES), f32)
    for h in range(2):
        unpack(h, jnp.int32(PEERS))
    for h in range(2):
        for group in range(3):
            all_received(returned.at[h, pl.ds(group * BACK_GROUP, BACK_GROUP)], 3 + 3 * h + group)
            lax.fori_loop(group * BACK_GROUP, (group + 1) * BACK_GROUP, unpack_step(h), 0)
    all_received(returned_extra.at[pl.ds(0, PEERS)], 9)
    lax.fori_loop(0, N_DP, unpack_late, 0)

    def finish(i, _):
        here = back[pl.ds(i * STEP + lead_rows, STEP)]
        after_rows = back[pl.ds(i * STEP + lead_rows + 1, STEP)]
        lane = lax.broadcasted_iota(jnp.int32, (STEP, LANES), 1)
        value = jnp.where(lane + lead_lanes < LANES, here, after_rows)
        out_ref[pl.ds(pl.multiple_of(i * STEP, 8), STEP)] = jnp.where(slots(i) < my_length, value, 0.0)
        return 0

    lax.fori_loop(0, FLAT_ROWS // STEP, finish, 0)

    remote = pl.ds(0, PEERS)
    halves_of_three = xs.at[0, pl.ds(0, RING - 1)]
    for ref, groups in (
        (arrived.at[0, remote], (OUT_0, OUT_1, BACK_0, BACK_1)),
        (arrived_extra.at[remote], (OUT_EXTRA, BACK_EXTRA)),
        (halves_of_three, (X_R0, X_R1, X_S0, X_S1, Z_A, Z_B)),
        (to_sib, (TO_SIB, G_SIB)),
        (ring_f, (RING_UP, RING_DOWN, G_UP, G_DOWN)),
        (y_in, (Y_SUM, Y_GATHER)),
    ):
        for group in groups:
            all_sent(ref, group)


def flatten_kernel(value_ref, out_ref):
    def step(i, _):
        value = value_ref[pl.ds(pl.multiple_of(i * STEP, 8), STEP)].reshape(1, STEP * LANES)
        out_ref[:, pl.ds(pl.multiple_of(i * STEP * LANES, LANES), STEP * LANES)] = value.astype(jnp.bfloat16)
        return 0

    lax.fori_loop(0, FLAT_ROWS // STEP, step, 0)


def newton_schulz(lengths, flat):
    bf, f32 = jnp.bfloat16, jnp.float32
    vmem = pltpu.VMEM
    value = pl.pallas_call(
        core_kernel,
        out_shape=jax.ShapeDtypeStruct((FLAT_ROWS, LANES), f32),
        in_specs=[pl.BlockSpec(memory_space=pltpu.SMEM), pl.BlockSpec(memory_space=pltpu.VMEM)],
        out_specs=pl.BlockSpec(memory_space=pltpu.VMEM),
        scratch_shapes=[
            vmem((LEAD + FLAT_ROWS + 88, LANES), f32),
            vmem((2, N_DP, MAIN, HALF_SLAB), bf),
            vmem((2, N_DP, MAIN, HALF_SLAB), bf),
            vmem((EXTRA, LANES), f32),
            vmem((N_DP, EXTRA, LANES), bf),
            vmem((2, N_DP, MAIN, HALF_SLAB), bf),
            vmem((N_DP, EXTRA, LANES), bf),
            vmem((GROUP_ROWS, SLAB), bf),
            vmem((2, RING, PANEL, HALF_SLAB), bf),
            vmem((2, RING, GROUP_ROWS, HALF_SLAB), bf),
            vmem((2, PANEL, BLOCK), f32),
            vmem((2, PANEL, BLOCK), f32),
            vmem((2, PANEL, BLOCK), bf),
            vmem((2, PANEL, BLOCK), bf),
            vmem((4, SHARD, BLOCK), bf),
            vmem((7, SHARD, BLOCK), bf),
            vmem((7, SHARD, BLOCK), bf),
            vmem((RING, PANEL, BLOCK), bf),
            vmem((2, RING, GROUP_ROWS, HALF_SLAB), bf),
            vmem((2, HALF_ROWS, HALF_SLAB), bf),
            vmem((2, HALF_ROWS, HALF_SLAB), bf),
            vmem((2, GROUP_ROWS, HALF_SLAB), bf),
            vmem((2, GROUP_ROWS, HALF_SLAB), bf),
            vmem((PANEL, SLAB), f32),
            vmem((RING, PANEL, HALF_SLAB), bf),
            vmem((RING, PANEL, HALF_SLAB), bf),
            vmem((RING, SHARD, SLAB), f32),
            vmem((N_Z, RING, SHARD, SLAB), bf),
            vmem((N_Z, RING - 1, SHARD, SLAB), bf),
            vmem((N_Z, SHARD, SLAB), f32),
            vmem((BLOCK, HALF_SLAB), f32),
            vmem((GROUP_ROWS, SLAB), f32),
            vmem((GROUP_ROWS, SLAB), bf),
            vmem((N_DP, EXTRA, LANES), bf),
            vmem((2, N_DP, MAIN, HALF_SLAB), bf),
            vmem((N_DP, EXTRA, LANES), bf),
            vmem((34 * CHUNKS + 8, LANES), f32),
            pltpu.SemaphoreType.DMA((N_SENT,)),
            pltpu.SemaphoreType.DMA((N_RECEIVED,)),
        ],
        compiler_params=pltpu.CompilerParams(
            collective_id=0, has_side_effects=True, vmem_limit_bytes=56 * 1024 * 1024
        ),
    )(lengths, flat)
    return pl.pallas_call(
        flatten_kernel,
        out_shape=jax.ShapeDtypeStruct((1, FLAT_ROWS * LANES), bf),
        in_specs=[pl.BlockSpec(memory_space=pltpu.VMEM)],
        out_specs=pl.BlockSpec(memory_space=pltpu.VMEM),
        compiler_params=pltpu.CompilerParams(vmem_limit_bytes=56 * 1024 * 1024),
    )(value)


def local(flat_iterate, lengths):
    return newton_schulz(lengths, flat_iterate)


def solution(mesh):
    return jax.shard_map(
        local,
        mesh=mesh,
        in_specs=(P(("dp", "row", "col"), None), P()),
        out_specs=P(("dp", "row", "col"), None),
        check_vma=False,
    )
```

```python
import math

import jax
import jax.numpy as jnp
from jax import lax
from jax.experimental import pallas as pl
from jax.experimental.pallas import tpu as pltpu
from jax.sharding import PartitionSpec as P

COLS = 8192
ROWS = 5632


LINEAR_COEF = 3.4445
CUBIC_COEF = -4.775
QUINTIC_COEF = 2.0315

N_DP = 16
N_Z = 8
RING = 4
GROUP_ROWS = 352
HALF_ROWS = 176
SLAB = 512
BLOCK = 1408
CORE_ROWS = 704
SHARD = 48
PANEL = N_Z * SHARD
HALF_SLAB = SLAB // 2
LANES = 128
CHUNKS = COLS // LANES
FLAT_ROWS = 2112
MAIN = 32
EXTRA = 16
LEAD = 72
STEP = 176
PEERS = N_DP - 1
BACK_GROUP = 5
PARTS = SLAB // LANES
OUT, X_R, X_S = 0, PARTS, 2 * PARTS
(
    OUT_EXTRA, BACK_0, BACK_1, BACK_EXTRA, TO_SIB, RING_UP, RING_DOWN, G_UP, G_DOWN, G_SIB,
    Y_SUM, Y_GATHER, Z_A, Z_B, N_SENT,
) = range(3 * PARTS, 3 * PARTS + 15)
N_RECEIVED = 112
MESH = pl.DeviceIdType.MESH
SCALE = 0.2 * math.sqrt(max(ROWS, COLS))


def slots(i):
    return (
        i * (STEP * LANES)
        + lax.broadcasted_iota(jnp.int32, (STEP, LANES), 0) * LANES
        + lax.broadcasted_iota(jnp.int32, (STEP, LANES), 1)
    )


def core_kernel(
    lengths_ref, flat_ref, out_ref, staged, canvas, outgoing, extra_tmp, extra, arrived, arrived_extra, x_ref, xr, xs, own_f32, sib_f32, to_sib, from_sib, gh, ring_f, ring_b, g_full,
    part, got_a, got_b, got_c, got_d, y_f32, ya, yb, y_tmp, y_out, y_in, y_own, z_b, z_f32, update, outgoing_extra, returned, returned_extra, back, send_sem, recv_sem,
):
    dp = lax.axis_index("dp")
    y = lax.axis_index("row")
    x = lax.axis_index("col")
    z, c = dp // 2, dp % 2
    sib_dp = z * 2 + 1 - c
    up_dp = ((z + 1) % N_Z) * 2 + c
    down_dp = ((z + 7) % N_Z) * 2 + c
    dev_sib = (sib_dp, y, x)
    dev_up = (up_dp, y, x)
    dev_down = (down_dp, y, x)
    near = {
        "col": ((dp, y, (x + 1) % RING), (dp, y, (x + 3) % RING)),
        "row": ((dp, (y + 1) % RING, x), (dp, (y + 3) % RING, x)),
    }
    place = {"col": x, "row": y}

    barrier = pltpu.get_barrier_semaphore()
    for peer in near["col"] + near["row"]:
        pl.semaphore_signal(barrier, inc=1, device_id=peer, device_id_type=MESH)

    def greet(o, _):
        pl.semaphore_signal(barrier, inc=1, device_id=((dp + o) % N_DP, y, x), device_id_type=MESH)
        return 0

    lax.fori_loop(1, N_DP, greet, 0)

    def by_distance(i):
        return N_DP // 2 + (i + 1) // 2 * (1 - 2 * (i % 2))

    counter = [12]

    def message(src, dst, device, group, slot):
        return pltpu.make_async_remote_copy(
            src_ref=src, dst_ref=dst, send_sem=send_sem.at[group], recv_sem=recv_sem.at[slot],
            device_id=device, device_id_type=MESH,
        )

    def new_slot():
        counter[0] += 1
        return counter[0] - 1

    def send(src, dst, device, group, slot=None):
        copy = message(src, dst, device, group, new_slot() if slot is None else slot)
        copy.start()
        return copy

    def all_sent(ref, group):
        message(ref, ref, dev_sib, group, 0).wait_send()

    def all_received(ref, slot):
        message(ref, ref, dev_sib, 0, slot).wait_recv()

    top, bottom = pl.ds(0, HALF_ROWS), pl.ds(HALF_ROWS, HALF_ROWS)

    def gather_start(axis, buf, group):
        p = place[axis]
        right, left = near[axis]
        tail = new_slot()
        from_left = send(buf.at[p, top], buf.at[p, top], right, group)
        from_right = send(buf.at[p, bottom], buf.at[p, bottom], left, group)
        send(buf.at[p, bottom], buf.at[p, bottom], right, group, tail)
        send(buf.at[p, top], buf.at[p, top], left, group, tail)
        return buf, group, from_left, from_right, tail

    def gather_pass(axis, state):
        p = place[axis]
        right, left = near[axis]
        buf, group, from_left, from_right, tail = state
        before, after = (p + 3) % RING, (p + 1) % RING
        from_left.wait_recv()
        send(buf.at[before, top], buf.at[before, top], right, group, tail)
        from_right.wait_recv()
        send(buf.at[after, bottom], buf.at[after, bottom], left, group, tail)

    def gather_end(state):
        all_received(state[0].at[pl.ds(0, 2), group_rows], state[4])

    group_rows = pl.ds(0, GROUP_ROWS)

    group = y * RING + x
    my_start = jnp.int32(0)
    begin = jnp.int32(0)
    first_rows = []
    for d in range(N_DP):
        first_rows.append(begin // COLS)
        my_start = jnp.where(dp == d, begin, my_start)
        begin = begin + lengths_ref[group, d]
    my_length = lengths_ref[group, dp]
    lead = my_start % COLS
    lead_rows, lead_lanes = lead // LANES, lead % LANES
    staged[pl.ds(0, LEAD)] = jnp.zeros((LEAD, LANES), jnp.float32)
    tail_rows = staged.shape[0] - LEAD - FLAT_ROWS
    staged[pl.ds(LEAD + FLAT_ROWS, tail_rows)] = jnp.zeros((tail_rows, LANES), jnp.float32)

    def stage(i, _):
        value = flat_ref[:, pl.ds(pl.multiple_of(i * STEP * LANES, LANES), STEP * LANES)].astype(jnp.float32).reshape(STEP, LANES)
        value = jnp.where(slots(i) < my_length, value, 0.0)
        staged[pl.ds(pl.multiple_of(i * STEP + LEAD, 8), STEP)] = pltpu.roll(value, lead_lanes, 1)
        return 0

    lax.fori_loop(0, FLAT_ROWS // STEP, stage, 0)
    extra_tmp[...] = jnp.zeros_like(extra_tmp)

    def partner(i):
        there = (dp + by_distance(i)) % N_DP
        return there, (there, y, x)

    def out_copies(i):
        there, device = partner(i)
        copies = [message(canvas.at[j, there], arrived.at[j, i], device, OUT + j, j) for j in range(PARTS)]
        return copies + [message(extra.at[there], arrived_extra.at[i], device, OUT_EXTRA, PARTS)]

    def place_part(o, _):
        there = (dp + o) % N_DP
        lane = lax.broadcasted_iota(jnp.int32, (MAIN, LANES), 1)
        lane2 = lax.broadcasted_iota(jnp.int32, (2, LANES), 1)
        start = LEAD - lead_rows + there * 4
        before = staged[pl.ds(start - 1, MAIN, stride=CHUNKS)]
        before2 = staged[pl.ds(start - 1 + MAIN * CHUNKS, 2, stride=CHUNKS)]
        for j in range(4):
            here = staged[pl.ds(start + j, MAIN, stride=CHUNKS)]
            here2 = staged[pl.ds(start + j + MAIN * CHUNKS, 2, stride=CHUNKS)]
            canvas[j, there] = jnp.where(lane >= lead_lanes, here, before).astype(jnp.bfloat16)
            extra_tmp[pl.ds(j * 2, 2)] = jnp.where(lane2 >= lead_lanes, here2, before2)
            before, before2 = here, here2
        extra[there] = extra_tmp[...].astype(jnp.bfloat16)
        return 0

    lax.fori_loop(1, N_DP + 1, place_part, 0)
    pl.semaphore_wait(barrier, 4 + N_DP - 1)

    for j in (PARTS, *range(PARTS)):

        def send_out(i, _):
            out_copies(i)[j].start()
            return 0

        lax.fori_loop(0, PEERS, send_out, 0)
    for j in range(PARTS):
        arrived[j, PEERS] = canvas[j, dp]
    arrived_extra[PEERS] = extra[dp]

    def targets(length, width, offset, shape, dim, slot_of):
        k = lax.broadcasted_iota(jnp.int32, shape, dim)
        found = jnp.full(shape, -1, jnp.int32)
        for d in range(N_DP):
            inside = k // width == slot_of(d)
            found = jnp.where(inside, first_rows[d] + k % width + offset, found)
        return k, found

    def arrival_slot(d):
        ahead = (dp - d + N_DP) % N_DP - N_DP // 2
        return jnp.where(ahead >= 0, 2 * ahead, -2 * ahead - 1)

    k, row_of = targets(N_DP * MAIN, MAIN, 0, (1, N_DP * MAIN), 1, arrival_slot)
    pick = (lax.broadcasted_iota(jnp.int32, (GROUP_ROWS, N_DP * MAIN), 0) == row_of).astype(jnp.float32).astype(jnp.bfloat16)
    ke, row_e = targets(N_DP * EXTRA, EXTRA, MAIN, (1, N_DP * EXTRA), 1, arrival_slot)
    ke = ke % EXTRA

    remote = pl.ds(0, PEERS)

    def land(j):
        if j == 0:
            all_received(arrived_extra.at[remote], PARTS)
        all_received(arrived.at[j, remote], j)
        value = jnp.dot(pick, arrived[j].reshape(N_DP * MAIN, LANES), preferred_element_type=jnp.float32)
        row_j = jnp.where(ke // 2 == j, row_e - 2 * j, -1)
        pick_j = (lax.broadcasted_iota(jnp.int32, (GROUP_ROWS, N_DP * EXTRA), 0) == row_j).astype(jnp.float32).astype(jnp.bfloat16)
        late = arrived_extra[...].reshape(N_DP * EXTRA, LANES)
        value = (value + jnp.dot(pick_j, late, preferred_element_type=jnp.float32)).astype(jnp.bfloat16)
        x_ref[:, pl.ds(j * LANES, LANES)] = value
        xr[j, x, group_rows] = value
        xs[j, y] = value
        return gather_start("col", xr.at[j], X_R + j), gather_start("row", xs.at[j], X_S + j)

    def pass_part(states):
        gather_pass("col", states[0])
        gather_pass("row", states[1])

    def end_part(states):
        gather_end(states[0])
        gather_end(states[1])

    def xs_half(h):
        return jnp.concatenate([xs[2 * h].reshape(BLOCK, LANES), xs[2 * h + 1].reshape(BLOCK, LANES)], axis=1)

    halves = (pl.ds(0, HALF_SLAB), pl.ds(HALF_SLAB, HALF_SLAB))
    pad = pl.ds(GROUP_ROWS, PANEL - GROUP_ROWS)
    for q in range(RING):
        for j in range(PARTS):
            xr[j, q, pad] = jnp.zeros((PANEL - GROUP_ROWS, LANES), jnp.bfloat16)
    for p in range(2):
        to_sib[p, pad] = jnp.zeros((PANEL - GROUP_ROWS, BLOCK), jnp.bfloat16)
        own_f32[p, pad] = jnp.zeros((PANEL - GROUP_ROWS, BLOCK), jnp.float32)

    def gram(core, h, store):
        def tile(i, _):
            rows = pl.ds(pl.multiple_of((i % 2) * HALF_ROWS, 16), HALF_ROWS)
            q = 2 * core + i // 2
            value = lax.dot_general(
                jnp.concatenate([xr[2 * h, q, rows], xr[2 * h + 1, q, rows]], axis=1), xs_half(h),
                (((1,), (1,)), ((), ())), preferred_element_type=jnp.float32,
            )
            store(i // 2, rows, value)
            return 0

        lax.fori_loop(0, 4, tile, 0)

    def keep_own(p, rows, value):
        own_f32[p, rows] = value

    def keep_sib(p, rows, value):
        sib_f32[p, rows] = value

    def add_own(p, rows, value):
        own_f32[p, rows] += value

    def add_sib(p, rows, value):
        to_sib[p, rows] = (sib_f32[p, rows] + value).astype(jnp.bfloat16)

    parts = [land(0), land(1)]
    pass_part(parts[0])
    parts.append(land(2))
    pass_part(parts[1])
    parts.append(land(3))
    pass_part(parts[2])
    end_part(parts[0])
    end_part(parts[1])
    gram(1 - c, 0, keep_sib)
    pass_part(parts[3])
    gram(c, 0, keep_own)
    end_part(parts[2])
    end_part(parts[3])
    gram(1 - c, 1, add_sib)

    def shard_rows(s):
        return pl.ds(pl.multiple_of(((s + N_Z) % N_Z) * SHARD, 16), SHARD)

    f32 = jnp.float32
    plan = []
    for k in range(8):
        distance = 4 - (k + 1) // 2
        plan.append((True, k % 2, distance))
        plan.append((False, 1 - k % 2, distance))
    sib_in = []
    for upward, panel, distance in plan:
        rows = shard_rows(z + distance if upward else z - distance)
        sib_in.append(send(to_sib.at[panel, rows], from_sib.at[panel, rows], dev_sib, TO_SIB))
    gram(c, 1, add_own)

    up_in, down_in = [], []
    for (upward, panel, distance), arrival in zip(plan, sib_in):
        rows = shard_rows(z + distance if upward else z - distance)
        arrival.wait_recv()
        term = own_f32[panel, rows] + from_sib[panel, rows].astype(f32)
        if distance == 0:
            up, down = (6, 5) if panel == 0 else (5, 6)
            up_in[up].wait_recv()
            down_in[down].wait_recv()
            term = term + ring_f[up].astype(f32) + ring_b[down].astype(f32)
            g_full[2 * c + panel, rows] = term.astype(jnp.bfloat16)
            continue
        arrivals, ring, device = (up_in, ring_f, dev_up) if upward else (down_in, ring_b, dev_down)
        k = len(arrivals)
        if k < 2:
            src = gh.at[2 * k + int(upward)]
        else:
            arrivals[k - 2].wait_recv()
            src = ring.at[k - 2]
            term = term + ring[k - 2].astype(f32)
        src[...] = term.astype(jnp.bfloat16)
        arrivals.append(send(src, ring.at[k], device, RING_UP if upward else RING_DOWN))
    mine = shard_rows(z)

    sib_slots = {shift: new_slot() for shift in (0, -1, 1, -2, 2, -3, 3, 4)}

    def relay(panel, rows, device, group, slot=None):
        ref = g_full.at[2 * c + panel, rows]
        return send(ref, ref, device, group, slot)

    y_slots = [new_slot() for _ in range(N_Z)]
    y_left, y_right = new_slot(), new_slot()
    order = (0, -1, 1, -2, 2, -3, 3, 4)

    def multiply(shift):
        i, rows = order.index(shift), shard_rows(z + shift)
        all_received(g_full.at[pl.ds(2 * (1 - c), 2), rows], sib_slots[shift])
        left = g_full[:, rows, :].reshape(RING * SHARD, BLOCK)
        for h in range(2):
            value = jnp.dot(left, xs_half(h), preferred_element_type=f32)
            y_tmp[:, :, halves[h]] = value.reshape(RING, SHARD, HALF_SLAB)
        y_out[i] = y_tmp[...].astype(jnp.bfloat16)
        for o in (2, 1, 3):
            there = (x + o) % RING
            send(y_out.at[i, there], y_in.at[i, o - 1], (dp, y, there), Y_SUM, y_slots[i])
        y_own[i] = y_tmp[x]

    def add_up(shift):
        i, rows = order.index(shift), shard_rows(z + shift)
        all_received(y_in.at[i], y_slots[i])
        value = y_own[i] + y_in[i, 0].astype(f32) + y_in[i, 1].astype(f32) + y_in[i, 2].astype(f32)
        y_f32[rows] = value
        ya[y, rows] = value[:, :HALF_SLAB].astype(jnp.bfloat16)
        yb[x, rows] = value[:, HALF_SLAB:].astype(jnp.bfloat16)
        for o in (2, 1, 3):
            send(ya.at[y, rows], ya.at[y, rows], (dp, (y + o) % RING, x), Y_GATHER, y_left)
            send(yb.at[x, rows], yb.at[x, rows], (dp, y, (x + o) % RING), Y_GATHER, y_right)

    up_in, down_in = [], []
    for k in range(9):
        back_by = k // 2
        up_part, down_part = (k % 2, shard_rows(z - back_by)), (1 - k % 2, shard_rows(z + back_by))
        if k >= 2:
            up_in[k - 2].wait_recv()
        if k < 7:
            up_in.append(relay(*up_part, dev_up, G_UP))
        if k >= 2:
            down_in[k - 2].wait_recv()
        if k < 7:
            down_in.append(relay(*down_part, dev_down, G_DOWN))
        relay(*up_part, dev_sib, G_SIB, sib_slots[4 if k == 8 else -back_by])
        if k >= 2:
            relay(*down_part, dev_sib, G_SIB, sib_slots[back_by])
        for shift in {1: (0,), 3: (-1, 1), 5: (-2, 2), 7: (-3, 3), 8: (4,)}.get(k, ()):
            multiply(shift)
        for shift in {3: (0,), 6: (-1, 1), 8: (-2, 2, -3, 3, 4)}.get(k, ()):
            add_up(shift)

    def reduce_start(axis, buf, slots, group):
        right, left = near[axis]
        far = (place[axis] + 2) % RING
        return (
            send(buf.at[far, top], slots[0], right, group),
            send(buf.at[far, bottom], slots[1], left, group),
            new_slot(),
        )

    def reduce_near(axis, buf, slots, group, tail):
        p = place[axis]
        right, left = near[axis]
        after, before = (p + 1) % RING, (p + 3) % RING
        send(buf.at[after, bottom], slots[2].at[bottom], right, group, tail)
        send(buf.at[before, top], slots[3].at[top], left, group, tail)

    def reduce_pass(axis, buf, slots, group, state):
        p = place[axis]
        right, left = near[axis]
        after, before = (p + 1) % RING, (p + 3) % RING
        state[0].wait_recv()
        buf[after, top] = (buf[after, top].astype(f32) + slots[0][...].astype(f32)).astype(jnp.bfloat16)
        send(buf.at[after, top], slots[2].at[top], right, group, state[2])
        state[1].wait_recv()
        buf[before, bottom] = (buf[before, bottom].astype(f32) + slots[1][...].astype(f32)).astype(jnp.bfloat16)
        send(buf.at[before, bottom], slots[3].at[bottom], left, group, state[2])

    first, second = pl.ds(0, HALF_SLAB), pl.ds(HALF_SLAB, HALF_SLAB)
    slots_a, slots_b = [[r.at[i] for r in (got_a, got_b, got_c, got_d)] for i in range(2)]
    far, after, before = (x + 2) % RING, (x + 1) % RING, (x + 3) % RING

    def times(q, right):
        return jnp.dot(g_full[q, group_rows], right, preferred_element_type=f32)

    def open_a(buf, right, slots):
        buf[far] = times(far, right()).astype(jnp.bfloat16)
        state = reduce_start("col", buf, slots, Z_A)
        buf[after] = times(after, right()).astype(jnp.bfloat16)
        buf[before] = times(before, right()).astype(jnp.bfloat16)
        reduce_near("col", buf, slots, Z_A, state[2])
        return state

    def open_b(buf, right, slots):
        def columns(j, _):
            cols = pl.ds(pl.multiple_of(j * LANES, LANES), LANES)
            z_b[cols] = lax.dot_general(
                g_full[:, :, cols].reshape(RING * PANEL, LANES), right, (((0,), (0,)), ((), ())),
                preferred_element_type=f32,
            )
            return 0

        lax.fori_loop(0, BLOCK // LANES, columns, 0)
        buf[...] = z_b[...].astype(jnp.bfloat16).reshape(RING, GROUP_ROWS, HALF_SLAB)
        state = reduce_start("row", buf, slots, Z_B)
        reduce_near("row", buf, slots, Z_B, state[2])
        return state

    def close(state, slots, total, cols):
        all_received(xr.at[pl.ds(0, PARTS), 0, group_rows], state[2])
        total[:, cols] = total[:, cols] + slots[2][...].astype(f32) + slots[3][...].astype(f32)

    def own_b(total):
        total[:, second] = z_b[pl.ds(pl.multiple_of(y * GROUP_ROWS, 8), GROUP_ROWS)]

    three = pl.ds(0, RING - 1)
    all_received(ya.at[three], y_left)
    oa = open_a(part.at[0], lambda: ya[:, :GROUP_ROWS].reshape(BLOCK, HALF_SLAB), slots_a)
    all_received(yb.at[three], y_right)
    ob = open_b(part.at[1], yb[...].reshape(RING * PANEL, HALF_SLAB), slots_b)
    z_f32[:, first] = times(x, ya[:, :GROUP_ROWS].reshape(BLOCK, HALF_SLAB))
    own_b(z_f32)
    reduce_pass("col", part.at[0], slots_a, Z_A, oa)
    reduce_pass("row", part.at[1], slots_b, Z_B, ob)

    _, row_of = targets(N_DP * MAIN, MAIN, 0, (N_DP * MAIN, 1), 0, lambda d: d)
    pick = (lax.broadcasted_iota(jnp.int32, (N_DP * MAIN, GROUP_ROWS), 1) == row_of).astype(f32).astype(jnp.bfloat16)
    ke, row_e = targets(N_DP * EXTRA, EXTRA, MAIN, (N_DP * EXTRA, 1), 0, lambda d: d)
    ke = ke % EXTRA
    late_picks = []
    for j in range(4):
        row_j = jnp.where(ke // 2 == j, row_e - 2 * j, -1)
        pick_j = lax.broadcasted_iota(jnp.int32, (N_DP * EXTRA, GROUP_ROWS), 1) == row_j
        late_picks.append(pick_j.astype(f32).astype(jnp.bfloat16))

    def back_copies(i):
        there, device = partner(i)
        group = i // BACK_GROUP
        return (
            message(outgoing.at[0, there], returned.at[0, i], device, BACK_0, 5 + group),
            message(outgoing.at[1, there], returned.at[1, i], device, BACK_1, 8 + group),
            message(outgoing_extra.at[there], returned_extra.at[i], device, BACK_EXTRA, 11),
        )

    def send_back(n):
        def step(i, _):
            back_copies(i)[n].start()
            return 0

        lax.fori_loop(0, PEERS, step, 0)

    def late_rows(h):
        return sum(
            jnp.dot(late_picks[j], update[:, j * LANES : (j + 1) * LANES], preferred_element_type=f32)
            for j in (2 * h, 2 * h + 1)
        )

    def leave(h, cols):
        update[:, cols] = (
            SCALE * (LINEAR_COEF * x_ref[:, cols].astype(f32) + (CUBIC_COEF * y_f32[group_rows, cols] + QUINTIC_COEF * z_f32[:, cols]))
        ).astype(jnp.bfloat16)
        outgoing[h] = (
            jnp.dot(pick, update[:, cols], preferred_element_type=f32).astype(jnp.bfloat16).reshape(N_DP, MAIN, HALF_SLAB)
        )
        send_back(h)
        returned[h, PEERS] = outgoing[h, dp]

    close(oa, slots_a, z_f32, first)
    leave(0, first)
    late = late_rows(0)
    close(ob, slots_b, z_f32, second)
    leave(1, second)
    outgoing_extra[...] = (late + late_rows(1)).astype(jnp.bfloat16).reshape(N_DP, EXTRA, LANES)
    send_back(2)
    returned_extra[PEERS] = outgoing_extra[dp]

    turn = (LANES - lead_lanes) % LANES

    def unpack(h, i):
        d = (dp - by_distance(i) + N_DP) % N_DP
        for j in range(2):
            back[pl.ds(d * 4 + 2 * h + j, MAIN, stride=CHUNKS)] = pltpu.roll(
                returned[h, i, :, pl.ds(j * LANES, LANES)].astype(f32), turn, 1)

    def unpack_late(i, _):
        d = (dp - by_distance(i) + N_DP) % N_DP
        extra_tmp[...] = pltpu.roll(returned_extra[i].astype(f32), turn, 1)
        for j in range(4):
            back[pl.ds(d * 4 + j + MAIN * CHUNKS, 2, stride=CHUNKS)] = extra_tmp[2 * j : 2 * j + 2]
        return 0

    def unpack_step(h):
        def step(i, _):
            unpack(h, i)
            return 0

        return step

    back[pl.ds(34 * CHUNKS, 8)] = jnp.zeros((8, LANES), f32)
    for h in range(2):
        unpack(h, jnp.int32(PEERS))
    for h in range(2):
        for group in range(3):
            all_received(returned.at[h, pl.ds(group * BACK_GROUP, BACK_GROUP)], 5 + 3 * h + group)
            lax.fori_loop(group * BACK_GROUP, (group + 1) * BACK_GROUP, unpack_step(h), 0)
    all_received(returned_extra.at[pl.ds(0, PEERS)], 11)
    lax.fori_loop(0, N_DP, unpack_late, 0)

    def finish(i, _):
        here = back[pl.ds(i * STEP + lead_rows, STEP)]
        after_rows = back[pl.ds(i * STEP + lead_rows + 1, STEP)]
        lane = lax.broadcasted_iota(jnp.int32, (STEP, LANES), 1)
        value = jnp.where(lane + lead_lanes < LANES, here, after_rows)
        out_ref[pl.ds(pl.multiple_of(i * STEP, 8), STEP)] = jnp.where(slots(i) < my_length, value, 0.0)
        return 0

    lax.fori_loop(0, FLAT_ROWS // STEP, finish, 0)

    for ref, groups in (
        (arrived.at[0, remote], range(OUT, OUT + PARTS)),
        (returned.at[0, remote], (BACK_0, BACK_1)),
        (arrived_extra.at[remote], (OUT_EXTRA, BACK_EXTRA)),
        (xs.at[0, pl.ds(0, RING - 1)], range(X_R, X_S + PARTS)),
        (part.at[0, pl.ds(0, RING - 1)], (Z_A, Z_B)),
        (to_sib, (TO_SIB, G_SIB)),
        (ring_f, (RING_UP, RING_DOWN, G_UP, G_DOWN)),
        (y_in, (Y_SUM, Y_GATHER)),
    ):
        for group in groups:
            all_sent(ref, group)


def flatten_kernel(value_ref, out_ref):
    def step(i, _):
        value = value_ref[pl.ds(pl.multiple_of(i * STEP, 8), STEP)].reshape(1, STEP * LANES)
        out_ref[:, pl.ds(pl.multiple_of(i * STEP * LANES, LANES), STEP * LANES)] = value.astype(jnp.bfloat16)
        return 0

    lax.fori_loop(0, value_ref.shape[0] // STEP, step, 0)


def newton_schulz(lengths, flat):
    bf, f32 = jnp.bfloat16, jnp.float32
    vmem = pltpu.VMEM
    value = pl.pallas_call(
        core_kernel,
        out_shape=jax.ShapeDtypeStruct((FLAT_ROWS, LANES), f32),
        in_specs=[pl.BlockSpec(memory_space=pltpu.SMEM), pl.BlockSpec(memory_space=pltpu.VMEM)],
        out_specs=pl.BlockSpec(memory_space=pltpu.VMEM),
        scratch_shapes=[
            vmem((LEAD + FLAT_ROWS + 88, LANES), f32),
            vmem((PARTS, N_DP, MAIN, LANES), bf),
            vmem((2, N_DP, MAIN, HALF_SLAB), bf),
            vmem((EXTRA, LANES), f32),
            vmem((N_DP, EXTRA, LANES), bf),
            vmem((PARTS, N_DP, MAIN, LANES), bf),
            vmem((N_DP, EXTRA, LANES), bf),
            vmem((GROUP_ROWS, SLAB), bf),
            vmem((PARTS, RING, PANEL, LANES), bf),
            vmem((PARTS, RING, GROUP_ROWS, LANES), bf),
            vmem((2, PANEL, BLOCK), f32),
            vmem((2, PANEL, BLOCK), f32),
            vmem((2, PANEL, BLOCK), bf),
            vmem((2, PANEL, BLOCK), bf),
            vmem((4, SHARD, BLOCK), bf),
            vmem((7, SHARD, BLOCK), bf),
            vmem((7, SHARD, BLOCK), bf),
            vmem((RING, PANEL, BLOCK), bf),
            vmem((2, RING, GROUP_ROWS, HALF_SLAB), bf),
            vmem((2, HALF_ROWS, HALF_SLAB), bf),
            vmem((2, HALF_ROWS, HALF_SLAB), bf),
            vmem((2, GROUP_ROWS, HALF_SLAB), bf),
            vmem((2, GROUP_ROWS, HALF_SLAB), bf),
            vmem((PANEL, SLAB), f32),
            vmem((RING, PANEL, HALF_SLAB), bf),
            vmem((RING, PANEL, HALF_SLAB), bf),
            vmem((RING, SHARD, SLAB), f32),
            vmem((N_Z, RING, SHARD, SLAB), bf),
            vmem((N_Z, RING - 1, SHARD, SLAB), bf),
            vmem((N_Z, SHARD, SLAB), f32),
            vmem((BLOCK, HALF_SLAB), f32),
            vmem((GROUP_ROWS, SLAB), f32),
            vmem((GROUP_ROWS, SLAB), bf),
            vmem((N_DP, EXTRA, LANES), bf),
            vmem((2, N_DP, MAIN, HALF_SLAB), bf),
            vmem((N_DP, EXTRA, LANES), bf),
            vmem((34 * CHUNKS + 8, LANES), f32),
            pltpu.SemaphoreType.DMA((N_SENT,)),
            pltpu.SemaphoreType.DMA((N_RECEIVED,)),
        ],
        compiler_params=pltpu.CompilerParams(
            collective_id=0, has_side_effects=True, vmem_limit_bytes=56 * 1024 * 1024
        ),
    )(lengths, flat)
    return pl.pallas_call(
        flatten_kernel,
        out_shape=jax.ShapeDtypeStruct((1, FLAT_ROWS * LANES), bf),
        grid=(4,),
        in_specs=[pl.BlockSpec((FLAT_ROWS // 4, LANES), lambda i: (i, 0))],
        out_specs=pl.BlockSpec((1, FLAT_ROWS // 4 * LANES), lambda i: (0, i)),
        compiler_params=pltpu.CompilerParams(vmem_limit_bytes=56 * 1024 * 1024),
    )(value)


def local(flat_iterate, lengths):
    return newton_schulz(lengths, flat_iterate)


def solution(mesh):
    return jax.shard_map(
        local,
        mesh=mesh,
        in_specs=(P(("dp", "row", "col"), None), P()),
        out_specs=P(("dp", "row", "col"), None),
        check_vma=False,
    )
```

```python
import math

import jax
import jax.numpy as jnp
from jax import lax
from jax.experimental import pallas as pl
from jax.experimental.pallas import tpu as pltpu
from jax.sharding import PartitionSpec as P

COLS = 8192
ROWS = 5632


LINEAR_COEF = 3.4445
CUBIC_COEF = -4.775
QUINTIC_COEF = 2.0315

N_DP = 16
N_Z = 8
RING = 4
GROUP_ROWS = 352
HALF_ROWS = 176
SLAB = 512
BLOCK = 1408
CORE_ROWS = 704
SHARD = 48
PANEL = N_Z * SHARD
HALF_SLAB = SLAB // 2
LANES = 128
CHUNKS = COLS // LANES
FLAT_ROWS = 2112
MAIN = 32
EXTRA = 16
LEAD = 72
STEP = 176
PEERS = N_DP - 1
BACK_GROUP = 5
PARTS = SLAB // LANES
OUT, X_R, X_S = 0, PARTS, 2 * PARTS
(
    OUT_EXTRA, BACK_0, BACK_1, BACK_EXTRA, TO_SIB, RING_UP, RING_DOWN, G_UP, G_DOWN, G_SIB,
    Y_SUM, Y_GATHER, Z_A, Z_A_MORE, Z_B, N_SENT,
) = range(3 * PARTS, 3 * PARTS + 16)
LEFT = SLAB - LANES
N_RECEIVED = 112
MESH = pl.DeviceIdType.MESH
SCALE = 0.2 * math.sqrt(max(ROWS, COLS))


def slots(i):
    return (
        i * (STEP * LANES)
        + lax.broadcasted_iota(jnp.int32, (STEP, LANES), 0) * LANES
        + lax.broadcasted_iota(jnp.int32, (STEP, LANES), 1)
    )


def core_kernel(
    lengths_ref, flat_ref, out_ref, staged, canvas, outgoing, extra_tmp, extra, arrived, arrived_extra, x_ref, xr, xs, own_f32, sib_f32, to_sib, from_sib, gh, ring_f, ring_b, g_full,
    part, got_a, got_b, got_c, got_d, y_f32, ya, yb, y_tmp, y_out, y_in, y_own, z_b, z_f32, update, outgoing_extra, returned, returned_extra, back, send_sem, recv_sem,
):
    dp = lax.axis_index("dp")
    y = lax.axis_index("row")
    x = lax.axis_index("col")
    z, c = dp // 2, dp % 2
    sib_dp = z * 2 + 1 - c
    up_dp = ((z + 1) % N_Z) * 2 + c
    down_dp = ((z + 7) % N_Z) * 2 + c
    dev_sib = (sib_dp, y, x)
    dev_up = (up_dp, y, x)
    dev_down = (down_dp, y, x)
    near = {
        "col": ((dp, y, (x + 1) % RING), (dp, y, (x + 3) % RING)),
        "row": ((dp, (y + 1) % RING, x), (dp, (y + 3) % RING, x)),
    }
    place = {"col": x, "row": y}

    barrier = pltpu.get_barrier_semaphore()
    for peer in near["col"] + near["row"]:
        pl.semaphore_signal(barrier, inc=1, device_id=peer, device_id_type=MESH)

    def greet(o, _):
        pl.semaphore_signal(barrier, inc=1, device_id=((dp + o) % N_DP, y, x), device_id_type=MESH)
        return 0

    lax.fori_loop(1, N_DP, greet, 0)

    def by_distance(i):
        return N_DP // 2 + (i + 1) // 2 * (1 - 2 * (i % 2))

    counter = [12]

    def message(src, dst, device, group, slot):
        return pltpu.make_async_remote_copy(
            src_ref=src, dst_ref=dst, send_sem=send_sem.at[group], recv_sem=recv_sem.at[slot],
            device_id=device, device_id_type=MESH,
        )

    def new_slot():
        counter[0] += 1
        return counter[0] - 1

    def send(src, dst, device, group, slot=None):
        copy = message(src, dst, device, group, new_slot() if slot is None else slot)
        copy.start()
        return copy

    def all_sent(ref, group):
        message(ref, ref, dev_sib, group, 0).wait_send()

    def all_received(ref, slot):
        message(ref, ref, dev_sib, 0, slot).wait_recv()

    top, bottom = pl.ds(0, HALF_ROWS), pl.ds(HALF_ROWS, HALF_ROWS)

    def gather_start(axis, buf, group):
        p = place[axis]
        right, left = near[axis]
        tail = new_slot()
        from_left = send(buf.at[p, top], buf.at[p, top], right, group)
        from_right = send(buf.at[p, bottom], buf.at[p, bottom], left, group)
        send(buf.at[p, bottom], buf.at[p, bottom], right, group, tail)
        send(buf.at[p, top], buf.at[p, top], left, group, tail)
        return buf, group, from_left, from_right, tail

    def gather_pass(axis, state):
        p = place[axis]
        right, left = near[axis]
        buf, group, from_left, from_right, tail = state
        before, after = (p + 3) % RING, (p + 1) % RING
        from_left.wait_recv()
        send(buf.at[before, top], buf.at[before, top], right, group, tail)
        from_right.wait_recv()
        send(buf.at[after, bottom], buf.at[after, bottom], left, group, tail)

    def gather_end(state):
        all_received(state[0].at[pl.ds(0, 2), group_rows], state[4])

    group_rows = pl.ds(0, GROUP_ROWS)

    group = y * RING + x
    my_start = jnp.int32(0)
    begin = jnp.int32(0)
    first_rows = []
    for d in range(N_DP):
        first_rows.append(begin // COLS)
        my_start = jnp.where(dp == d, begin, my_start)
        begin = begin + lengths_ref[group, d]
    my_length = lengths_ref[group, dp]
    lead = my_start % COLS
    lead_rows, lead_lanes = lead // LANES, lead % LANES
    staged[pl.ds(0, LEAD)] = jnp.zeros((LEAD, LANES), jnp.float32)
    tail_rows = staged.shape[0] - LEAD - FLAT_ROWS
    staged[pl.ds(LEAD + FLAT_ROWS, tail_rows)] = jnp.zeros((tail_rows, LANES), jnp.float32)

    def stage(i, _):
        value = flat_ref[:, pl.ds(pl.multiple_of(i * STEP * LANES, LANES), STEP * LANES)].astype(jnp.float32).reshape(STEP, LANES)
        value = jnp.where(slots(i) < my_length, value, 0.0)
        staged[pl.ds(pl.multiple_of(i * STEP + LEAD, 8), STEP)] = pltpu.roll(value, lead_lanes, 1)
        return 0

    lax.fori_loop(0, FLAT_ROWS // STEP, stage, 0)
    extra_tmp[...] = jnp.zeros_like(extra_tmp)

    def partner(i):
        there = (dp + by_distance(i)) % N_DP
        return there, (there, y, x)

    def out_copies(i):
        there, device = partner(i)
        copies = [message(canvas.at[j, there], arrived.at[j, i], device, OUT + j, j) for j in range(PARTS)]
        return copies + [message(extra.at[there], arrived_extra.at[i], device, OUT_EXTRA, PARTS)]

    def place_part(o, _):
        there = (dp + o) % N_DP
        lane = lax.broadcasted_iota(jnp.int32, (MAIN, LANES), 1)
        lane2 = lax.broadcasted_iota(jnp.int32, (2, LANES), 1)
        start = LEAD - lead_rows + there * 4
        before = staged[pl.ds(start - 1, MAIN, stride=CHUNKS)]
        before2 = staged[pl.ds(start - 1 + MAIN * CHUNKS, 2, stride=CHUNKS)]
        for j in range(4):
            here = staged[pl.ds(start + j, MAIN, stride=CHUNKS)]
            here2 = staged[pl.ds(start + j + MAIN * CHUNKS, 2, stride=CHUNKS)]
            canvas[j, there] = jnp.where(lane >= lead_lanes, here, before).astype(jnp.bfloat16)
            extra_tmp[pl.ds(j * 2, 2)] = jnp.where(lane2 >= lead_lanes, here2, before2)
            before, before2 = here, here2
        extra[there] = extra_tmp[...].astype(jnp.bfloat16)
        return 0

    lax.fori_loop(1, N_DP + 1, place_part, 0)
    pl.semaphore_wait(barrier, 4 + N_DP - 1)

    for j in (PARTS, *range(PARTS)):

        def send_out(i, _):
            out_copies(i)[j].start()
            return 0

        lax.fori_loop(0, PEERS, send_out, 0)
    for j in range(PARTS):
        arrived[j, PEERS] = canvas[j, dp]
    arrived_extra[PEERS] = extra[dp]

    def targets(length, width, offset, shape, dim, slot_of):
        k = lax.broadcasted_iota(jnp.int32, shape, dim)
        found = jnp.full(shape, -1, jnp.int32)
        for d in range(N_DP):
            inside = k // width == slot_of(d)
            found = jnp.where(inside, first_rows[d] + k % width + offset, found)
        return k, found

    def arrival_slot(d):
        ahead = (dp - d + N_DP) % N_DP - N_DP // 2
        return jnp.where(ahead >= 0, 2 * ahead, -2 * ahead - 1)

    k, row_of = targets(N_DP * MAIN, MAIN, 0, (1, N_DP * MAIN), 1, arrival_slot)
    pick = (lax.broadcasted_iota(jnp.int32, (GROUP_ROWS, N_DP * MAIN), 0) == row_of).astype(jnp.float32).astype(jnp.bfloat16)
    ke, row_e = targets(N_DP * EXTRA, EXTRA, MAIN, (1, N_DP * EXTRA), 1, arrival_slot)
    ke = ke % EXTRA

    remote = pl.ds(0, PEERS)

    def land(j):
        if j == 0:
            all_received(arrived_extra.at[remote], PARTS)
        all_received(arrived.at[j, remote], j)
        value = jnp.dot(pick, arrived[j].reshape(N_DP * MAIN, LANES), preferred_element_type=jnp.float32)
        row_j = jnp.where(ke // 2 == j, row_e - 2 * j, -1)
        pick_j = (lax.broadcasted_iota(jnp.int32, (GROUP_ROWS, N_DP * EXTRA), 0) == row_j).astype(jnp.float32).astype(jnp.bfloat16)
        late = arrived_extra[...].reshape(N_DP * EXTRA, LANES)
        value = (value + jnp.dot(pick_j, late, preferred_element_type=jnp.float32)).astype(jnp.bfloat16)
        x_ref[:, pl.ds(j * LANES, LANES)] = value
        xr[j, x, group_rows] = value
        xs[j, y] = value
        return gather_start("col", xr.at[j], X_R + j), gather_start("row", xs.at[j], X_S + j)

    def pass_part(states):
        gather_pass("col", states[0])
        gather_pass("row", states[1])

    def end_part(states):
        gather_end(states[0])
        gather_end(states[1])

    def xs_half(h):
        return jnp.concatenate([xs[2 * h].reshape(BLOCK, LANES), xs[2 * h + 1].reshape(BLOCK, LANES)], axis=1)

    halves = (pl.ds(0, HALF_SLAB), pl.ds(HALF_SLAB, HALF_SLAB))
    pad = pl.ds(GROUP_ROWS, PANEL - GROUP_ROWS)
    for q in range(RING):
        for j in range(PARTS):
            xr[j, q, pad] = jnp.zeros((PANEL - GROUP_ROWS, LANES), jnp.bfloat16)
    for p in range(2):
        to_sib[p, pad] = jnp.zeros((PANEL - GROUP_ROWS, BLOCK), jnp.bfloat16)
        own_f32[p, pad] = jnp.zeros((PANEL - GROUP_ROWS, BLOCK), jnp.float32)

    def gram(core, h, store):
        def tile(i, _):
            rows = pl.ds(pl.multiple_of((i % 2) * HALF_ROWS, 16), HALF_ROWS)
            q = 2 * core + i // 2
            value = lax.dot_general(
                jnp.concatenate([xr[2 * h, q, rows], xr[2 * h + 1, q, rows]], axis=1), xs_half(h),
                (((1,), (1,)), ((), ())), preferred_element_type=jnp.float32,
            )
            store(i // 2, rows, value)
            return 0

        lax.fori_loop(0, 4, tile, 0)

    def keep_own(p, rows, value):
        own_f32[p, rows] = value

    def keep_sib(p, rows, value):
        sib_f32[p, rows] = value

    def add_own(p, rows, value):
        own_f32[p, rows] += value

    def add_sib(p, rows, value):
        to_sib[p, rows] = (sib_f32[p, rows] + value).astype(jnp.bfloat16)

    parts = [land(0), land(1)]
    pass_part(parts[0])
    parts.append(land(2))
    pass_part(parts[1])
    parts.append(land(3))
    pass_part(parts[2])
    end_part(parts[0])
    end_part(parts[1])
    gram(1 - c, 0, keep_sib)
    pass_part(parts[3])
    gram(c, 0, keep_own)
    end_part(parts[2])
    end_part(parts[3])
    gram(1 - c, 1, add_sib)

    def shard_rows(s):
        return pl.ds(pl.multiple_of(((s + N_Z) % N_Z) * SHARD, 16), SHARD)

    f32 = jnp.float32
    plan = []
    for k in range(8):
        distance = 4 - (k + 1) // 2
        plan.append((True, k % 2, distance))
        plan.append((False, 1 - k % 2, distance))
    sib_in = []
    for upward, panel, distance in plan:
        rows = shard_rows(z + distance if upward else z - distance)
        sib_in.append(send(to_sib.at[panel, rows], from_sib.at[panel, rows], dev_sib, TO_SIB))
    gram(c, 1, add_own)

    up_in, down_in = [], []
    for (upward, panel, distance), arrival in zip(plan, sib_in):
        rows = shard_rows(z + distance if upward else z - distance)
        arrival.wait_recv()
        term = own_f32[panel, rows] + from_sib[panel, rows].astype(f32)
        if distance == 0:
            up, down = (6, 5) if panel == 0 else (5, 6)
            up_in[up].wait_recv()
            down_in[down].wait_recv()
            term = term + ring_f[up].astype(f32) + ring_b[down].astype(f32)
            g_full[2 * c + panel, rows] = term.astype(jnp.bfloat16)
            continue
        arrivals, ring, device = (up_in, ring_f, dev_up) if upward else (down_in, ring_b, dev_down)
        k = len(arrivals)
        if k < 2:
            src = gh.at[2 * k + int(upward)]
        else:
            arrivals[k - 2].wait_recv()
            src = ring.at[k - 2]
            term = term + ring[k - 2].astype(f32)
        src[...] = term.astype(jnp.bfloat16)
        arrivals.append(send(src, ring.at[k], device, RING_UP if upward else RING_DOWN))
    mine = shard_rows(z)

    sib_slots = {shift: new_slot() for shift in (0, -1, 1, -2, 2, -3, 3, 4)}

    def relay(panel, rows, device, group, slot=None):
        ref = g_full.at[2 * c + panel, rows]
        return send(ref, ref, device, group, slot)

    y_slots = [new_slot() for _ in range(N_Z)]
    y_left, y_right = new_slot(), new_slot()
    far_slots = {shift: new_slot() for shift in (0, -1, 1, -2, 2)}
    order = (0, -1, 1, -2, 2, -3, 3, 4)

    def multiply(shift):
        i, rows = order.index(shift), shard_rows(z + shift)
        all_received(g_full.at[pl.ds(2 * (1 - c), 2), rows], sib_slots[shift])
        left = g_full[:, rows, :].reshape(RING * SHARD, BLOCK)
        for h in range(2):
            value = jnp.dot(left, xs_half(h), preferred_element_type=f32)
            y_tmp[:, :, halves[h]] = value.reshape(RING, SHARD, HALF_SLAB)
        y_out[i] = y_tmp[...].astype(jnp.bfloat16)
        y_own[i] = y_tmp[x]
        if shift not in far_slots:
            for o in (2, 1, 3):
                there = (x + o) % RING
                send(y_out.at[i, there], y_in.at[i, o - 1], (dp, y, there), Y_SUM, y_slots[i])
            return
        right, left = near["col"]
        far, after, before = (x + 2) % RING, (x + 1) % RING, (x + 3) % RING
        low, high = halves
        send(y_out.at[i, far, :, low], y_in.at[i, 2, :, low], right, Y_SUM, far_slots[shift])
        send(y_out.at[i, far, :, high], y_in.at[i, 2, :, high], left, Y_SUM, far_slots[shift])
        send(y_out.at[i, after, :, high], y_in.at[i, 0, :, high], right, Y_SUM, y_slots[i])
        send(y_out.at[i, before, :, low], y_in.at[i, 1, :, low], left, Y_SUM, y_slots[i])

    def pass_sums(shift):
        i = order.index(shift)
        right, left = near["col"]
        after, before = (x + 1) % RING, (x + 3) % RING
        low, high = halves
        all_received(y_in.at[i, 2], far_slots[shift])
        for there, cols, device, to in ((after, low, right, 0), (before, high, left, 1)):
            total = y_out[i, there, :, cols].astype(f32) + y_in[i, 2, :, cols].astype(f32)
            y_out[i, there, :, cols] = total.astype(jnp.bfloat16)
            send(y_out.at[i, there, :, cols], y_in.at[i, to, :, cols], device, Y_SUM, y_slots[i])

    def add_up(shift):
        i, rows = order.index(shift), shard_rows(z + shift)
        terms = 2 if shift in far_slots else 3
        all_received(y_in.at[i, pl.ds(0, terms)], y_slots[i])
        value = y_own[i]
        for t in range(terms):
            value = value + y_in[i, t].astype(f32)
        y_f32[rows] = value
        ya[y, rows] = value[:, :LEFT].astype(jnp.bfloat16)
        yb[x, rows] = value[:, LEFT:].astype(jnp.bfloat16)
        for o in (2, 1, 3):
            send(ya.at[y, rows], ya.at[y, rows], (dp, (y + o) % RING, x), Y_GATHER, y_left)
            send(yb.at[x, rows], yb.at[x, rows], (dp, y, (x + o) % RING), Y_GATHER, y_right)

    up_in, down_in = [], []
    for k in range(9):
        back_by = k // 2
        up_part, down_part = (k % 2, shard_rows(z - back_by)), (1 - k % 2, shard_rows(z + back_by))
        if k >= 2:
            up_in[k - 2].wait_recv()
        if k < 7:
            up_in.append(relay(*up_part, dev_up, G_UP))
        if k >= 2:
            down_in[k - 2].wait_recv()
        if k < 7:
            down_in.append(relay(*down_part, dev_down, G_DOWN))
        relay(*up_part, dev_sib, G_SIB, sib_slots[4 if k == 8 else -back_by])
        if k >= 2:
            relay(*down_part, dev_sib, G_SIB, sib_slots[back_by])
        for shift in {3: (0,), 5: (-1, 1), 7: (-2, 2)}.get(k, ()):
            pass_sums(shift)
        for shift in {5: (0,), 7: (-1, 1)}.get(k, ()):
            add_up(shift)
        for shift in {1: (0,), 3: (-1, 1), 5: (-2, 2), 7: (-3, 3), 8: (4,)}.get(k, ()):
            multiply(shift)
    for shift in (-2, 2, -3, 3, 4):
        add_up(shift)

    def reduce_start(axis, buf, slots, group):
        right, left = near[axis]
        far = (place[axis] + 2) % RING
        return (
            send(buf.at[far, top], slots[0], right, group),
            send(buf.at[far, bottom], slots[1], left, group),
            new_slot(),
        )

    def reduce_near(axis, buf, slots, group, tail):
        p = place[axis]
        right, left = near[axis]
        after, before = (p + 1) % RING, (p + 3) % RING
        send(buf.at[after, bottom], slots[2].at[bottom], right, group, tail)
        send(buf.at[before, top], slots[3].at[top], left, group, tail)

    def reduce_pass(axis, buf, slots, group, state):
        p = place[axis]
        right, left = near[axis]
        after, before = (p + 1) % RING, (p + 3) % RING
        state[0].wait_recv()
        buf[after, top] = (buf[after, top].astype(f32) + slots[0][...].astype(f32)).astype(jnp.bfloat16)
        send(buf.at[after, top], slots[2].at[top], right, group, state[2])
        state[1].wait_recv()
        buf[before, bottom] = (buf[before, bottom].astype(f32) + slots[1][...].astype(f32)).astype(jnp.bfloat16)
        send(buf.at[before, bottom], slots[3].at[bottom], left, group, state[2])

    first, second = pl.ds(0, HALF_SLAB), pl.ds(HALF_SLAB, HALF_SLAB)
    got = (got_a, got_b, got_c, got_d)
    one_lane, other_lane = pl.ds(0, LANES), pl.ds(LANES, LANES)
    slots_a = [r.at[0] for r in got]
    slots_m = [r.at[1, :, one_lane] for r in got]
    slots_b = [r.at[1, :, other_lane] for r in got]
    part_a, part_m, part_b = part.at[0], part.at[1, :, :, one_lane], part.at[1, :, :, other_lane]
    more, last = pl.ds(HALF_SLAB, LANES), pl.ds(LEFT, LANES)
    far, after, before = (x + 2) % RING, (x + 1) % RING, (x + 3) % RING

    def times(q, right):
        return jnp.dot(g_full[q, group_rows], right, preferred_element_type=f32)

    def open_a(buf, right, slots, group):
        buf[far] = times(far, right()).astype(jnp.bfloat16)
        state = reduce_start("col", buf, slots, group)
        buf[after] = times(after, right()).astype(jnp.bfloat16)
        buf[before] = times(before, right()).astype(jnp.bfloat16)
        reduce_near("col", buf, slots, group, state[2])
        return state

    def open_b(buf, right, slots):
        def columns(j, _):
            cols = pl.ds(pl.multiple_of(j * LANES, LANES), LANES)
            z_b[cols] = lax.dot_general(
                g_full[:, :, cols].reshape(RING * PANEL, LANES), right, (((0,), (0,)), ((), ())),
                preferred_element_type=f32,
            )
            return 0

        lax.fori_loop(0, BLOCK // LANES, columns, 0)
        buf[...] = z_b[...].astype(jnp.bfloat16).reshape(RING, GROUP_ROWS, LANES)
        state = reduce_start("row", buf, slots, Z_B)
        reduce_near("row", buf, slots, Z_B, state[2])
        return state

    def close(state, slots, total, cols):
        all_received(xr.at[pl.ds(0, RING * slots[2].shape[-1] // HALF_SLAB), 0, group_rows], state[2])
        total[:, cols] = total[:, cols] + slots[2][...].astype(f32) + slots[3][...].astype(f32)

    def own_b(total):
        total[:, last] = z_b[pl.ds(pl.multiple_of(y * GROUP_ROWS, 8), GROUP_ROWS)]

    three = pl.ds(0, RING - 1)
    all_received(ya.at[three], y_left)
    def y_part(cols):
        return ya[:, group_rows, cols].reshape(BLOCK, -1)

    oa = open_a(part_a, lambda: y_part(first), slots_a, Z_A)
    om = open_a(part_m, lambda: y_part(more), slots_m, Z_A_MORE)
    all_received(yb.at[three], y_right)
    ob = open_b(part_b, yb[...].reshape(RING * PANEL, LANES), slots_b)
    z_f32[:, first] = times(x, y_part(first))
    reduce_pass("col", part_a, slots_a, Z_A, oa)
    z_f32[:, more] = times(x, y_part(more))
    own_b(z_f32)
    reduce_pass("col", part_m, slots_m, Z_A_MORE, om)
    reduce_pass("row", part_b, slots_b, Z_B, ob)

    _, row_of = targets(N_DP * MAIN, MAIN, 0, (N_DP * MAIN, 1), 0, lambda d: d)
    pick = (lax.broadcasted_iota(jnp.int32, (N_DP * MAIN, GROUP_ROWS), 1) == row_of).astype(f32).astype(jnp.bfloat16)
    ke, row_e = targets(N_DP * EXTRA, EXTRA, MAIN, (N_DP * EXTRA, 1), 0, lambda d: d)
    ke = ke % EXTRA
    late_picks = []
    for j in range(4):
        row_j = jnp.where(ke // 2 == j, row_e - 2 * j, -1)
        pick_j = lax.broadcasted_iota(jnp.int32, (N_DP * EXTRA, GROUP_ROWS), 1) == row_j
        late_picks.append(pick_j.astype(f32).astype(jnp.bfloat16))

    def back_copies(i):
        there, device = partner(i)
        group = i // BACK_GROUP
        return (
            message(outgoing.at[0, there], returned.at[0, i], device, BACK_0, 5 + group),
            message(outgoing.at[1, there], returned.at[1, i], device, BACK_1, 8 + group),
            message(outgoing_extra.at[there], returned_extra.at[i], device, BACK_EXTRA, 11),
        )

    def send_back(n):
        def step(i, _):
            back_copies(i)[n].start()
            return 0

        lax.fori_loop(0, PEERS, step, 0)

    def late_rows(h):
        return sum(
            jnp.dot(late_picks[j], update[:, j * LANES : (j + 1) * LANES], preferred_element_type=f32)
            for j in (2 * h, 2 * h + 1)
        )

    def leave(h, cols):
        update[:, cols] = (
            SCALE * (LINEAR_COEF * x_ref[:, cols].astype(f32) + (CUBIC_COEF * y_f32[group_rows, cols] + QUINTIC_COEF * z_f32[:, cols]))
        ).astype(jnp.bfloat16)
        outgoing[h] = (
            jnp.dot(pick, update[:, cols], preferred_element_type=f32).astype(jnp.bfloat16).reshape(N_DP, MAIN, HALF_SLAB)
        )
        send_back(h)
        returned[h, PEERS] = outgoing[h, dp]

    close(oa, slots_a, z_f32, first)
    leave(0, first)
    late = late_rows(0)
    close(om, slots_m, z_f32, more)
    close(ob, slots_b, z_f32, last)
    leave(1, second)
    outgoing_extra[...] = (late + late_rows(1)).astype(jnp.bfloat16).reshape(N_DP, EXTRA, LANES)
    send_back(2)
    returned_extra[PEERS] = outgoing_extra[dp]

    turn = (LANES - lead_lanes) % LANES

    def unpack(h, i):
        d = (dp - by_distance(i) + N_DP) % N_DP
        for j in range(2):
            back[pl.ds(d * 4 + 2 * h + j, MAIN, stride=CHUNKS)] = pltpu.roll(
                returned[h, i, :, pl.ds(j * LANES, LANES)].astype(f32), turn, 1)

    def unpack_late(i, _):
        d = (dp - by_distance(i) + N_DP) % N_DP
        extra_tmp[...] = pltpu.roll(returned_extra[i].astype(f32), turn, 1)
        for j in range(4):
            back[pl.ds(d * 4 + j + MAIN * CHUNKS, 2, stride=CHUNKS)] = extra_tmp[2 * j : 2 * j + 2]
        return 0

    def unpack_step(h):
        def step(i, _):
            unpack(h, i)
            return 0

        return step

    back[pl.ds(34 * CHUNKS, 8)] = jnp.zeros((8, LANES), f32)
    for h in range(2):
        unpack(h, jnp.int32(PEERS))
    for h in range(2):
        for group in range(3):
            all_received(returned.at[h, pl.ds(group * BACK_GROUP, BACK_GROUP)], 5 + 3 * h + group)
            lax.fori_loop(group * BACK_GROUP, (group + 1) * BACK_GROUP, unpack_step(h), 0)
    all_received(returned_extra.at[pl.ds(0, PEERS)], 11)
    lax.fori_loop(0, N_DP, unpack_late, 0)

    def finish(i, _):
        here = back[pl.ds(i * STEP + lead_rows, STEP)]
        after_rows = back[pl.ds(i * STEP + lead_rows + 1, STEP)]
        lane = lax.broadcasted_iota(jnp.int32, (STEP, LANES), 1)
        value = jnp.where(lane + lead_lanes < LANES, here, after_rows)
        out_ref[pl.ds(pl.multiple_of(i * STEP, 8), STEP)] = jnp.where(slots(i) < my_length, value, 0.0)
        return 0

    lax.fori_loop(0, FLAT_ROWS // STEP, finish, 0)

    for ref, groups in (
        (arrived.at[0, remote], range(OUT, OUT + PARTS)),
        (returned.at[0, remote], (BACK_0, BACK_1)),
        (arrived_extra.at[remote], (OUT_EXTRA, BACK_EXTRA)),
        (xs.at[0, pl.ds(0, RING - 1)], (*range(X_R, X_S + PARTS), Z_A_MORE, Z_B)),
        (part.at[0, pl.ds(0, RING - 1)], (Z_A,)),
        (to_sib, (TO_SIB, G_SIB)),
        (ring_f, (RING_UP, RING_DOWN, G_UP, G_DOWN)),
        (y_in, (Y_SUM, Y_GATHER)),
    ):
        for group in groups:
            all_sent(ref, group)


def flatten_kernel(value_ref, out_ref):
    def step(i, _):
        value = value_ref[pl.ds(pl.multiple_of(i * STEP, 8), STEP)].reshape(1, STEP * LANES)
        out_ref[:, pl.ds(pl.multiple_of(i * STEP * LANES, LANES), STEP * LANES)] = value.astype(jnp.bfloat16)
        return 0

    lax.fori_loop(0, value_ref.shape[0] // STEP, step, 0)


def newton_schulz(lengths, flat):
    bf, f32 = jnp.bfloat16, jnp.float32
    vmem = pltpu.VMEM
    value = pl.pallas_call(
        core_kernel,
        out_shape=jax.ShapeDtypeStruct((FLAT_ROWS, LANES), f32),
        in_specs=[pl.BlockSpec(memory_space=pltpu.SMEM), pl.BlockSpec(memory_space=pltpu.VMEM)],
        out_specs=pl.BlockSpec(memory_space=pltpu.VMEM),
        scratch_shapes=[
            vmem((LEAD + FLAT_ROWS + 88, LANES), f32),
            vmem((PARTS, N_DP, MAIN, LANES), bf),
            vmem((2, N_DP, MAIN, HALF_SLAB), bf),
            vmem((EXTRA, LANES), f32),
            vmem((N_DP, EXTRA, LANES), bf),
            vmem((PARTS, N_DP, MAIN, LANES), bf),
            vmem((N_DP, EXTRA, LANES), bf),
            vmem((GROUP_ROWS, SLAB), bf),
            vmem((PARTS, RING, PANEL, LANES), bf),
            vmem((PARTS, RING, GROUP_ROWS, LANES), bf),
            vmem((2, PANEL, BLOCK), f32),
            vmem((2, PANEL, BLOCK), f32),
            vmem((2, PANEL, BLOCK), bf),
            vmem((2, PANEL, BLOCK), bf),
            vmem((4, SHARD, BLOCK), bf),
            vmem((7, SHARD, BLOCK), bf),
            vmem((7, SHARD, BLOCK), bf),
            vmem((RING, PANEL, BLOCK), bf),
            vmem((2, RING, GROUP_ROWS, HALF_SLAB), bf),
            vmem((2, HALF_ROWS, HALF_SLAB), bf),
            vmem((2, HALF_ROWS, HALF_SLAB), bf),
            vmem((2, GROUP_ROWS, HALF_SLAB), bf),
            vmem((2, GROUP_ROWS, HALF_SLAB), bf),
            vmem((PANEL, SLAB), f32),
            vmem((RING, PANEL, LEFT), bf),
            vmem((RING, PANEL, LANES), bf),
            vmem((RING, SHARD, SLAB), f32),
            vmem((N_Z, RING, SHARD, SLAB), bf),
            vmem((N_Z, RING - 1, SHARD, SLAB), bf),
            vmem((N_Z, SHARD, SLAB), f32),
            vmem((BLOCK, LANES), f32),
            vmem((GROUP_ROWS, SLAB), f32),
            vmem((GROUP_ROWS, SLAB), bf),
            vmem((N_DP, EXTRA, LANES), bf),
            vmem((2, N_DP, MAIN, HALF_SLAB), bf),
            vmem((N_DP, EXTRA, LANES), bf),
            vmem((34 * CHUNKS + 8, LANES), f32),
            pltpu.SemaphoreType.DMA((N_SENT,)),
            pltpu.SemaphoreType.DMA((N_RECEIVED,)),
        ],
        compiler_params=pltpu.CompilerParams(
            collective_id=0, has_side_effects=True, vmem_limit_bytes=56 * 1024 * 1024
        ),
    )(lengths, flat)
    return pl.pallas_call(
        flatten_kernel,
        out_shape=jax.ShapeDtypeStruct((1, FLAT_ROWS * LANES), bf),
        grid=(4,),
        in_specs=[pl.BlockSpec((FLAT_ROWS // 4, LANES), lambda i: (i, 0))],
        out_specs=pl.BlockSpec((1, FLAT_ROWS // 4 * LANES), lambda i: (0, i)),
        compiler_params=pltpu.CompilerParams(vmem_limit_bytes=56 * 1024 * 1024),
    )(value)


def local(flat_iterate, lengths):
    return newton_schulz(lengths, flat_iterate)


def solution(mesh):
    return jax.shard_map(
        local,
        mesh=mesh,
        in_specs=(P(("dp", "row", "col"), None), P()),
        out_specs=P(("dp", "row", "col"), None),
        check_vma=False,
    )
```

```python
import math

import jax
import jax.numpy as jnp
from jax import lax
from jax.experimental import pallas as pl
from jax.experimental.pallas import tpu as pltpu
from jax.sharding import PartitionSpec as P

COLS = 8192
ROWS = 5632


LINEAR_COEF = 3.4445
CUBIC_COEF = -4.775
QUINTIC_COEF = 2.0315

N_DP = 16
N_Z = 8
RING = 4
GROUP_ROWS = 352
HALF_ROWS = 176
SLAB = 512
BLOCK = 1408
CORE_ROWS = 704
SHARD = 48
PANEL = N_Z * SHARD
HALF_SLAB = SLAB // 2
LANES = 128
CHUNKS = COLS // LANES
FLAT_ROWS = 2112
MAIN = 32
EXTRA = 16
LEAD = 72
STEP = 176
PEERS = N_DP - 1
WIDE = 768
BACK_GROUP = 5
PARTS = SLAB // LANES
OUT, X_R, X_S = 0, PARTS, 2 * PARTS
(
    OUT_EXTRA, BACK_0, BACK_1, BACK_EXTRA, TO_SIB, RING_UP, RING_DOWN, G_UP, G_DOWN, G_SIB,
    Y_SUM, Y_GATHER, Z_A, Z_B, N_SENT,
) = range(3 * PARTS, 3 * PARTS + 15)
N_RECEIVED = 120
MESH = pl.DeviceIdType.MESH
SCALE = 0.2 * math.sqrt(max(ROWS, COLS))


def slots(i):
    return (
        i * (STEP * LANES)
        + lax.broadcasted_iota(jnp.int32, (STEP, LANES), 0) * LANES
        + lax.broadcasted_iota(jnp.int32, (STEP, LANES), 1)
    )


def core_kernel(
    lengths_ref, flat_ref, out_ref, staged, canvas, outgoing, extra_tmp, extra, arrived, arrived_extra, x_ref, xr, xs, own_f32, sib_f32, to_sib, from_sib, gh, ring_f, ring_b, g_full,
    part, got_a, got_b, got_c, got_d, y_f32, ya, yb, y_tmp, y_out, y_in, y_own, z_b, z_f32, update, outgoing_extra, returned, returned_extra, back, send_sem, recv_sem,
):
    dp = lax.axis_index("dp")
    y = lax.axis_index("row")
    x = lax.axis_index("col")
    z, c = dp // 2, dp % 2
    sib_dp = z * 2 + 1 - c
    up_dp = ((z + 1) % N_Z) * 2 + c
    down_dp = ((z + 7) % N_Z) * 2 + c
    dev_sib = (sib_dp, y, x)
    dev_up = (up_dp, y, x)
    dev_down = (down_dp, y, x)
    near = {
        "col": ((dp, y, (x + 1) % RING), (dp, y, (x + 3) % RING)),
        "row": ((dp, (y + 1) % RING, x), (dp, (y + 3) % RING, x)),
    }
    far = {"col": (dp, y, (x + 2) % RING), "row": (dp, (y + 2) % RING, x)}
    place = {"col": x, "row": y}

    barrier = pltpu.get_barrier_semaphore()
    for peer in (*near["col"], *near["row"], far["col"], far["row"]):
        pl.semaphore_signal(barrier, inc=1, device_id=peer, device_id_type=MESH)

    def greet(o, _):
        pl.semaphore_signal(barrier, inc=1, device_id=((dp + o) % N_DP, y, x), device_id_type=MESH)
        return 0

    lax.fori_loop(1, N_DP, greet, 0)

    def by_distance(i):
        return N_DP // 2 + (i + 1) // 2 * (1 - 2 * (i % 2))

    counter = [12]

    def message(src, dst, device, group, slot):
        return pltpu.make_async_remote_copy(
            src_ref=src, dst_ref=dst, send_sem=send_sem.at[group], recv_sem=recv_sem.at[slot],
            device_id=device, device_id_type=MESH,
        )

    def new_slot():
        counter[0] += 1
        return counter[0] - 1

    def send(src, dst, device, group, slot=None):
        copy = message(src, dst, device, group, new_slot() if slot is None else slot)
        copy.start()
        return copy

    def all_sent(ref, group):
        message(ref, ref, dev_sib, group, 0).wait_send()

    def all_received(ref, slot):
        message(ref, ref, dev_sib, 0, slot).wait_recv()

    top, bottom = pl.ds(0, HALF_ROWS), pl.ds(HALF_ROWS, HALF_ROWS)

    def gather_start(axis, buf, group):
        p = place[axis]
        right, left = near[axis]
        tail = new_slot()
        if group in (X_R + PARTS - 1, X_S + PARTS - 1):
            own = buf.at[p, group_rows]
            for device in (far[axis], right, left):
                send(own, own, device, group, tail)
            return buf, tail
        from_left = send(buf.at[p, top], buf.at[p, top], right, group)
        from_right = send(buf.at[p, bottom], buf.at[p, bottom], left, group)
        send(buf.at[p, bottom], buf.at[p, bottom], right, group, tail)
        send(buf.at[p, top], buf.at[p, top], left, group, tail)
        return buf, group, from_left, from_right, tail

    def gather_pass(axis, state):
        p = place[axis]
        right, left = near[axis]
        buf, group, from_left, from_right, tail = state
        before, after = (p + 3) % RING, (p + 1) % RING
        from_left.wait_recv()
        send(buf.at[before, top], buf.at[before, top], right, group, tail)
        from_right.wait_recv()
        send(buf.at[after, bottom], buf.at[after, bottom], left, group, tail)

    def gather_end(state):
        all_received(state[0].at[pl.ds(0, 2 if len(state) > 2 else RING - 1), group_rows], state[-1])

    group_rows = pl.ds(0, GROUP_ROWS)

    group = y * RING + x
    my_start = jnp.int32(0)
    begin = jnp.int32(0)
    first_rows = []
    for d in range(N_DP):
        first_rows.append(begin // COLS)
        my_start = jnp.where(dp == d, begin, my_start)
        begin = begin + lengths_ref[group, d]
    my_length = lengths_ref[group, dp]
    lead = my_start % COLS
    lead_rows, lead_lanes = lead // LANES, lead % LANES
    staged[pl.ds(0, LEAD)] = jnp.zeros((LEAD, LANES), jnp.float32)
    tail_rows = staged.shape[0] - LEAD - FLAT_ROWS
    staged[pl.ds(LEAD + FLAT_ROWS, tail_rows)] = jnp.zeros((tail_rows, LANES), jnp.float32)

    def stage(i, _):
        value = flat_ref[:, pl.ds(pl.multiple_of(i * STEP * LANES, LANES), STEP * LANES)].astype(jnp.float32).reshape(STEP, LANES)
        value = jnp.where(slots(i) < my_length, value, 0.0)
        staged[pl.ds(pl.multiple_of(i * STEP + LEAD, 8), STEP)] = pltpu.roll(value, lead_lanes, 1)
        return 0

    lax.fori_loop(0, FLAT_ROWS // STEP, stage, 0)
    extra_tmp[...] = jnp.zeros_like(extra_tmp)

    def partner(i):
        there = (dp + by_distance(i)) % N_DP
        return there, (there, y, x)

    def out_copies(i):
        there, device = partner(i)
        copies = [message(canvas.at[j, there], arrived.at[j, i], device, OUT + j, j) for j in range(PARTS)]
        return copies + [message(extra.at[there], arrived_extra.at[i], device, OUT_EXTRA, PARTS)]

    def place_part(o, _):
        there = (dp + o) % N_DP
        lane = lax.broadcasted_iota(jnp.int32, (MAIN, LANES), 1)
        lane2 = lax.broadcasted_iota(jnp.int32, (2, LANES), 1)
        start = LEAD - lead_rows + there * 4
        before = staged[pl.ds(start - 1, MAIN, stride=CHUNKS)]
        before2 = staged[pl.ds(start - 1 + MAIN * CHUNKS, 2, stride=CHUNKS)]
        for j in range(4):
            here = staged[pl.ds(start + j, MAIN, stride=CHUNKS)]
            here2 = staged[pl.ds(start + j + MAIN * CHUNKS, 2, stride=CHUNKS)]
            canvas[j, there] = jnp.where(lane >= lead_lanes, here, before).astype(jnp.bfloat16)
            extra_tmp[pl.ds(j * 2, 2)] = jnp.where(lane2 >= lead_lanes, here2, before2)
            before, before2 = here, here2
        extra[there] = extra_tmp[...].astype(jnp.bfloat16)
        return 0

    lax.fori_loop(1, N_DP + 1, place_part, 0)
    pl.semaphore_wait(barrier, 6 + N_DP - 1)

    for j in (PARTS, *range(PARTS)):

        def send_out(i, _):
            out_copies(i)[j].start()
            return 0

        lax.fori_loop(0, PEERS, send_out, 0)
    for j in range(PARTS):
        arrived[j, PEERS] = canvas[j, dp]
    arrived_extra[PEERS] = extra[dp]

    def targets(length, width, offset, shape, dim, slot_of):
        k = lax.broadcasted_iota(jnp.int32, shape, dim)
        found = jnp.full(shape, -1, jnp.int32)
        for d in range(N_DP):
            inside = k // width == slot_of(d)
            found = jnp.where(inside, first_rows[d] + k % width + offset, found)
        return k, found

    def arrival_slot(d):
        ahead = (dp - d + N_DP) % N_DP - N_DP // 2
        return jnp.where(ahead >= 0, 2 * ahead, -2 * ahead - 1)

    k, row_of = targets(N_DP * MAIN, MAIN, 0, (1, N_DP * MAIN), 1, arrival_slot)
    pick = (lax.broadcasted_iota(jnp.int32, (GROUP_ROWS, N_DP * MAIN), 0) == row_of).astype(jnp.float32).astype(jnp.bfloat16)
    ke, row_e = targets(N_DP * EXTRA, EXTRA, MAIN, (1, N_DP * EXTRA), 1, arrival_slot)
    ke = ke % EXTRA

    remote = pl.ds(0, PEERS)

    def land(j):
        if j == 0:
            all_received(arrived_extra.at[remote], PARTS)
        all_received(arrived.at[j, remote], j)
        value = jnp.dot(pick, arrived[j].reshape(N_DP * MAIN, LANES), preferred_element_type=jnp.float32)
        row_j = jnp.where(ke // 2 == j, row_e - 2 * j, -1)
        pick_j = (lax.broadcasted_iota(jnp.int32, (GROUP_ROWS, N_DP * EXTRA), 0) == row_j).astype(jnp.float32).astype(jnp.bfloat16)
        late = arrived_extra[...].reshape(N_DP * EXTRA, LANES)
        value = (value + jnp.dot(pick_j, late, preferred_element_type=jnp.float32)).astype(jnp.bfloat16)
        x_ref[:, pl.ds(j * LANES, LANES)] = value
        xr[j, x, group_rows] = value
        xs[j, y] = value
        return gather_start("col", xr.at[j], X_R + j), gather_start("row", xs.at[j], X_S + j)

    def pass_part(states):
        gather_pass("col", states[0])
        gather_pass("row", states[1])

    def end_part(states):
        gather_end(states[0])
        gather_end(states[1])

    def xs_half(h):
        return jnp.concatenate([xs[2 * h].reshape(BLOCK, LANES), xs[2 * h + 1].reshape(BLOCK, LANES)], axis=1)

    halves = (pl.ds(0, HALF_SLAB), pl.ds(HALF_SLAB, HALF_SLAB))
    pad = pl.ds(GROUP_ROWS, PANEL - GROUP_ROWS)
    for q in range(RING):
        for j in range(PARTS):
            xr[j, q, pad] = jnp.zeros((PANEL - GROUP_ROWS, LANES), jnp.bfloat16)
    for p in range(2):
        to_sib[p, pad] = jnp.zeros((PANEL - GROUP_ROWS, BLOCK), jnp.bfloat16)
        own_f32[p, pad] = jnp.zeros((PANEL - GROUP_ROWS, BLOCK), jnp.float32)

    def gram(core, h, store):
        def tile(i, _):
            rows = pl.ds(pl.multiple_of((i % 2) * HALF_ROWS, 16), HALF_ROWS)
            q = 2 * core + i // 2
            value = lax.dot_general(
                jnp.concatenate([xr[2 * h, q, rows], xr[2 * h + 1, q, rows]], axis=1), xs_half(h),
                (((1,), (1,)), ((), ())), preferred_element_type=jnp.float32,
            )
            store(i // 2, rows, value)
            return 0

        lax.fori_loop(0, 4, tile, 0)

    def keep_own(p, rows, value):
        own_f32[p, rows] = value

    def keep_sib(p, rows, value):
        sib_f32[p, rows] = value

    def add_own(p, rows, value):
        own_f32[p, rows] += value

    def add_sib(p, rows, value):
        to_sib[p, rows] = (sib_f32[p, rows] + value).astype(jnp.bfloat16)

    parts = [land(0), land(1)]
    pass_part(parts[0])
    parts.append(land(2))
    pass_part(parts[1])
    parts.append(land(3))
    pass_part(parts[2])
    end_part(parts[0])
    end_part(parts[1])
    gram(1 - c, 0, keep_sib)
    gram(c, 0, keep_own)
    end_part(parts[2])
    end_part(parts[3])
    gram(1 - c, 1, add_sib)

    def shard_rows(s):
        return pl.ds(pl.multiple_of(((s + N_Z) % N_Z) * SHARD, 16), SHARD)

    f32 = jnp.float32
    plan = []
    for k in range(8):
        distance = 4 - (k + 1) // 2
        plan.append((True, k % 2, distance))
        plan.append((False, 1 - k % 2, distance))
    sib_in = []
    for upward, panel, distance in plan:
        rows = shard_rows(z + distance if upward else z - distance)
        sib_in.append(send(to_sib.at[panel, rows], from_sib.at[panel, rows], dev_sib, TO_SIB))
    gram(c, 1, add_own)

    ring_cols = (pl.ds(0, WIDE), pl.ds(WIDE, BLOCK - WIDE))
    up_in, down_in = [], []
    for (upward, panel, distance), arrival in zip(plan, sib_in):
        rows = shard_rows(z + distance if upward else z - distance)
        arrival.wait_recv()
        arrivals, ring, device = (up_in, ring_f, dev_up) if upward else (down_in, ring_b, dev_down)
        k = len(arrivals)
        copies = []
        for n, cols in enumerate(ring_cols):
            term = own_f32[panel, rows, cols] + from_sib[panel, rows, cols].astype(f32)
            if distance == 0:
                up, down = (6, 5) if panel == 0 else (5, 6)
                up_in[up][n].wait_recv()
                down_in[down][n].wait_recv()
                term = term + ring_f[up, :, cols].astype(f32) + ring_b[down, :, cols].astype(f32)
                g_full[2 * c + panel, rows, cols] = term.astype(jnp.bfloat16)
                continue
            if k < 2:
                src = gh.at[2 * k + int(upward), :, cols]
            else:
                arrivals[k - 2][n].wait_recv()
                src = ring.at[k - 2, :, cols]
                term = term + ring[k - 2, :, cols].astype(f32)
            src[...] = term.astype(jnp.bfloat16)
            copies.append(send(src, ring.at[k, :, cols], device, RING_UP if upward else RING_DOWN))
        if distance:
            arrivals.append(copies)
    mine = shard_rows(z)

    sib_slots = {shift: new_slot() for shift in (0, -1, 1, -2, 2, -3, 3, 4)}

    def relay(panel, rows, device, group, slot=None):
        ref = g_full.at[2 * c + panel, rows]
        return send(ref, ref, device, group, slot)

    y_slots = [new_slot() for _ in range(N_Z)]
    y_left, y_right = new_slot(), new_slot()
    order = (0, -1, 1, -2, 2, -3, 3, 4)

    def multiply(shift):
        i, rows = order.index(shift), shard_rows(z + shift)
        all_received(g_full.at[pl.ds(2 * (1 - c), 2), rows], sib_slots[shift])
        left = g_full[:, rows, :].reshape(RING * SHARD, BLOCK)
        for h in range(2):
            value = jnp.dot(left, xs_half(h), preferred_element_type=f32)
            y_tmp[:, :, halves[h]] = value.reshape(RING, SHARD, HALF_SLAB)
        y_out[i] = y_tmp[...].astype(jnp.bfloat16)
        for o in (2, 1, 3):
            there = (x + o) % RING
            send(y_out.at[i, there], y_in.at[i, o - 1], (dp, y, there), Y_SUM, y_slots[i])
        y_own[i] = y_tmp[x]

    def add_up(shift):
        i, rows = order.index(shift), shard_rows(z + shift)
        all_received(y_in.at[i], y_slots[i])
        value = y_own[i] + y_in[i, 0].astype(f32) + y_in[i, 1].astype(f32) + y_in[i, 2].astype(f32)
        y_f32[rows] = value
        ya[y, rows] = value[:, :HALF_SLAB].astype(jnp.bfloat16)
        yb[x, rows] = value[:, HALF_SLAB:].astype(jnp.bfloat16)
        for o in (2, 1, 3):
            send(ya.at[y, rows], ya.at[y, rows], (dp, (y + o) % RING, x), Y_GATHER, y_left)
            send(yb.at[x, rows], yb.at[x, rows], (dp, y, (x + o) % RING), Y_GATHER, y_right)

    up_in, down_in = [], []
    for k in range(9):
        back_by = k // 2
        up_part, down_part = (k % 2, shard_rows(z - back_by)), (1 - k % 2, shard_rows(z + back_by))
        if k >= 2:
            up_in[k - 2].wait_recv()
        if k < 7:
            up_in.append(relay(*up_part, dev_up, G_UP))
        if k >= 2:
            down_in[k - 2].wait_recv()
        if k < 7:
            down_in.append(relay(*down_part, dev_down, G_DOWN))
        relay(*up_part, dev_sib, G_SIB, sib_slots[4 if k == 8 else -back_by])
        if k >= 2:
            relay(*down_part, dev_sib, G_SIB, sib_slots[back_by])
        for shift in {1: (0,), 3: (-1, 1), 5: (-2, 2), 7: (-3, 3), 8: (4,)}.get(k, ()):
            multiply(shift)
        for shift in {3: (0,), 6: (-1, 1), 7: (-2, 2)}.get(k, ()):
            add_up(shift)
    for shift in (-3, 3, 4):
        add_up(shift)

    def reduce_start(axis, buf, slots, group):
        right, left = near[axis]
        farthest = (place[axis] + 2) % RING
        return (
            send(buf.at[farthest, top], slots[0], right, group),
            send(buf.at[farthest, bottom], slots[1], left, group),
            new_slot(),
        )

    def reduce_near(axis, buf, slots, group, tail):
        p = place[axis]
        right, left = near[axis]
        after, before = (p + 1) % RING, (p + 3) % RING
        send(buf.at[after, bottom], slots[2].at[bottom], right, group, tail)
        send(buf.at[before, top], slots[3].at[top], left, group, tail)

    def reduce_pass(axis, buf, slots, group, state):
        p = place[axis]
        right, left = near[axis]
        after, before = (p + 1) % RING, (p + 3) % RING
        state[0].wait_recv()
        buf[after, top] = (buf[after, top].astype(f32) + slots[0][...].astype(f32)).astype(jnp.bfloat16)
        send(buf.at[after, top], slots[2].at[top], right, group, state[2])
        state[1].wait_recv()
        buf[before, bottom] = (buf[before, bottom].astype(f32) + slots[1][...].astype(f32)).astype(jnp.bfloat16)
        send(buf.at[before, bottom], slots[3].at[bottom], left, group, state[2])

    first, second = pl.ds(0, HALF_SLAB), pl.ds(HALF_SLAB, HALF_SLAB)
    slots_a, slots_b = [[r.at[i] for r in (got_a, got_b, got_c, got_d)] for i in range(2)]
    farthest, after, before = (x + 2) % RING, (x + 1) % RING, (x + 3) % RING

    def times(q, right):
        return jnp.dot(g_full[q, group_rows], right, preferred_element_type=f32)

    def open_a(buf, right, slots):
        buf[farthest] = times(farthest, right()).astype(jnp.bfloat16)
        state = reduce_start("col", buf, slots, Z_A)
        buf[after] = times(after, right()).astype(jnp.bfloat16)
        buf[before] = times(before, right()).astype(jnp.bfloat16)
        reduce_near("col", buf, slots, Z_A, state[2])
        return state

    def open_b(buf, right, slots):
        def columns(j, _):
            cols = pl.ds(pl.multiple_of(j * LANES, LANES), LANES)
            z_b[cols] = lax.dot_general(
                g_full[:, :, cols].reshape(RING * PANEL, LANES), right, (((0,), (0,)), ((), ())),
                preferred_element_type=f32,
            )
            return 0

        lax.fori_loop(0, BLOCK // LANES, columns, 0)
        buf[...] = z_b[...].astype(jnp.bfloat16).reshape(RING, GROUP_ROWS, HALF_SLAB)
        state = reduce_start("row", buf, slots, Z_B)
        reduce_near("row", buf, slots, Z_B, state[2])
        return state

    def close(state, slots, total, cols):
        all_received(xr.at[pl.ds(0, PARTS), 0, group_rows], state[2])
        total[:, cols] = total[:, cols] + slots[2][...].astype(f32) + slots[3][...].astype(f32)

    def own_b(total):
        total[:, second] = z_b[pl.ds(pl.multiple_of(y * GROUP_ROWS, 8), GROUP_ROWS)]

    three = pl.ds(0, RING - 1)
    all_received(ya.at[three], y_left)
    oa = open_a(part.at[0], lambda: ya[:, :GROUP_ROWS].reshape(BLOCK, HALF_SLAB), slots_a)
    all_received(yb.at[three], y_right)
    ob = open_b(part.at[1], yb[...].reshape(RING * PANEL, HALF_SLAB), slots_b)
    z_f32[:, first] = times(x, ya[:, :GROUP_ROWS].reshape(BLOCK, HALF_SLAB))
    own_b(z_f32)
    reduce_pass("col", part.at[0], slots_a, Z_A, oa)
    reduce_pass("row", part.at[1], slots_b, Z_B, ob)

    _, row_of = targets(N_DP * MAIN, MAIN, 0, (N_DP * MAIN, 1), 0, lambda d: d)
    pick = (lax.broadcasted_iota(jnp.int32, (N_DP * MAIN, GROUP_ROWS), 1) == row_of).astype(f32).astype(jnp.bfloat16)
    ke, row_e = targets(N_DP * EXTRA, EXTRA, MAIN, (N_DP * EXTRA, 1), 0, lambda d: d)
    ke = ke % EXTRA
    late_picks = []
    for j in range(4):
        row_j = jnp.where(ke // 2 == j, row_e - 2 * j, -1)
        pick_j = lax.broadcasted_iota(jnp.int32, (N_DP * EXTRA, GROUP_ROWS), 1) == row_j
        late_picks.append(pick_j.astype(f32).astype(jnp.bfloat16))

    def back_copies(i):
        there, device = partner(i)
        group = i // BACK_GROUP
        return (
            message(outgoing.at[0, there], returned.at[0, i], device, BACK_0, 5 + group),
            message(outgoing.at[1, there], returned.at[1, i], device, BACK_1, 8 + group),
            message(outgoing_extra.at[there], returned_extra.at[i], device, BACK_EXTRA, 11),
        )

    def send_back(n):
        def step(i, _):
            back_copies(i)[n].start()
            return 0

        lax.fori_loop(0, PEERS, step, 0)

    def late_rows(h):
        return sum(
            jnp.dot(late_picks[j], update[:, j * LANES : (j + 1) * LANES], preferred_element_type=f32)
            for j in (2 * h, 2 * h + 1)
        )

    def leave(h, cols):
        update[:, cols] = (
            SCALE * (LINEAR_COEF * x_ref[:, cols].astype(f32) + (CUBIC_COEF * y_f32[group_rows, cols] + QUINTIC_COEF * z_f32[:, cols]))
        ).astype(jnp.bfloat16)
        outgoing[h] = (
            jnp.dot(pick, update[:, cols], preferred_element_type=f32).astype(jnp.bfloat16).reshape(N_DP, MAIN, HALF_SLAB)
        )
        send_back(h)
        returned[h, PEERS] = outgoing[h, dp]

    close(oa, slots_a, z_f32, first)
    leave(0, first)
    late = late_rows(0)
    close(ob, slots_b, z_f32, second)
    leave(1, second)
    outgoing_extra[...] = (late + late_rows(1)).astype(jnp.bfloat16).reshape(N_DP, EXTRA, LANES)
    send_back(2)
    returned_extra[PEERS] = outgoing_extra[dp]

    turn = (LANES - lead_lanes) % LANES

    def unpack(h, i):
        d = (dp - by_distance(i) + N_DP) % N_DP
        for j in range(2):
            back[pl.ds(d * 4 + 2 * h + j, MAIN, stride=CHUNKS)] = pltpu.roll(
                returned[h, i, :, pl.ds(j * LANES, LANES)].astype(f32), turn, 1)

    def unpack_late(i, _):
        d = (dp - by_distance(i) + N_DP) % N_DP
        extra_tmp[...] = pltpu.roll(returned_extra[i].astype(f32), turn, 1)
        for j in range(4):
            back[pl.ds(d * 4 + j + MAIN * CHUNKS, 2, stride=CHUNKS)] = extra_tmp[2 * j : 2 * j + 2]
        return 0

    def unpack_step(h):
        def step(i, _):
            unpack(h, i)
            return 0

        return step

    back[pl.ds(34 * CHUNKS, 8)] = jnp.zeros((8, LANES), f32)
    for h in range(2):
        unpack(h, jnp.int32(PEERS))
    for h in range(2):
        for group in range(3):
            all_received(returned.at[h, pl.ds(group * BACK_GROUP, BACK_GROUP)], 5 + 3 * h + group)
            lax.fori_loop(group * BACK_GROUP, (group + 1) * BACK_GROUP, unpack_step(h), 0)
    all_received(returned_extra.at[pl.ds(0, PEERS)], 11)
    lax.fori_loop(0, N_DP, unpack_late, 0)

    def finish(i, _):
        here = back[pl.ds(i * STEP + lead_rows, STEP)]
        after_rows = back[pl.ds(i * STEP + lead_rows + 1, STEP)]
        lane = lax.broadcasted_iota(jnp.int32, (STEP, LANES), 1)
        value = jnp.where(lane + lead_lanes < LANES, here, after_rows)
        out_ref[pl.ds(pl.multiple_of(i * STEP, 8), STEP)] = jnp.where(slots(i) < my_length, value, 0.0)
        return 0

    lax.fori_loop(0, FLAT_ROWS // STEP, finish, 0)

    for ref, groups in (
        (arrived.at[0, remote], range(OUT, OUT + PARTS)),
        (returned.at[0, remote], (BACK_0, BACK_1)),
        (arrived_extra.at[remote], (OUT_EXTRA, BACK_EXTRA)),
        (xs.at[0, pl.ds(0, RING - 1)], range(X_R, X_S + PARTS)),
        (part.at[0, pl.ds(0, RING - 1)], (Z_A, Z_B)),
        (to_sib, (TO_SIB, G_SIB)),
        (ring_f, (RING_UP, RING_DOWN, G_UP, G_DOWN)),
        (y_in, (Y_SUM, Y_GATHER)),
    ):
        for group in groups:
            all_sent(ref, group)


def flatten_kernel(value_ref, out_ref):
    def step(i, _):
        value = value_ref[pl.ds(pl.multiple_of(i * STEP, 8), STEP)].reshape(1, STEP * LANES)
        out_ref[:, pl.ds(pl.multiple_of(i * STEP * LANES, LANES), STEP * LANES)] = value.astype(jnp.bfloat16)
        return 0

    lax.fori_loop(0, value_ref.shape[0] // STEP, step, 0)


def newton_schulz(lengths, flat):
    bf, f32 = jnp.bfloat16, jnp.float32
    vmem = pltpu.VMEM
    value = pl.pallas_call(
        core_kernel,
        out_shape=jax.ShapeDtypeStruct((FLAT_ROWS, LANES), f32),
        in_specs=[pl.BlockSpec(memory_space=pltpu.SMEM), pl.BlockSpec(memory_space=pltpu.VMEM)],
        out_specs=pl.BlockSpec(memory_space=pltpu.VMEM),
        scratch_shapes=[
            vmem((LEAD + FLAT_ROWS + 88, LANES), f32),
            vmem((PARTS, N_DP, MAIN, LANES), bf),
            vmem((2, N_DP, MAIN, HALF_SLAB), bf),
            vmem((EXTRA, LANES), f32),
            vmem((N_DP, EXTRA, LANES), bf),
            vmem((PARTS, N_DP, MAIN, LANES), bf),
            vmem((N_DP, EXTRA, LANES), bf),
            vmem((GROUP_ROWS, SLAB), bf),
            vmem((PARTS, RING, PANEL, LANES), bf),
            vmem((PARTS, RING, GROUP_ROWS, LANES), bf),
            vmem((2, PANEL, BLOCK), f32),
            vmem((2, PANEL, BLOCK), f32),
            vmem((2, PANEL, BLOCK), bf),
            vmem((2, PANEL, BLOCK), bf),
            vmem((4, SHARD, BLOCK), bf),
            vmem((7, SHARD, BLOCK), bf),
            vmem((7, SHARD, BLOCK), bf),
            vmem((RING, PANEL, BLOCK), bf),
            vmem((2, RING, GROUP_ROWS, HALF_SLAB), bf),
            vmem((2, HALF_ROWS, HALF_SLAB), bf),
            vmem((2, HALF_ROWS, HALF_SLAB), bf),
            vmem((2, GROUP_ROWS, HALF_SLAB), bf),
            vmem((2, GROUP_ROWS, HALF_SLAB), bf),
            vmem((PANEL, SLAB), f32),
            vmem((RING, PANEL, HALF_SLAB), bf),
            vmem((RING, PANEL, HALF_SLAB), bf),
            vmem((RING, SHARD, SLAB), f32),
            vmem((N_Z, RING, SHARD, SLAB), bf),
            vmem((N_Z, RING - 1, SHARD, SLAB), bf),
            vmem((N_Z, SHARD, SLAB), f32),
            vmem((BLOCK, HALF_SLAB), f32),
            vmem((GROUP_ROWS, SLAB), f32),
            vmem((GROUP_ROWS, SLAB), bf),
            vmem((N_DP, EXTRA, LANES), bf),
            vmem((2, N_DP, MAIN, HALF_SLAB), bf),
            vmem((N_DP, EXTRA, LANES), bf),
            vmem((34 * CHUNKS + 8, LANES), f32),
            pltpu.SemaphoreType.DMA((N_SENT,)),
            pltpu.SemaphoreType.DMA((N_RECEIVED,)),
        ],
        compiler_params=pltpu.CompilerParams(
            collective_id=0, has_side_effects=True, vmem_limit_bytes=56 * 1024 * 1024
        ),
    )(lengths, flat)
    return pl.pallas_call(
        flatten_kernel,
        out_shape=jax.ShapeDtypeStruct((1, FLAT_ROWS * LANES), bf),
        in_specs=[pl.BlockSpec(memory_space=pltpu.VMEM)],
        out_specs=pl.BlockSpec(memory_space=pltpu.VMEM),
        compiler_params=pltpu.CompilerParams(vmem_limit_bytes=56 * 1024 * 1024),
    )(value)


def local(flat_iterate, lengths):
    return newton_schulz(lengths, flat_iterate)


def solution(mesh):
    return jax.shard_map(
        local,
        mesh=mesh,
        in_specs=(P(("dp", "row", "col"), None), P()),
        out_specs=P(("dp", "row", "col"), None),
        check_vma=False,
    )
```

```python
import math

import jax
import jax.numpy as jnp
from jax import lax
from jax.experimental import pallas as pl
from jax.experimental.pallas import tpu as pltpu
from jax.sharding import PartitionSpec as P

COLS = 8192
ROWS = 5632


LINEAR_COEF = 3.4445
CUBIC_COEF = -4.775
QUINTIC_COEF = 2.0315

N_DP = 16
N_Z = 8
RING = 4
GROUP_ROWS = 352
HALF_ROWS = 176
SLAB = 512
BLOCK = 1408
CORE_ROWS = 704
SHARD = 48
PANEL = N_Z * SHARD
HALF_SLAB = SLAB // 2
LANES = 128
CHUNKS = COLS // LANES
FLAT_ROWS = 2112
MAIN = 32
EXTRA = 16
LEAD = 72
STEP = 176
PEERS = N_DP - 1
WIDE = 768
BACK_GROUP = 5
PARTS = SLAB // LANES
OUT, X_R, X_S = 0, PARTS, 2 * PARTS
(
    OUT_EXTRA, BACK_0, BACK_1, BACK_EXTRA, TO_SIB, RING_UP, RING_DOWN, G_UP, G_DOWN, G_SIB,
    Y_SUM, Y_GATHER, Z_A, Z_B, N_SENT,
) = range(3 * PARTS, 3 * PARTS + 15)
N_RECEIVED = 120
MESH = pl.DeviceIdType.MESH
SCALE = 0.2 * math.sqrt(max(ROWS, COLS))


def slots(i):
    return (
        i * (STEP * LANES)
        + lax.broadcasted_iota(jnp.int32, (STEP, LANES), 0) * LANES
        + lax.broadcasted_iota(jnp.int32, (STEP, LANES), 1)
    )


def core_kernel(
    lengths_ref, flat_ref, out_ref, staged, canvas, outgoing, extra_tmp, extra, arrived, arrived_extra, x_ref, xr, xs, own_f32, sib_f32, to_sib, from_sib, gh, ring_f, ring_b, g_full,
    part, got_a, got_b, got_c, got_d, y_f32, ya, yb, y_tmp, y_out, y_in, y_own, z_b, z_f32, update, outgoing_extra, returned, returned_extra, back, send_sem, recv_sem,
):
    dp = lax.axis_index("dp")
    y = lax.axis_index("row")
    x = lax.axis_index("col")
    z, c = dp // 2, dp % 2
    sib_dp = z * 2 + 1 - c
    up_dp = ((z + 1) % N_Z) * 2 + c
    down_dp = ((z + 7) % N_Z) * 2 + c
    dev_sib = (sib_dp, y, x)
    dev_up = (up_dp, y, x)
    dev_down = (down_dp, y, x)
    near = {
        "col": ((dp, y, (x + 1) % RING), (dp, y, (x + 3) % RING)),
        "row": ((dp, (y + 1) % RING, x), (dp, (y + 3) % RING, x)),
    }
    far = {"col": (dp, y, (x + 2) % RING), "row": (dp, (y + 2) % RING, x)}
    place = {"col": x, "row": y}

    barrier = pltpu.get_barrier_semaphore()
    for peer in (*near["col"], *near["row"], far["col"], far["row"]):
        pl.semaphore_signal(barrier, inc=1, device_id=peer, device_id_type=MESH)

    def greet(o, _):
        pl.semaphore_signal(barrier, inc=1, device_id=((dp + o) % N_DP, y, x), device_id_type=MESH)
        return 0

    lax.fori_loop(1, N_DP, greet, 0)

    def by_distance(i):
        return N_DP // 2 + (i + 1) // 2 * (1 - 2 * (i % 2))

    counter = [12]

    def message(src, dst, device, group, slot):
        return pltpu.make_async_remote_copy(
            src_ref=src, dst_ref=dst, send_sem=send_sem.at[group], recv_sem=recv_sem.at[slot],
            device_id=device, device_id_type=MESH,
        )

    def new_slot():
        counter[0] += 1
        return counter[0] - 1

    def send(src, dst, device, group, slot=None):
        copy = message(src, dst, device, group, new_slot() if slot is None else slot)
        copy.start()
        return copy

    def all_sent(ref, group):
        message(ref, ref, dev_sib, group, 0).wait_send()

    def all_received(ref, slot):
        message(ref, ref, dev_sib, 0, slot).wait_recv()

    top, bottom = pl.ds(0, HALF_ROWS), pl.ds(HALF_ROWS, HALF_ROWS)

    def gather_start(axis, buf, group):
        p = place[axis]
        right, left = near[axis]
        tail = new_slot()
        if group in (X_R + PARTS - 1, X_S + PARTS - 1):
            own = buf.at[p, group_rows]
            for device in (far[axis], right, left):
                send(own, own, device, group, tail)
            return buf, tail
        from_left = send(buf.at[p, top], buf.at[p, top], right, group)
        from_right = send(buf.at[p, bottom], buf.at[p, bottom], left, group)
        send(buf.at[p, bottom], buf.at[p, bottom], right, group, tail)
        send(buf.at[p, top], buf.at[p, top], left, group, tail)
        return buf, group, from_left, from_right, tail

    def gather_pass(axis, state):
        p = place[axis]
        right, left = near[axis]
        buf, group, from_left, from_right, tail = state
        before, after = (p + 3) % RING, (p + 1) % RING
        from_left.wait_recv()
        send(buf.at[before, top], buf.at[before, top], right, group, tail)
        from_right.wait_recv()
        send(buf.at[after, bottom], buf.at[after, bottom], left, group, tail)

    def gather_end(state):
        all_received(state[0].at[pl.ds(0, 2 if len(state) > 2 else RING - 1), group_rows], state[-1])

    group_rows = pl.ds(0, GROUP_ROWS)

    group = y * RING + x
    my_start = jnp.int32(0)
    begin = jnp.int32(0)
    first_rows = []
    for d in range(N_DP):
        first_rows.append(begin // COLS)
        my_start = jnp.where(dp == d, begin, my_start)
        begin = begin + lengths_ref[group, d]
    my_length = lengths_ref[group, dp]
    lead = my_start % COLS
    lead_rows, lead_lanes = lead // LANES, lead % LANES
    staged[pl.ds(0, LEAD)] = jnp.zeros((LEAD, LANES), jnp.float32)
    tail_rows = staged.shape[0] - LEAD - FLAT_ROWS
    staged[pl.ds(LEAD + FLAT_ROWS, tail_rows)] = jnp.zeros((tail_rows, LANES), jnp.float32)

    def stage(i, _):
        value = flat_ref[:, pl.ds(pl.multiple_of(i * STEP * LANES, LANES), STEP * LANES)].astype(jnp.float32).reshape(STEP, LANES)
        value = jnp.where(slots(i) < my_length, value, 0.0)
        staged[pl.ds(pl.multiple_of(i * STEP + LEAD, 8), STEP)] = pltpu.roll(value, lead_lanes, 1)
        return 0

    lax.fori_loop(0, FLAT_ROWS // STEP, stage, 0)
    extra_tmp[...] = jnp.zeros_like(extra_tmp)

    def partner(i):
        there = (dp + by_distance(i)) % N_DP
        return there, (there, y, x)

    def out_copies(i):
        there, device = partner(i)
        copies = [message(canvas.at[j, there], arrived.at[j, i], device, OUT + j, j) for j in range(PARTS)]
        return copies + [message(extra.at[there], arrived_extra.at[i], device, OUT_EXTRA, PARTS)]

    def place_part(o, _):
        there = (dp + o) % N_DP
        lane = lax.broadcasted_iota(jnp.int32, (MAIN, LANES), 1)
        lane2 = lax.broadcasted_iota(jnp.int32, (2, LANES), 1)
        start = LEAD - lead_rows + there * 4
        before = staged[pl.ds(start - 1, MAIN, stride=CHUNKS)]
        before2 = staged[pl.ds(start - 1 + MAIN * CHUNKS, 2, stride=CHUNKS)]
        for j in range(4):
            here = staged[pl.ds(start + j, MAIN, stride=CHUNKS)]
            here2 = staged[pl.ds(start + j + MAIN * CHUNKS, 2, stride=CHUNKS)]
            canvas[j, there] = jnp.where(lane >= lead_lanes, here, before).astype(jnp.bfloat16)
            extra_tmp[pl.ds(j * 2, 2)] = jnp.where(lane2 >= lead_lanes, here2, before2)
            before, before2 = here, here2
        extra[there] = extra_tmp[...].astype(jnp.bfloat16)
        return 0

    lax.fori_loop(1, N_DP + 1, place_part, 0)
    pl.semaphore_wait(barrier, 6 + N_DP - 1)

    for j in (PARTS, *range(PARTS)):

        def send_out(i, _):
            out_copies(i)[j].start()
            return 0

        lax.fori_loop(0, PEERS, send_out, 0)
    for j in range(PARTS):
        arrived[j, PEERS] = canvas[j, dp]
    arrived_extra[PEERS] = extra[dp]

    def targets(length, width, offset, shape, dim, slot_of):
        k = lax.broadcasted_iota(jnp.int32, shape, dim)
        found = jnp.full(shape, -1, jnp.int32)
        for d in range(N_DP):
            inside = k // width == slot_of(d)
            found = jnp.where(inside, first_rows[d] + k % width + offset, found)
        return k, found

    def arrival_slot(d):
        ahead = (dp - d + N_DP) % N_DP - N_DP // 2
        return jnp.where(ahead >= 0, 2 * ahead, -2 * ahead - 1)

    k, row_of = targets(N_DP * MAIN, MAIN, 0, (1, N_DP * MAIN), 1, arrival_slot)
    pick = (lax.broadcasted_iota(jnp.int32, (GROUP_ROWS, N_DP * MAIN), 0) == row_of).astype(jnp.float32).astype(jnp.bfloat16)
    ke, row_e = targets(N_DP * EXTRA, EXTRA, MAIN, (1, N_DP * EXTRA), 1, arrival_slot)
    ke = ke % EXTRA

    remote = pl.ds(0, PEERS)

    def land(j):
        if j == 0:
            all_received(arrived_extra.at[remote], PARTS)
        all_received(arrived.at[j, remote], j)
        value = jnp.dot(pick, arrived[j].reshape(N_DP * MAIN, LANES), preferred_element_type=jnp.float32)
        row_j = jnp.where(ke // 2 == j, row_e - 2 * j, -1)
        pick_j = (lax.broadcasted_iota(jnp.int32, (GROUP_ROWS, N_DP * EXTRA), 0) == row_j).astype(jnp.float32).astype(jnp.bfloat16)
        late = arrived_extra[...].reshape(N_DP * EXTRA, LANES)
        value = (value + jnp.dot(pick_j, late, preferred_element_type=jnp.float32)).astype(jnp.bfloat16)
        x_ref[:, pl.ds(j * LANES, LANES)] = value
        xr[j, x, group_rows] = value
        xs[j, y] = value
        return gather_start("col", xr.at[j], X_R + j), gather_start("row", xs.at[j], X_S + j)

    def pass_part(states):
        gather_pass("col", states[0])
        gather_pass("row", states[1])

    def end_part(states):
        gather_end(states[0])
        gather_end(states[1])

    def xs_half(h):
        return jnp.concatenate([xs[2 * h].reshape(BLOCK, LANES), xs[2 * h + 1].reshape(BLOCK, LANES)], axis=1)

    halves = (pl.ds(0, HALF_SLAB), pl.ds(HALF_SLAB, HALF_SLAB))
    pad = pl.ds(GROUP_ROWS, PANEL - GROUP_ROWS)
    for q in range(RING):
        for j in range(PARTS):
            xr[j, q, pad] = jnp.zeros((PANEL - GROUP_ROWS, LANES), jnp.bfloat16)
    for p in range(2):
        to_sib[p, pad] = jnp.zeros((PANEL - GROUP_ROWS, BLOCK), jnp.bfloat16)
        own_f32[p, pad] = jnp.zeros((PANEL - GROUP_ROWS, BLOCK), jnp.float32)

    def gram(core, h, store):
        def tile(i, _):
            rows = pl.ds(pl.multiple_of((i % 2) * HALF_ROWS, 16), HALF_ROWS)
            q = 2 * core + i // 2
            value = lax.dot_general(
                jnp.concatenate([xr[2 * h, q, rows], xr[2 * h + 1, q, rows]], axis=1), xs_half(h),
                (((1,), (1,)), ((), ())), preferred_element_type=jnp.float32,
            )
            store(i // 2, rows, value)
            return 0

        lax.fori_loop(0, 4, tile, 0)

    def keep_own(p, rows, value):
        own_f32[p, rows] = value

    def keep_sib(p, rows, value):
        sib_f32[p, rows] = value

    def add_own(p, rows, value):
        own_f32[p, rows] += value

    def add_sib(p, rows, value):
        to_sib[p, rows] = (sib_f32[p, rows] + value).astype(jnp.bfloat16)

    parts = [land(0), land(1)]
    pass_part(parts[0])
    parts.append(land(2))
    pass_part(parts[1])
    parts.append(land(3))
    pass_part(parts[2])
    end_part(parts[0])
    end_part(parts[1])
    gram(1 - c, 0, keep_sib)
    gram(c, 0, keep_own)
    end_part(parts[2])
    end_part(parts[3])
    gram(1 - c, 1, add_sib)

    def shard_rows(s):
        return pl.ds(pl.multiple_of(((s + N_Z) % N_Z) * SHARD, 16), SHARD)

    f32 = jnp.float32
    plan = []
    for k in range(8):
        distance = 4 - (k + 1) // 2
        plan.append((True, k % 2, distance))
        plan.append((False, 1 - k % 2, distance))
    sib_in = []
    for upward, panel, distance in plan:
        rows = shard_rows(z + distance if upward else z - distance)
        sib_in.append(send(to_sib.at[panel, rows], from_sib.at[panel, rows], dev_sib, TO_SIB))
    gram(c, 1, add_own)

    ring_cols = (pl.ds(0, WIDE), pl.ds(WIDE, BLOCK - WIDE))
    up_in, down_in = [], []
    for (upward, panel, distance), arrival in zip(plan, sib_in):
        rows = shard_rows(z + distance if upward else z - distance)
        arrival.wait_recv()
        arrivals, ring, device = (up_in, ring_f, dev_up) if upward else (down_in, ring_b, dev_down)
        k = len(arrivals)
        copies = []
        for n, cols in enumerate(ring_cols):
            term = own_f32[panel, rows, cols] + from_sib[panel, rows, cols].astype(f32)
            if distance == 0:
                up, down = (6, 5) if panel == 0 else (5, 6)
                up_in[up][n].wait_recv()
                down_in[down][n].wait_recv()
                term = term + ring_f[up, :, cols].astype(f32) + ring_b[down, :, cols].astype(f32)
                g_full[2 * c + panel, rows, cols] = term.astype(jnp.bfloat16)
                continue
            if k < 2:
                src = gh.at[2 * k + int(upward), :, cols]
            else:
                arrivals[k - 2][n].wait_recv()
                src = ring.at[k - 2, :, cols]
                term = term + ring[k - 2, :, cols].astype(f32)
            src[...] = term.astype(jnp.bfloat16)
            copies.append(send(src, ring.at[k, :, cols], device, RING_UP if upward else RING_DOWN))
        if distance:
            arrivals.append(copies)
    mine = shard_rows(z)

    sib_slots = {shift: new_slot() for shift in (0, -1, 1, -2, 2, -3, 3, 4)}

    def relay(panel, rows, device, group, slot=None):
        ref = g_full.at[2 * c + panel, rows]
        return send(ref, ref, device, group, slot)

    y_slots = [new_slot() for _ in range(N_Z)]
    y_left, y_right = new_slot(), new_slot()
    order = (0, -1, 1, -2, 2, -3, 3, 4)

    def multiply(shift):
        i, rows = order.index(shift), shard_rows(z + shift)
        all_received(g_full.at[pl.ds(2 * (1 - c), 2), rows], sib_slots[shift])
        left = g_full[:, rows, :].reshape(RING * SHARD, BLOCK)
        for h in range(2):
            value = jnp.dot(left, xs_half(h), preferred_element_type=f32)
            y_tmp[:, :, halves[h]] = value.reshape(RING, SHARD, HALF_SLAB)
        y_out[i] = y_tmp[...].astype(jnp.bfloat16)
        for o in (2, 1, 3):
            there = (x + o) % RING
            send(y_out.at[i, there], y_in.at[i, o - 1], (dp, y, there), Y_SUM, y_slots[i])
        y_own[i] = y_tmp[x]

    def add_up(shift):
        i, rows = order.index(shift), shard_rows(z + shift)
        all_received(y_in.at[i], y_slots[i])
        value = y_own[i] + y_in[i, 0].astype(f32) + y_in[i, 1].astype(f32) + y_in[i, 2].astype(f32)
        y_f32[rows] = value
        ya[y, rows] = value[:, :HALF_SLAB].astype(jnp.bfloat16)
        yb[x, rows] = value[:, HALF_SLAB:].astype(jnp.bfloat16)
        for o in (2, 1, 3):
            send(ya.at[y, rows], ya.at[y, rows], (dp, (y + o) % RING, x), Y_GATHER, y_left)
            send(yb.at[x, rows], yb.at[x, rows], (dp, y, (x + o) % RING), Y_GATHER, y_right)

    up_in, down_in = [], []
    for k in range(9):
        back_by = k // 2
        up_part, down_part = (k % 2, shard_rows(z - back_by)), (1 - k % 2, shard_rows(z + back_by))
        if k >= 2:
            up_in[k - 2].wait_recv()
        if k < 7:
            up_in.append(relay(*up_part, dev_up, G_UP))
        if k >= 2:
            down_in[k - 2].wait_recv()
        if k < 7:
            down_in.append(relay(*down_part, dev_down, G_DOWN))
        relay(*up_part, dev_sib, G_SIB, sib_slots[4 if k == 8 else -back_by])
        if k >= 2:
            relay(*down_part, dev_sib, G_SIB, sib_slots[back_by])
        for shift in {3: (0,), 6: (-1, 1)}.get(k, ()):
            add_up(shift)
        for shift in {1: (0,), 3: (-1, 1), 5: (-2, 2), 7: (-3, 3), 8: (4,)}.get(k, ()):
            multiply(shift)
    for shift in (-2, 2, -3, 3, 4):
        add_up(shift)

    def reduce_start(axis, buf, slots, group):
        right, left = near[axis]
        farthest = (place[axis] + 2) % RING
        return (
            send(buf.at[farthest, top], slots[0], right, group),
            send(buf.at[farthest, bottom], slots[1], left, group),
            new_slot(),
        )

    def reduce_near(axis, buf, slots, group, tail):
        p = place[axis]
        right, left = near[axis]
        after, before = (p + 1) % RING, (p + 3) % RING
        send(buf.at[after, bottom], slots[2].at[bottom], right, group, tail)
        send(buf.at[before, top], slots[3].at[top], left, group, tail)

    def reduce_pass(axis, buf, slots, group, state):
        p = place[axis]
        right, left = near[axis]
        after, before = (p + 1) % RING, (p + 3) % RING
        state[0].wait_recv()
        buf[after, top] = (buf[after, top].astype(f32) + slots[0][...].astype(f32)).astype(jnp.bfloat16)
        send(buf.at[after, top], slots[2].at[top], right, group, state[2])
        state[1].wait_recv()
        buf[before, bottom] = (buf[before, bottom].astype(f32) + slots[1][...].astype(f32)).astype(jnp.bfloat16)
        send(buf.at[before, bottom], slots[3].at[bottom], left, group, state[2])

    first, second = pl.ds(0, HALF_SLAB), pl.ds(HALF_SLAB, HALF_SLAB)
    slots_a, slots_b = [[r.at[i] for r in (got_a, got_b, got_c, got_d)] for i in range(2)]
    farthest, after, before = (x + 2) % RING, (x + 1) % RING, (x + 3) % RING

    def times(q, right):
        return jnp.dot(g_full[q, group_rows], right, preferred_element_type=f32)

    def open_a(buf, right, slots):
        buf[farthest] = times(farthest, right()).astype(jnp.bfloat16)
        state = reduce_start("col", buf, slots, Z_A)
        buf[after] = times(after, right()).astype(jnp.bfloat16)
        buf[before] = times(before, right()).astype(jnp.bfloat16)
        reduce_near("col", buf, slots, Z_A, state[2])
        return state

    def open_b(buf, right, slots):
        def columns(j, _):
            cols = pl.ds(pl.multiple_of(j * LANES, LANES), LANES)
            z_b[cols] = lax.dot_general(
                g_full[:, :, cols].reshape(RING * PANEL, LANES), right, (((0,), (0,)), ((), ())),
                preferred_element_type=f32,
            )
            return 0

        lax.fori_loop(0, BLOCK // LANES, columns, 0)
        buf[...] = z_b[...].astype(jnp.bfloat16).reshape(RING, GROUP_ROWS, HALF_SLAB)
        state = reduce_start("row", buf, slots, Z_B)
        reduce_near("row", buf, slots, Z_B, state[2])
        return state

    def close(state, slots, total, cols):
        all_received(xr.at[pl.ds(0, PARTS), 0, group_rows], state[2])
        total[:, cols] = total[:, cols] + slots[2][...].astype(f32) + slots[3][...].astype(f32)

    def own_b(total):
        total[:, second] = z_b[pl.ds(pl.multiple_of(y * GROUP_ROWS, 8), GROUP_ROWS)]

    three = pl.ds(0, RING - 1)
    all_received(ya.at[three], y_left)
    oa = open_a(part.at[0], lambda: ya[:, :GROUP_ROWS].reshape(BLOCK, HALF_SLAB), slots_a)
    all_received(yb.at[three], y_right)
    ob = open_b(part.at[1], yb[...].reshape(RING * PANEL, HALF_SLAB), slots_b)
    z_f32[:, first] = times(x, ya[:, :GROUP_ROWS].reshape(BLOCK, HALF_SLAB))
    own_b(z_f32)
    reduce_pass("col", part.at[0], slots_a, Z_A, oa)
    reduce_pass("row", part.at[1], slots_b, Z_B, ob)

    _, row_of = targets(N_DP * MAIN, MAIN, 0, (N_DP * MAIN, 1), 0, lambda d: d)
    pick = (lax.broadcasted_iota(jnp.int32, (N_DP * MAIN, GROUP_ROWS), 1) == row_of).astype(f32).astype(jnp.bfloat16)
    ke, row_e = targets(N_DP * EXTRA, EXTRA, MAIN, (N_DP * EXTRA, 1), 0, lambda d: d)
    ke = ke % EXTRA
    late_picks = []
    for j in range(4):
        row_j = jnp.where(ke // 2 == j, row_e - 2 * j, -1)
        pick_j = lax.broadcasted_iota(jnp.int32, (N_DP * EXTRA, GROUP_ROWS), 1) == row_j
        late_picks.append(pick_j.astype(f32).astype(jnp.bfloat16))

    def back_copies(i):
        there, device = partner(i)
        group = i // BACK_GROUP
        return (
            message(outgoing.at[0, there], returned.at[0, i], device, BACK_0, 5 + group),
            message(outgoing.at[1, there], returned.at[1, i], device, BACK_1, 8 + group),
            message(outgoing_extra.at[there], returned_extra.at[i], device, BACK_EXTRA, 11),
        )

    def send_back(n):
        def step(i, _):
            back_copies(i)[n].start()
            return 0

        lax.fori_loop(0, PEERS, step, 0)

    def late_rows(h):
        return sum(
            jnp.dot(late_picks[j], update[:, j * LANES : (j + 1) * LANES], preferred_element_type=f32)
            for j in (2 * h, 2 * h + 1)
        )

    def leave(h, cols):
        update[:, cols] = (
            SCALE * (LINEAR_COEF * x_ref[:, cols].astype(f32) + (CUBIC_COEF * y_f32[group_rows, cols] + QUINTIC_COEF * z_f32[:, cols]))
        ).astype(jnp.bfloat16)
        outgoing[h] = (
            jnp.dot(pick, update[:, cols], preferred_element_type=f32).astype(jnp.bfloat16).reshape(N_DP, MAIN, HALF_SLAB)
        )
        send_back(h)
        returned[h, PEERS] = outgoing[h, dp]

    close(oa, slots_a, z_f32, first)
    leave(0, first)
    late = late_rows(0)
    close(ob, slots_b, z_f32, second)
    leave(1, second)
    outgoing_extra[...] = (late + late_rows(1)).astype(jnp.bfloat16).reshape(N_DP, EXTRA, LANES)
    send_back(2)
    returned_extra[PEERS] = outgoing_extra[dp]

    turn = (LANES - lead_lanes) % LANES

    def unpack(h, i):
        d = (dp - by_distance(i) + N_DP) % N_DP
        for j in range(2):
            back[pl.ds(d * 4 + 2 * h + j, MAIN, stride=CHUNKS)] = pltpu.roll(
                returned[h, i, :, pl.ds(j * LANES, LANES)].astype(f32), turn, 1)

    def unpack_late(i, _):
        d = (dp - by_distance(i) + N_DP) % N_DP
        extra_tmp[...] = pltpu.roll(returned_extra[i].astype(f32), turn, 1)
        for j in range(4):
            back[pl.ds(d * 4 + j + MAIN * CHUNKS, 2, stride=CHUNKS)] = extra_tmp[2 * j : 2 * j + 2]
        return 0

    def unpack_step(h):
        def step(i, _):
            unpack(h, i)
            return 0

        return step

    back[pl.ds(34 * CHUNKS, 8)] = jnp.zeros((8, LANES), f32)
    for h in range(2):
        unpack(h, jnp.int32(PEERS))
    for h in range(2):
        for group in range(3):
            all_received(returned.at[h, pl.ds(group * BACK_GROUP, BACK_GROUP)], 5 + 3 * h + group)
            lax.fori_loop(group * BACK_GROUP, (group + 1) * BACK_GROUP, unpack_step(h), 0)
    all_received(returned_extra.at[pl.ds(0, PEERS)], 11)
    lax.fori_loop(0, N_DP, unpack_late, 0)

    def finish(i, _):
        here = back[pl.ds(i * STEP + lead_rows, STEP)]
        after_rows = back[pl.ds(i * STEP + lead_rows + 1, STEP)]
        lane = lax.broadcasted_iota(jnp.int32, (STEP, LANES), 1)
        value = jnp.where(lane + lead_lanes < LANES, here, after_rows)
        out_ref[pl.ds(pl.multiple_of(i * STEP, 8), STEP)] = jnp.where(slots(i) < my_length, value, 0.0)
        return 0

    lax.fori_loop(0, FLAT_ROWS // STEP, finish, 0)

    for ref, groups in (
        (arrived.at[0, remote], range(OUT, OUT + PARTS)),
        (returned.at[0, remote], (BACK_0, BACK_1)),
        (arrived_extra.at[remote], (OUT_EXTRA, BACK_EXTRA)),
        (xs.at[0, pl.ds(0, RING - 1)], range(X_R, X_S + PARTS)),
        (part.at[0, pl.ds(0, RING - 1)], (Z_A, Z_B)),
        (to_sib, (TO_SIB, G_SIB)),
        (ring_f, (RING_UP, RING_DOWN, G_UP, G_DOWN)),
        (y_in, (Y_SUM, Y_GATHER)),
    ):
        for group in groups:
            all_sent(ref, group)


def flatten_kernel(value_ref, out_ref):
    def step(i, _):
        value = value_ref[pl.ds(pl.multiple_of(i * STEP, 8), STEP)].reshape(1, STEP * LANES)
        out_ref[:, pl.ds(pl.multiple_of(i * STEP * LANES, LANES), STEP * LANES)] = value.astype(jnp.bfloat16)
        return 0

    lax.fori_loop(0, value_ref.shape[0] // STEP, step, 0)


def newton_schulz(lengths, flat):
    bf, f32 = jnp.bfloat16, jnp.float32
    vmem = pltpu.VMEM
    value = pl.pallas_call(
        core_kernel,
        out_shape=jax.ShapeDtypeStruct((FLAT_ROWS, LANES), f32),
        in_specs=[pl.BlockSpec(memory_space=pltpu.SMEM), pl.BlockSpec(memory_space=pltpu.VMEM)],
        out_specs=pl.BlockSpec(memory_space=pltpu.VMEM),
        scratch_shapes=[
            vmem((LEAD + FLAT_ROWS + 88, LANES), f32),
            vmem((PARTS, N_DP, MAIN, LANES), bf),
            vmem((2, N_DP, MAIN, HALF_SLAB), bf),
            vmem((EXTRA, LANES), f32),
            vmem((N_DP, EXTRA, LANES), bf),
            vmem((PARTS, N_DP, MAIN, LANES), bf),
            vmem((N_DP, EXTRA, LANES), bf),
            vmem((GROUP_ROWS, SLAB), bf),
            vmem((PARTS, RING, PANEL, LANES), bf),
            vmem((PARTS, RING, GROUP_ROWS, LANES), bf),
            vmem((2, PANEL, BLOCK), f32),
            vmem((2, PANEL, BLOCK), f32),
            vmem((2, PANEL, BLOCK), bf),
            vmem((2, PANEL, BLOCK), bf),
            vmem((4, SHARD, BLOCK), bf),
            vmem((7, SHARD, BLOCK), bf),
            vmem((7, SHARD, BLOCK), bf),
            vmem((RING, PANEL, BLOCK), bf),
            vmem((2, RING, GROUP_ROWS, HALF_SLAB), bf),
            vmem((2, HALF_ROWS, HALF_SLAB), bf),
            vmem((2, HALF_ROWS, HALF_SLAB), bf),
            vmem((2, GROUP_ROWS, HALF_SLAB), bf),
            vmem((2, GROUP_ROWS, HALF_SLAB), bf),
            vmem((PANEL, SLAB), f32),
            vmem((RING, PANEL, HALF_SLAB), bf),
            vmem((RING, PANEL, HALF_SLAB), bf),
            vmem((RING, SHARD, SLAB), f32),
            vmem((N_Z, RING, SHARD, SLAB), bf),
            vmem((N_Z, RING - 1, SHARD, SLAB), bf),
            vmem((N_Z, SHARD, SLAB), f32),
            vmem((BLOCK, HALF_SLAB), f32),
            vmem((GROUP_ROWS, SLAB), f32),
            vmem((GROUP_ROWS, SLAB), bf),
            vmem((N_DP, EXTRA, LANES), bf),
            vmem((2, N_DP, MAIN, HALF_SLAB), bf),
            vmem((N_DP, EXTRA, LANES), bf),
            vmem((34 * CHUNKS + 8, LANES), f32),
            pltpu.SemaphoreType.DMA((N_SENT,)),
            pltpu.SemaphoreType.DMA((N_RECEIVED,)),
        ],
        compiler_params=pltpu.CompilerParams(
            collective_id=0, has_side_effects=True, vmem_limit_bytes=56 * 1024 * 1024
        ),
    )(lengths, flat)
    return pl.pallas_call(
        flatten_kernel,
        out_shape=jax.ShapeDtypeStruct((1, FLAT_ROWS * LANES), bf),
        in_specs=[pl.BlockSpec(memory_space=pltpu.VMEM)],
        out_specs=pl.BlockSpec(memory_space=pltpu.VMEM),
        compiler_params=pltpu.CompilerParams(vmem_limit_bytes=56 * 1024 * 1024),
    )(value)


def local(flat_iterate, lengths):
    return newton_schulz(lengths, flat_iterate)


def solution(mesh):
    return jax.shard_map(
        local,
        mesh=mesh,
        in_specs=(P(("dp", "row", "col"), None), P()),
        out_specs=P(("dp", "row", "col"), None),
        check_vma=False,
    )
```
